32 devices in a mesh: rep: 2 (over core), shard: 8 (over z, y), seq: 2 (over x).
Axes of the slice: x: 2, y: 2, z: 4, core: 2. Of those that a mesh axis runs over, the one named last changes fastest.
Arguments:
- latents: bfloat16 [16, 1024, 768], P(('rep', 'shard'), 'seq'), may hold values from -6 to 6
- image_loads: int32 [16], P(('rep', 'shard')), may hold values from 0 to 1, as said below
- timesteps: int32 [16], P(('rep', 'shard')), may hold values from 0 to 999
- classes: int32 [16], P(('rep', 'shard')), may hold values from 0 to 999
- label_table: bfloat16 [1000, 768], replicated, may hold values from -6 to 6
- ada_weight: bfloat16 [2, 768, 4608], P(None, 'shard'), may hold values from -0.21875 to 0.21875
- ada_bias: bfloat16 [2, 4608], P(None, 'shard'), may hold values from -3 to 3
- qkv_weight: bfloat16 [2, 768, 2304], P(None, 'shard'), may hold values from -0.21875 to 0.21875
- qv_bias: bfloat16 [2, 1536], P(None, 'shard'), may hold values from -3 to 3
- proj_weight: bfloat16 [2, 768, 768], P(None, 'shard'), may hold values from -0.625 to 0.625
- proj_bias: bfloat16 [2, 768], P(None, 'shard'), may hold values from -3 to 3
- fc1_weight: bfloat16 [2, 768, 3072], P(None, 'shard'), may hold values from -0.21875 to 0.21875
- fc1_bias: bfloat16 [2, 3072], P(None, 'shard'), may hold values from -3 to 3
- fc2_weight: bfloat16 [2, 3072, 768], P(None, 'shard'), may hold values from -0.109375 to 0.109375
- fc2_bias: bfloat16 [2, 768], P(None, 'shard'), may hold values from -3 to 3
- cotangent: bfloat16 [16, 1024, 768], P(('rep', 'shard'), 'seq'), may hold values from -6 to 6
Outputs:
- activations: float32 [16, 1024, 768], P(('rep', 'shard'), 'seq')
- latent_grad: float32 [16, 1024, 768], P(('rep', 'shard'), 'seq')
- cond_grad: float32 [16, 768], P(('rep', 'shard'))
- ada_weight_grad: float32 [2, 768, 4608], P(None, 'shard')
- ada_bias_grad: float32 [2, 4608], P(None, 'shard')
- qkv_weight_grad: float32 [2, 768, 2304], P(None, 'shard')
- qv_bias_grad: float32 [2, 1536], P(None, 'shard')
- proj_weight_grad: float32 [2, 768, 768], P(None, 'shard')
- proj_bias_grad: float32 [2, 768], P(None, 'shard')
- fc1_weight_grad: float32 [2, 768, 3072], P(None, 'shard')
- fc1_bias_grad: float32 [2, 3072], P(None, 'shard')
- fc2_weight_grad: float32 [2, 3072, 768], P(None, 'shard')
- fc2_bias_grad: float32 [2, 768], P(None, 'shard')
The draws below stay inside these ranges and needn't reach their ends.
Inputs may be any that keep to these rules, and one draw needn't show every extreme that they name: Position p holds image_loads[p] live images in its first slots; its other slots of the 1 are empty and give zero outputs. Some position holds 1 live images and some holds none.
All inputs are finite; a program needn't handle non-finite values.
Results may differ from the reference program's by a relative error of at most 0.04.
Values may be sent and summed in bfloat16 or wider, within the bound.
No kernel may reach another device: no remote copies, remote signals or barrier semaphores. Data moves between devices by JAX's collectives and lax.ppermute only.
A program may use at most 320 MiB of HBM per device.

```python
import math
import jax
import jax.numpy as jnp
from jax import lax

D = 768
HEADS = 12
HEAD_DIM = 64
FF = 3072
CLASSES = 1000
IMG_TOKENS = 1024
SLOTS = 1
LAYERS = 2
TSTEPS = 1000
POSITIONS = 16
IMAGES = 16


def draw_image_loads(key, part):
    counts = jax.random.randint(jax.random.fold_in(key, 11), (POSITIONS,), 0, SLOTS + 1)
    chosen = jax.random.permutation(jax.random.fold_in(key, 12), POSITIONS)
    counts = counts.at[chosen[0]].set(SLOTS)
    counts = counts.at[chosen[1]].set(0)
    return counts.astype(jnp.int32)


def place_ends(values, rng, low, top_value):
    dims = values.shape
    index_at = [jax.random.randint(jax.random.fold_in(rng, axis), (), 0, dims[axis]) for axis in range(len(dims))]
    values = values.at[tuple(index_at)].set(low)
    longest = dims.index(max(dims))
    index_at[longest] = (index_at[longest] + 1) % dims[longest]
    return values.at[tuple(index_at)].set(top_value)


def levels(rng, extent, shards, least, largest):
    loudness, own = 1.0, jax.random.fold_in(rng, 6)
    for dim, parts in shards:
        steps = jnp.exp(jax.random.uniform(jax.random.fold_in(own, dim), (parts,), jnp.float32, least / len(shards), largest / len(shards)))
        loudness = loudness * jnp.repeat(steps, extent[dim] // parts).reshape([-1 if axis == dim else 1 for axis in range(len(extent))])
    return loudness


def normal_values(own_key, dims, width, limit, pieces=(), held_as=jnp.bfloat16):
    values = width * jax.random.normal(own_key, dims, jnp.float32)
    if pieces:
        values = values * levels(own_key, dims, pieces, -0.22, 0.18)
    return jnp.clip(values, -limit, limit).astype(held_as)


def setup_inputs(seed: int = 0) -> dict:
    streams_of = jax.random.split(jax.random.key(seed), 17)
    latents = normal_values(streams_of[0], (IMAGES, IMG_TOKENS, D), 1.0, 6.0, ((0, 16), (1, 2)))
    image_loads = draw_image_loads(jax.random.fold_in(streams_of[16], 71), 0)
    timesteps = place_ends(jax.random.randint(streams_of[2], (IMAGES,), 0, TSTEPS), jax.random.fold_in(streams_of[2], 1), 0, TSTEPS - 1).astype(jnp.int32)
    classes = place_ends(jax.random.randint(streams_of[3], (IMAGES,), 0, CLASSES), jax.random.fold_in(streams_of[3], 1), 0, CLASSES - 1).astype(jnp.int32)
    label_table = normal_values(streams_of[4], (CLASSES, D), 1.0, 6.0)
    ada_weight = normal_values(streams_of[5], (LAYERS, D, 6 * D), D ** -0.5, 0.21875, ((1, 8),))
    ada_bias = normal_values(streams_of[6], (LAYERS, 6 * D), 0.5, 3.0, ((1, 8),))
    qkv_weight = normal_values(streams_of[7], (LAYERS, D, 3 * D), D ** -0.5, 0.21875, ((1, 8),))
    qv_bias = normal_values(streams_of[8], (LAYERS, 2 * D), 0.5, 3.0, ((1, 8),))
    proj_weight = normal_values(streams_of[9], (LAYERS, D, D), (D // 8) ** -0.5, 0.625, ((1, 8),))
    proj_bias = normal_values(streams_of[10], (LAYERS, D), 0.5, 3.0, ((1, 8),))
    fc1_weight = normal_values(streams_of[11], (LAYERS, D, FF), D ** -0.5, 0.21875, ((1, 8),))
    fc1_bias = normal_values(streams_of[12], (LAYERS, FF), 0.5, 3.0, ((1, 8),))
    fc2_weight = normal_values(streams_of[13], (LAYERS, FF, D), FF ** -0.5, 0.109375, ((1, 8),))
    fc2_bias = normal_values(streams_of[14], (LAYERS, D), 0.5, 3.0, ((1, 8),))
    cotangent = normal_values(streams_of[15], (IMAGES, IMG_TOKENS, D), 1.0, 6.0, ((0, 16), (1, 2)))
    return dict(latents=latents, image_loads=image_loads, timesteps=timesteps, classes=classes, label_table=label_table, ada_weight=ada_weight, ada_bias=ada_bias, qkv_weight=qkv_weight, qv_bias=qv_bias, proj_weight=proj_weight, proj_bias=proj_bias, fc1_weight=fc1_weight, fc1_bias=fc1_bias, fc2_weight=fc2_weight, fc2_bias=fc2_bias, cotangent=cotangent)


@jax.custom_vjp
def low(v):
    return lax.optimization_barrier(v.astype(jnp.bfloat16)).astype(jnp.float32)

@jax.custom_vjp
def low_back(v):
    return v

def low_keep(v):
    return (low(v), None)

def low_pass(kept, grad):
    return (grad,)

def back_keep(v):
    return (v, None)

def back_low(kept, grad):
    return (low(grad),)
low.defvjp(low_keep, low_pass)
low_back.defvjp(back_keep, back_low)
EPSILON = 1e-06
HIGHEST = lax.Precision.HIGHEST

def product(left, right):
    return jnp.matmul(left, right, precision=HIGHEST)

def normalize(values):
    centered = values - lax.optimization_barrier(jnp.mean(values, axis=-1, keepdims=True))
    return centered * lax.rsqrt(lax.optimization_barrier(jnp.mean(centered * centered, axis=-1, keepdims=True)) + EPSILON)

def modulate(values, shift, factor):
    return normalize(values) * (1.0 + factor[:, None, :]) + shift[:, None, :]

def time_embed(steps):
    half_width = D // 2
    freqs = jnp.exp(-math.log(10000.0) * jnp.arange(half_width, dtype=jnp.float32) / half_width)
    angles = steps.astype(jnp.float32)[:, None] * freqs[None, :]
    return jnp.concatenate([jnp.cos(angles), jnp.sin(angles)], axis=-1)

def block(stream, cond_low, params):
    ada_weight, ada_bias, qkv_weight, qv_bias, proj_weight, proj_bias, fc1_weight, fc1_bias, fc2_weight, fc2_bias = params
    batch = stream.shape[0]
    modulation = low_back(product(cond_low, ada_weight) + ada_bias)
    shift_attn, factor_attn, gate_attn, shift_mlp, factor_mlp, gate_mlp = jnp.split(modulation, 6, axis=-1)
    normed = low(modulate(stream, shift_attn, factor_attn))
    qkv_full_bias = jnp.concatenate([qv_bias[:D], jnp.zeros((D,), jnp.float32), qv_bias[D:]])
    projected = low_back(low(product(normed, qkv_weight) + qkv_full_bias))
    queries = projected[..., :D].reshape(batch, IMG_TOKENS, HEADS, HEAD_DIM)
    keys = projected[..., D:2 * D].reshape(batch, IMG_TOKENS, HEADS, HEAD_DIM)
    values = projected[..., 2 * D:].reshape(batch, IMG_TOKENS, HEADS, HEAD_DIM)
    scores = low_back(jnp.einsum('bqhd,bkhd->bhqk', queries, keys, precision=HIGHEST) * HEAD_DIM ** (-0.5))
    expo = jnp.exp(scores - lax.optimization_barrier(jnp.max(scores, axis=-1, keepdims=True)))
    probs = low(expo / lax.optimization_barrier(jnp.sum(expo, axis=-1, keepdims=True)))
    mixed = jnp.einsum('bhqk,bkhd->bqhd', probs, values, precision=HIGHEST).reshape(batch, IMG_TOKENS, D)
    mixed = low_back(low(mixed))
    attn_out = low_back(product(mixed, proj_weight) + proj_bias)
    middle = stream + gate_attn[:, None, :] * attn_out
    normed_mlp = low(modulate(middle, shift_mlp, factor_mlp))
    hidden = low_back(product(normed_mlp, fc1_weight) + fc1_bias)
    activated = low(jax.nn.gelu(hidden, approximate=True))
    mlp_out = low_back(product(activated, fc2_weight) + fc2_bias)
    return middle + gate_mlp[:, None, :] * mlp_out

def reference(latents, image_loads, timesteps, classes, label_table, ada_weight, ada_bias, qkv_weight, qv_bias, proj_weight, proj_bias, fc1_weight, fc1_bias, fc2_weight, fc2_bias, cotangent):
    slot_ids = jnp.arange(IMAGES, dtype=jnp.int32)
    live = (slot_ids % SLOTS < image_loads[slot_ids // SLOTS]).astype(jnp.float32)
    cond = jnp.take(label_table.astype(jnp.float32), classes, axis=0) + time_embed(timesteps)
    params = tuple((p.astype(jnp.float32) for p in (ada_weight, ada_bias, qkv_weight, qv_bias, proj_weight, proj_bias, fc1_weight, fc1_bias, fc2_weight, fc2_bias)))
    groups = IMAGES // SLOTS

    def forward(stream, cond_vec, weights):
        cond_low = low(jax.nn.silu(cond_vec))

        def group_run(inputs):
            group_stream, group_cond = inputs
            for layer_index in range(LAYERS):
                group_stream = block(group_stream, group_cond, tuple((w[layer_index] for w in weights)))
            return group_stream
        result = lax.map(jax.checkpoint(group_run), (stream.reshape(groups, SLOTS, IMG_TOKENS, D), cond_low.reshape(groups, SLOTS, D)))
        return result.reshape(IMAGES, IMG_TOKENS, D) * live[:, None, None]
    result, pull = jax.vjp(forward, latents.astype(jnp.float32), cond, params)
    grad_stream, grad_cond, grad_params = pull(cotangent.astype(jnp.float32))
    return (result, grad_stream, grad_cond, grad_params[0], grad_params[1], grad_params[2], grad_params[3], grad_params[4], grad_params[5], grad_params[6], grad_params[7], grad_params[8], grad_params[9])
```

```python
import functools
import math

import jax
import jax.numpy as jnp
from jax import lax
from jax.experimental import pallas as pl
from jax.experimental.pallas import tpu as pltpu
from jax.sharding import PartitionSpec as P

HEADS = 12
LAYERS = 2
EPSILON = 1e-06
BF16 = jnp.bfloat16
F32 = jnp.float32


def swap_pairs(value, axis):
    return lax.ppermute(value, axis, [(0, 1), (1, 0)])


def swap_layout(value):
    return lax.ppermute(value, ("rep", "seq"), [(0, 0), (1, 2), (2, 1), (3, 3)])


def ring_order(size):
    half = size // 2
    return [2 * place for place in range(half)] + [2 * place + 1 for place in reversed(range(half))]


def ring_step(value, forward):
    size = lax.axis_size("shard")
    order = ring_order(size)
    step = 1 if forward else size - 1
    return lax.ppermute(
        value, "shard", [(order[at], order[(at + step) % size]) for at in range(size)]
    )


def ring_ids():
    size = lax.axis_size("shard")
    order = ring_order(size)
    places = [order.index(shard) for shard in range(size)]
    place = jnp.array(places, jnp.int32)[lax.axis_index("shard")]
    return jnp.array(order, jnp.int32)[(place + jnp.arange(size, dtype=jnp.int32)) % size]


OFFSETS = (-1, 1, -2, 2, -3, 3, 4)


def place_kernel(plain, split, where, *refs):
    (own, *rest) = refs[:19]
    outs = refs[19:-1]
    sem = refs[-1]
    blocks, near_x, far_x = rest[0:7], rest[7], rest[8]
    core_blocks, core_near_x, core_far_x = rest[9:16], rest[16], rest[17]
    rep, seq = where[8], where[9]
    unit = own.shape[1] // 6

    def put(src, shard, row, rows):
        copies = []
        if plain:
            start = pl.multiple_of(shard * (6 * unit) + row * unit, unit)
            copies.append(
                pltpu.make_async_copy(src.at[0:plain], outs[0].at[:, pl.ds(start, rows), :], sem)
            )
        if split:
            start = pl.multiple_of(row * unit, unit)
            copies.append(
                pltpu.make_async_copy(
                    src.at[plain : plain + split],
                    outs[-1].at[shard, :, pl.ds(start, rows), :],
                    sem,
                )
            )
        for copy in copies:
            copy.start()
        return copies

    copies = put(own, where[0], 0, 6 * unit)
    for slot, offset in enumerate(OFFSETS):
        shard = where[offset % 8]
        beside = (near_x, core_near_x) if slot < 4 else (far_x, core_far_x)
        at = slot if slot < 4 else slot - 4
        copies += put(blocks[slot], shard, 3 * rep + seq, 2 * unit)
        copies += put(beside[0].at[at], shard, 3 * rep + 2 * (1 - seq), unit)
        copies += put(core_blocks[slot], shard, 3 * (1 - rep) + seq, 2 * unit)
        copies += put(beside[1].at[at], shard, 3 * (1 - rep) + 2 * (1 - seq), unit)
    for copy in copies:
        copy.wait()


def gather_ring(piece, split):
    count, rows, width = piece.shape
    shards = lax.axis_size("shard")
    unit = rows // 6
    rep, seq = lax.axis_index("rep"), lax.axis_index("seq")
    mine = lax.dynamic_slice(piece, (0, (3 * rep + seq) * unit, 0), (count, 2 * unit, width))

    def cross(blocks):
        cut = [
            lax.dynamic_slice(block, (0, seq * unit, 0), (count, unit, width)) for block in blocks
        ]
        return swap_pairs(jnp.stack(cut), "seq")

    up1, down1 = ring_step(mine, True), ring_step(mine, False)
    up2, down2 = ring_step(up1, True), ring_step(down1, False)
    near_x = cross([up1, down1, up2, down2])
    up3, down3 = ring_step(up2, True), ring_step(down2, False)
    up4, down4 = ring_step(up3[:, :unit], True), ring_step(down3[:, unit:], False)
    far = jnp.concatenate([up4, down4], axis=1)
    far_x = cross([up3, down3, far])
    parts = [up1, down1, up2, down2, up3, down3, far, near_x, far_x]
    parts += [swap_pairs(part, "rep") for part in parts]
    where = jnp.concatenate([ring_ids(), jnp.stack([rep, seq]).astype(jnp.int32)])
    plain = count - split
    shapes = []
    if plain:
        shapes.append(jax.ShapeDtypeStruct((plain, shards * rows, width), piece.dtype))
    if split:
        shapes.append(jax.ShapeDtypeStruct((shards, split, rows, width), piece.dtype))
    anywhere = pl.BlockSpec(memory_space=pl.ANY)
    return pl.pallas_call(
        functools.partial(place_kernel, plain, split),
        out_shape=tuple(shapes),
        in_specs=[pl.BlockSpec(memory_space=pltpu.SMEM)] + [anywhere] * 19,
        out_specs=(anywhere,) * len(shapes),
        scratch_shapes=[pltpu.SemaphoreType.DMA],
        cost_estimate=pl.CostEstimate(
            flops=0, transcendentals=0, bytes_accessed=2 * shards * piece.size * 2
        ),
    )(where, piece, *parts)


def gather_plain(piece, split):
    count, rows, width = piece.shape
    shards = lax.axis_size("shard")
    plain = count - split
    outs = []
    if plain:
        outs.append(lax.all_gather(piece[:plain], "shard", axis=1, tiled=True))
    if split:
        outs.append(lax.all_gather(piece[plain:], "shard", axis=0, tiled=False))
    return tuple(outs)


def ring_fits(rows):
    return (
        lax.axis_size("shard") == 8
        and lax.axis_size("rep") == 2
        and lax.axis_size("seq") == 2
        and rows % 96 == 0
    )


def gather(piece, split):
    return (gather_ring if ring_fits(piece.shape[1]) else gather_plain)(piece, split)


def add(left, right):
    return (left.astype(F32) + right.astype(F32)).astype(BF16)


def scatter_ring(grads):
    shards, count, rows, width = grads.shape
    unit = rows // 6
    rep, seq = lax.axis_index("rep"), lax.axis_index("seq")
    ids = ring_ids()

    def half(which):
        return lax.dynamic_slice(
            grads, (0, 0, 3 * unit * which, 0), (shards, count, 3 * unit, width)
        )

    paired = add(half(rep), swap_pairs(half(1 - rep), "rep"))

    def parts(offsets):
        blocks = [
            lax.dynamic_index_in_dim(paired, ids[offset % 8], 0, keepdims=False)
            for offset in offsets
        ]
        sent = jnp.stack(
            [
                lax.dynamic_slice(block, (0, 2 * (1 - seq) * unit, 0), (count, unit, width))
                for block in blocks
            ]
        )
        got = swap_pairs(sent, "seq")
        out = []
        for at, block in enumerate(blocks):
            kept = lax.dynamic_slice(block, (0, seq * unit, 0), (count, 2 * unit, width))
            zero = jnp.zeros_like(got[at])
            beside = jnp.where(
                seq == 0,
                jnp.concatenate([got[at], zero], axis=1),
                jnp.concatenate([zero, got[at]], axis=1),
            )
            out.append(add(kept, beside))
        return out

    (far,) = parts((4,))
    up3, down3 = parts((3, -3))
    up2, down2 = parts((2, -2))
    up1, down1, here = parts((1, -1, 0))
    up = ring_step(far[:, :unit], True)
    down = ring_step(far[:, unit:], False)
    up = jnp.concatenate([add(up3[:, :unit], up), up3[:, unit:]], axis=1)
    down = jnp.concatenate([down3[:, :unit], add(down3[:, unit:], down)], axis=1)
    up, down = ring_step(up, True), ring_step(down, False)
    up, down = ring_step(add(up2, up), True), ring_step(add(down2, down), False)
    up, down = ring_step(add(up1, up), True), ring_step(add(down1, down), False)
    total = (here.astype(F32) + up.astype(F32) + down.astype(F32)).astype(BF16)
    other = swap_pairs(total, "seq")
    left, right = jnp.where(seq == 0, total, other), jnp.where(seq == 0, other, total)
    mine = jnp.concatenate(
        [left[:, :unit], add(left[:, unit:], right[:, :unit]), right[:, unit:]], axis=1
    )
    other = swap_pairs(mine, "rep")
    return jnp.where(
        rep == 0,
        jnp.concatenate([mine, other], axis=1),
        jnp.concatenate([other, mine], axis=1),
    ).astype(F32)


def scatter_plain(grads):
    owned = lax.psum_scatter(grads.astype(F32), "shard", scatter_dimension=0, tiled=False)
    return lax.psum(owned.astype(BF16), ("rep", "seq")).astype(F32)


def scatter(grads):
    return (scatter_ring if ring_fits(grads.shape[2]) else scatter_plain)(grads)


def normalize(values):
    centered = values - jnp.mean(values, axis=-1, keepdims=True)
    scale = lax.rsqrt(jnp.mean(centered * centered, axis=-1, keepdims=True) + EPSILON)
    return centered * scale, scale


def norm_back(grad, normal, scale, factor):
    u = grad * (1.0 + factor)
    return (
        u
        - jnp.mean(u, axis=-1, keepdims=True)
        - normal * jnp.mean(u * normal, axis=-1, keepdims=True)
    ) * scale


def time_embed(steps, width):
    half_width = width // 2
    freqs = jnp.exp(-math.log(10000.0) * jnp.arange(half_width, dtype=F32) / half_width)
    angles = steps.astype(F32)[:, None] * freqs[None, :]
    return jnp.concatenate([jnp.cos(angles), jnp.sin(angles)], axis=-1)


def dot(left, right, left_dims, right_dims):
    return lax.dot_general(
        left, right, ((left_dims, right_dims), ((), ())), preferred_element_type=F32
    )


def split_heads(values):
    return values.reshape(values.shape[0], HEADS, values.shape[1] // HEADS)


def attend(queries, keys, values):
    q, k, v = split_heads(queries), split_heads(keys), split_heads(values)
    scale_factor = q.shape[-1] ** (-0.5)
    scores = jnp.einsum("qhd,khd->hqk", q, k, preferred_element_type=F32) * scale_factor
    top_score = jnp.max(scores, axis=-1, keepdims=True)
    expo = jnp.exp(scores - top_score)
    totals = jnp.sum(expo, axis=-1, keepdims=True)
    probs_low = (expo / totals).astype(BF16)
    mixed = jnp.einsum("hqk,khd->qhd", probs_low, v, preferred_element_type=F32)
    return mixed.reshape(queries.shape).astype(BF16), top_score + jnp.log(totals)


def attend_back(queries, keys, values, log_total, grad_mixed):
    q, k, v, g = split_heads(queries), split_heads(keys), split_heads(values), split_heads(grad_mixed)
    scale_factor = q.shape[-1] ** (-0.5)
    scores = jnp.einsum("qhd,khd->hqk", q, k, preferred_element_type=F32) * scale_factor
    probs = jnp.exp(scores - log_total)
    probs_low = probs.astype(BF16)
    grad_probs = jnp.einsum("qhd,khd->hqk", g, v, preferred_element_type=F32)
    grad_scores = probs * (grad_probs - jnp.sum(probs * grad_probs, axis=-1, keepdims=True))
    grad_low = grad_scores.astype(BF16)
    grad_q = jnp.einsum("hqk,khd->qhd", grad_low, k, preferred_element_type=F32) * scale_factor
    grad_k = jnp.einsum("hqk,qhd->khd", grad_low, q, preferred_element_type=F32) * scale_factor
    grad_v = jnp.einsum("hqk,qhd->khd", probs_low, g, preferred_element_type=F32)
    return grad_q.reshape(queries.shape), grad_k.reshape(keys.shape), grad_v.reshape(keys.shape)


def layer_forward(stream, modulation, weights, biases):
    qkv_w, proj_w, fc1_w, fc2_w = weights
    qkv_b, proj_b, fc1_b, fc2_b = biases
    width = stream.shape[-1]
    shift_attn, factor_attn, gate_attn, shift_mlp, factor_mlp, gate_mlp = modulation
    normal, scale = normalize(stream)
    normed = (normal * (1.0 + factor_attn) + shift_attn).astype(BF16)
    queries, keys, values = [
        (dot(normed, qkv_w[part], (1,), (0,)) + qkv_b[part]).astype(BF16) for part in range(3)
    ]
    own_kv = jnp.stack([keys, values])
    both_kv = jnp.concatenate([own_kv, swap_pairs(own_kv, "rep")], axis=1)
    mixed, log_total = attend(queries, both_kv[0], both_kv[1])
    attn_out = dot(mixed, proj_w, (1,), (0,)) + proj_b
    middle = stream + gate_attn * attn_out
    normal_mlp, scale_mlp = normalize(middle)
    normed_mlp = (normal_mlp * (1.0 + factor_mlp) + shift_mlp).astype(BF16)
    hidden = jnp.concatenate(
        [dot(normed_mlp, fc1_w[part], (1,), (0,)) for part in range(fc1_w.shape[0])], axis=-1
    )
    hidden = hidden + fc1_b
    activated = jax.nn.gelu(hidden, approximate=True).astype(BF16)
    mlp_out = dot(activated, fc2_w, (1,), (0,)) + fc2_b
    result = middle + gate_mlp * mlp_out
    return result, (
        stream, normed, queries, both_kv, mixed, log_total, attn_out, middle, normed_mlp, hidden,
        activated, mlp_out,
    )


def token_sum(values):
    return jnp.sum(values.astype(F32), axis=0)


def by_shard(matrix, shards):
    return matrix.reshape(shards, matrix.shape[0] // shards, matrix.shape[1])


def layer_backward(grad_out, modulation, weights, kept, shards):
    qkv_w, proj_w, fc1_w, fc2_w = weights
    (
        stream, normed, queries, both_kv, mixed, log_total, attn_out, middle, normed_mlp, hidden,
        activated, mlp_out,
    ) = kept
    width = stream.shape[-1]
    half_tokens = stream.shape[0]
    shift_attn, factor_attn, gate_attn, shift_mlp, factor_mlp, gate_mlp = modulation
    grad_gate_mlp = token_sum(grad_out * mlp_out)
    grad_mlp = (grad_out * gate_mlp).astype(BF16)
    grad_fc2_w = dot(activated, grad_mlp, (0,), (0,)).astype(BF16)
    grad_fc2_b = token_sum(grad_mlp)
    grad_activated = dot(grad_mlp, fc2_w, (1,), (1,))
    _, gelu_pull = jax.vjp(lambda v: jax.nn.gelu(v, approximate=True), hidden)
    grad_hidden = gelu_pull(grad_activated)[0].astype(BF16)
    parts = [
        grad_hidden[:, part * width : (part + 1) * width] for part in range(fc1_w.shape[0])
    ]
    grad_fc1_w = [dot(normed_mlp, part, (0,), (0,)).astype(BF16) for part in parts]
    grad_fc1_b = token_sum(grad_hidden)
    grad_normed = sum(dot(part, fc1_w[at], (1,), (1,)) for at, part in enumerate(parts))
    fc2_grads = grad_fc2_w.reshape(shards, -1, width // shards, width)
    fc1_grads = jnp.stack([by_shard(part, shards) for part in grad_fc1_w], axis=1)
    mlp_grads = scatter(jnp.concatenate([fc1_grads, fc2_grads], axis=1))
    normal, scale = normalize(middle)
    grad_shift_mlp = token_sum(grad_normed)
    grad_factor_mlp = token_sum(grad_normed * normal)
    grad_middle = grad_out + norm_back(grad_normed, normal, scale, factor_mlp)
    grad_gate_attn = token_sum(grad_middle * attn_out)
    grad_attn = (grad_middle * gate_attn).astype(BF16)
    grad_proj_w = dot(mixed, grad_attn, (0,), (0,)).astype(BF16)
    grad_proj_b = token_sum(grad_attn)
    grad_mixed = dot(grad_attn, proj_w, (1,), (1,)).astype(BF16)
    grad_q, grad_k, grad_v = attend_back(queries, both_kv[0], both_kv[1], log_total, grad_mixed)
    returned = swap_pairs(
        jnp.stack([grad_k[half_tokens:], grad_v[half_tokens:]]).astype(BF16), "rep"
    )
    grad_k = grad_k[:half_tokens] + returned[0].astype(F32)
    grad_v = grad_v[:half_tokens] + returned[1].astype(F32)
    grad_projected = [part.astype(BF16) for part in (grad_q, grad_k, grad_v)]
    grad_qkv_w = [dot(normed, part, (0,), (0,)).astype(BF16) for part in grad_projected]
    attn_grads = scatter(
        jnp.stack([by_shard(part, shards) for part in grad_qkv_w + [grad_proj_w]], axis=1)
    )
    grad_qv_b = jnp.concatenate([token_sum(grad_projected[0]), token_sum(grad_projected[2])])
    grad_normed = sum(dot(part, qkv_w[at], (1,), (1,)) for at, part in enumerate(grad_projected))
    normal, scale = normalize(stream)
    grad_shift_attn = token_sum(grad_normed)
    grad_factor_attn = token_sum(grad_normed * normal)
    grad_stream = grad_middle + norm_back(grad_normed, normal, scale, factor_attn)
    grad_modulation = jnp.concatenate(
        [
            grad_shift_attn,
            grad_factor_attn,
            grad_gate_attn,
            grad_shift_mlp,
            grad_factor_mlp,
            grad_gate_mlp,
        ]
    )
    bias_grads = [
        part.reshape(shards, -1) for part in (grad_qv_b, grad_proj_b, grad_fc1_b, grad_fc2_b)
    ]
    return grad_stream, grad_modulation, jnp.concatenate(bias_grads, axis=1), mlp_grads, attn_grads


def columns(matrix, width):
    return jnp.stack(jnp.split(matrix, matrix.shape[1] // width, axis=1))


def uncolumns(blocks):
    return jnp.concatenate(list(blocks), axis=1)


def shards_program(
    latents,
    image_loads,
    timesteps,
    classes,
    label_table,
    ada_weight,
    ada_bias,
    qkv_weight,
    qv_bias,
    proj_weight,
    proj_bias,
    fc1_weight,
    fc1_bias,
    fc2_weight,
    fc2_bias,
    cotangent,
):
    shards = lax.axis_size("shard")
    width = latents.shape[2]
    own_rows = width // shards
    ff_parts = fc1_weight.shape[2] // width
    shard, rep, seq = lax.axis_index("shard"), lax.axis_index("rep"), lax.axis_index("seq")

    one_hot = (
        classes[:, None] == jnp.arange(label_table.shape[0], dtype=jnp.int32)[None, :]
    ).astype(BF16)
    cond = dot(one_hot, label_table, (1,), (0,)) + time_embed(timesteps, width)
    cond_low = jax.nn.silu(cond).astype(BF16)
    live_own = (image_loads > 0).astype(BF16)
    shared = lax.all_gather(
        jnp.concatenate([cond_low, jnp.broadcast_to(live_own[:, None], (1, 128))], axis=1),
        ("rep", "shard"),
        axis=0,
        tiled=True,
    )
    live = lax.dynamic_slice(shared, (seq * shards + shard, width), (1, 1)).astype(F32)
    cond_rows = lax.dynamic_slice(
        shared[:, :width], (0, shard * own_rows), (shared.shape[0], own_rows)
    )
    stream = swap_layout(latents[0]).astype(F32)

    packs = []
    for layer in range(LAYERS):
        fc2_piece = fc2_weight[layer].reshape(ff_parts, own_rows, width)
        rest = jnp.concatenate(
            [proj_weight[layer][None], columns(fc1_weight[layer], width), fc2_piece]
        )
        packs.append((columns(qkv_weight[layer], width), rest))
    gathered = []
    for layer in range(LAYERS):
        (qkv_w,) = gather(packs[layer][0], 0)
        rest_w, fc2_w = gather(packs[layer][1], ff_parts)
        gathered.append((qkv_w, rest_w[0], rest_w[1:], fc2_w.reshape(ff_parts * width, width)))

    small = jnp.concatenate([ada_bias, qv_bias, proj_bias, fc1_bias, fc2_bias], axis=1)
    small = lax.all_gather(small, "shard", axis=0, tiled=False).astype(F32)
    ends = [0]
    for bias in (ada_bias, qv_bias, proj_bias, fc1_bias, fc2_bias):
        ends.append(ends[-1] + bias.shape[1])
    biases, ada_b = [], []
    for layer in range(LAYERS):
        full = [small[:, layer, ends[at] : ends[at + 1]].reshape(-1) for at in range(5)]
        ada_b.append(full[0])
        qkv_b = [full[1][:width], jnp.zeros((width,), F32), full[1][width:]]
        biases.append((qkv_b, full[2], full[3], full[4]))

    mine = lax.dynamic_slice(cond_rows, (seq * shards, 0), (shards, own_rows))
    partial = jnp.concatenate(
        [dot(mine, ada_weight[layer], (1,), (0,)) for layer in range(LAYERS)], axis=1
    )
    modulations = lax.psum_scatter(partial, "shard", scatter_dimension=0, tiled=True)[0]
    modulations = [
        jnp.split((modulations.reshape(LAYERS, -1)[layer] + ada_b[layer])[None, :], 6, axis=1)
        for layer in range(LAYERS)
    ]

    kept = []
    for layer in range(LAYERS):
        stream, layer_kept = layer_forward(stream, modulations[layer], gathered[layer], biases[layer])
        kept.append(layer_kept)
    activations = swap_layout((stream * live).astype(BF16)).astype(F32)
    grad_stream = swap_layout(cotangent[0]).astype(F32) * live

    weight_grads = [None] * LAYERS
    bias_grads = [None] * LAYERS
    ada_w_grads = [None] * LAYERS
    ada_b_grads = [None] * LAYERS
    grad_cond = 0.0
    for layer in reversed(range(LAYERS)):
        grad_stream, grad_mod, bias_grads[layer], mlp_grads, attn_grads = layer_backward(
            grad_stream, modulations[layer], gathered[layer], kept[layer], shards
        )
        weight_grads[layer] = (
            uncolumns(attn_grads[:3]),
            attn_grads[3],
            uncolumns(mlp_grads[:ff_parts]),
            mlp_grads[ff_parts:].reshape(ff_parts * own_rows, width),
        )
        grad_mod = (grad_mod + swap_pairs(grad_mod, "rep")).astype(BF16)
        all_mod = lax.all_gather(grad_mod, ("seq", "shard"), axis=0, tiled=False)
        ada_w_grads[layer] = dot(cond_rows, all_mod, (0,), (0,))
        own_mod = lax.dynamic_slice(
            all_mod, (0, shard * ada_bias.shape[1]), (all_mod.shape[0], ada_bias.shape[1])
        )
        ada_b_grads[layer] = token_sum(own_mod)
        rep_mod = lax.dynamic_slice(all_mod, (rep * shards, 0), (shards, all_mod.shape[1]))
        grad_cond = grad_cond + dot(rep_mod, ada_weight[layer], (1,), (1,))

    latent_grad = swap_layout(grad_stream.astype(BF16)).astype(F32)
    all_cond = lax.all_gather(grad_cond, "shard", axis=0, tiled=False)
    grad_cond_low = lax.dynamic_slice(all_cond, (0, shard, 0), (shards, 1, own_rows)).reshape(
        1, width
    )
    _, silu_pull = jax.vjp(jax.nn.silu, cond)
    cond_grad = silu_pull(grad_cond_low)[0]

    bias_total = lax.psum_scatter(
        jnp.concatenate(bias_grads, axis=1), "shard", scatter_dimension=0, tiled=True
    ).reshape(LAYERS, -1)
    bias_total = bias_total + swap_pairs(bias_total, "rep")
    bias_total = bias_total + swap_pairs(bias_total, "seq")
    qv_b, proj_b, fc1_b, fc2_b = [
        bias_total[:, ends[at] - ends[1] : ends[at + 1] - ends[1]] for at in range(1, 5)
    ]
    qkv_g, proj_g, fc1_g, fc2_g = [
        jnp.stack([weight_grads[layer][at] for layer in range(LAYERS)]) for at in range(4)
    ]
    return (
        activations[None],
        latent_grad[None],
        cond_grad,
        jnp.stack(ada_w_grads),
        jnp.stack(ada_b_grads),
        qkv_g,
        qv_b,
        proj_g,
        proj_b,
        fc1_g,
        fc1_b,
        fc2_g,
        fc2_b,
    )


def solution(mesh):
    tokens = P(("rep", "shard"), "seq", None)
    images = P(("rep", "shard"))
    matrix = P(None, "shard", None)
    vector = P(None, "shard")
    return jax.shard_map(
        shards_program,
        mesh=mesh,
        in_specs=(tokens, images, images, images, P())
        + (matrix, vector) * 5
        + (tokens,),
        out_specs=(tokens, tokens, P(("rep", "shard"), None)) + (matrix, vector) * 5,
        check_vma=False,
    )
```

```python
import functools
import math

import jax
import jax.numpy as jnp
from jax import lax
from jax.experimental import pallas as pl
from jax.experimental.pallas import tpu as pltpu
from jax.sharding import PartitionSpec as P

HEADS = 12
LAYERS = 2
EPSILON = 1e-06
BF16 = jnp.bfloat16
F32 = jnp.float32


def swap_pairs(value, axis):
    return lax.ppermute(value, axis, [(0, 1), (1, 0)])


def swap_layout(value):
    return lax.ppermute(value, ("rep", "seq"), [(0, 0), (1, 2), (2, 1), (3, 3)])


def cube_pairs(value, axis, bit):
    return lax.ppermute(value, axis, [(at, at ^ bit) for at in range(lax.axis_size(axis))])


def cube_bits(axis):
    return [1 << place for place in range(lax.axis_size(axis).bit_length() - 1)]


def cube_gather(value, axes):
    value = value[None]
    for axis in reversed(axes):
        for bit in cube_bits(axis):
            other = cube_pairs(value, axis, bit)
            value = jnp.where(
                lax.axis_index(axis) & bit == 0,
                jnp.concatenate([value, other]),
                jnp.concatenate([other, value]),
            )
    return value


def cube_scatter(value, axis):
    for bit in reversed(cube_bits(axis)):
        low, high = value[:bit], value[bit:]
        first = lax.axis_index(axis) & bit == 0
        value = jnp.where(first, low, high) + cube_pairs(jnp.where(first, high, low), axis, bit)
    return value[0]


def ring_order(size):
    half = size // 2
    return [2 * place for place in range(half)] + [2 * place + 1 for place in reversed(range(half))]


def ring_step(value, forward):
    size = lax.axis_size("shard")
    order = ring_order(size)
    step = 1 if forward else size - 1
    return lax.ppermute(
        value, "shard", [(order[at], order[(at + step) % size]) for at in range(size)]
    )


def ring_ids():
    size = lax.axis_size("shard")
    order = ring_order(size)
    places = [order.index(shard) for shard in range(size)]
    place = jnp.array(places, jnp.int32)[lax.axis_index("shard")]
    return jnp.array(order, jnp.int32)[(place + jnp.arange(size, dtype=jnp.int32)) % size]


OFFSETS = (-1, 1, -2, 2, -3, 3, 4)


def place_kernel(plain, split, where, *refs):
    (own, *rest) = refs[:19]
    outs = refs[19:-1]
    sem = refs[-1]
    blocks, near_x, far_x = rest[0:7], rest[7], rest[8]
    core_blocks, core_near_x, core_far_x = rest[9:16], rest[16], rest[17]
    rep, seq = where[8], where[9]
    unit = own.shape[1] // 6

    def put(src, shard, row, rows):
        copies = []
        if plain:
            start = pl.multiple_of(shard * (6 * unit) + row * unit, unit)
            copies.append(
                pltpu.make_async_copy(src.at[0:plain], outs[0].at[:, pl.ds(start, rows), :], sem)
            )
        if split:
            start = pl.multiple_of(row * unit, unit)
            copies.append(
                pltpu.make_async_copy(
                    src.at[plain : plain + split],
                    outs[-1].at[shard, :, pl.ds(start, rows), :],
                    sem,
                )
            )
        for copy in copies:
            copy.start()
        return copies

    copies = put(own, where[0], 0, 6 * unit)
    for slot, offset in enumerate(OFFSETS):
        shard = where[offset % 8]
        beside = (near_x, core_near_x) if slot < 4 else (far_x, core_far_x)
        at = slot if slot < 4 else slot - 4
        copies += put(blocks[slot], shard, 3 * rep + seq, 2 * unit)
        copies += put(beside[0].at[at], shard, 3 * rep + 2 * (1 - seq), unit)
        copies += put(core_blocks[slot], shard, 3 * (1 - rep) + seq, 2 * unit)
        copies += put(beside[1].at[at], shard, 3 * (1 - rep) + 2 * (1 - seq), unit)
    for copy in copies:
        copy.wait()


def gather_ring(piece, split):
    count, rows, width = piece.shape
    shards = lax.axis_size("shard")
    unit = rows // 6
    rep, seq = lax.axis_index("rep"), lax.axis_index("seq")
    mine = lax.dynamic_slice(piece, (0, (3 * rep + seq) * unit, 0), (count, 2 * unit, width))

    def cross(blocks):
        cut = [
            lax.dynamic_slice(block, (0, seq * unit, 0), (count, unit, width)) for block in blocks
        ]
        return swap_pairs(jnp.stack(cut), "seq")

    up1, down1 = ring_step(mine, True), ring_step(mine, False)
    up2, down2 = ring_step(up1, True), ring_step(down1, False)
    near_x = cross([up1, down1, up2, down2])
    up3, down3 = ring_step(up2, True), ring_step(down2, False)
    up4, down4 = ring_step(up3[:, :unit], True), ring_step(down3[:, unit:], False)
    far = jnp.concatenate([up4, down4], axis=1)
    far_x = cross([up3, down3, far])
    parts = [up1, down1, up2, down2, up3, down3, far, near_x, far_x]
    parts += [swap_pairs(part, "rep") for part in parts]
    where = jnp.concatenate([ring_ids(), jnp.stack([rep, seq]).astype(jnp.int32)])
    plain = count - split
    shapes = []
    if plain:
        shapes.append(jax.ShapeDtypeStruct((plain, shards * rows, width), piece.dtype))
    if split:
        shapes.append(jax.ShapeDtypeStruct((shards, split, rows, width), piece.dtype))
    anywhere = pl.BlockSpec(memory_space=pl.ANY)
    return pl.pallas_call(
        functools.partial(place_kernel, plain, split),
        out_shape=tuple(shapes),
        in_specs=[pl.BlockSpec(memory_space=pltpu.SMEM)] + [anywhere] * 19,
        out_specs=(pl.BlockSpec(memory_space=pltpu.VMEM),) * len(shapes),
        compiler_params=pltpu.CompilerParams(vmem_limit_bytes=32 * 2**20),
        scratch_shapes=[pltpu.SemaphoreType.DMA],
        cost_estimate=pl.CostEstimate(
            flops=0, transcendentals=0, bytes_accessed=2 * shards * piece.size * 2
        ),
    )(where, piece, *parts)


def gather_plain(piece, split):
    count, rows, width = piece.shape
    shards = lax.axis_size("shard")
    plain = count - split
    outs = []
    if plain:
        outs.append(lax.all_gather(piece[:plain], "shard", axis=1, tiled=True))
    if split:
        outs.append(lax.all_gather(piece[plain:], "shard", axis=0, tiled=False))
    return tuple(outs)


def ring_fits(rows):
    return (
        lax.axis_size("shard") == 8
        and lax.axis_size("rep") == 2
        and lax.axis_size("seq") == 2
        and rows % 96 == 0
    )


def gather(piece, split):
    return (gather_ring if ring_fits(piece.shape[1]) else gather_plain)(piece, split)


def add(left, right):
    return (left.astype(F32) + right.astype(F32)).astype(BF16)


def scatter_ring(grads):
    shards, count, rows, width = grads.shape
    unit = rows // 6
    rep, seq = lax.axis_index("rep"), lax.axis_index("seq")
    ids = ring_ids()

    def half(which):
        return lax.dynamic_slice(
            grads, (0, 0, 3 * unit * which, 0), (shards, count, 3 * unit, width)
        )

    (got,) = yield (swap_pairs(half(1 - rep), "rep"),)
    paired = add(half(rep), got)

    def block(offset):
        return lax.dynamic_index_in_dim(paired, ids[offset % 8], 0, keepdims=False)

    def send(offsets):
        sent = [
            lax.dynamic_slice(block(offset), (0, 2 * (1 - seq) * unit, 0), (count, unit, width))
            for offset in offsets
        ]
        return swap_pairs(jnp.stack(sent), "seq")

    def join(offset, got):
        kept = lax.dynamic_slice(block(offset), (0, seq * unit, 0), (count, 2 * unit, width))
        zero = jnp.zeros_like(got)
        beside = jnp.where(
            seq == 0,
            jnp.concatenate([got, zero], axis=1),
            jnp.concatenate([zero, got], axis=1),
        )
        return add(kept, beside)

    far, near3 = yield (send((4,)), send((3, -3)))
    far = join(4, far[0])
    up, down, near2 = yield (
        ring_step(far[:, :unit], True),
        ring_step(far[:, unit:], False),
        send((2, -2)),
    )
    up3, down3 = join(3, near3[0]), join(-3, near3[1])
    up = jnp.concatenate([add(up3[:, :unit], up), up3[:, unit:]], axis=1)
    down = jnp.concatenate([down3[:, :unit], add(down3[:, unit:], down)], axis=1)
    up, down, near1 = yield (ring_step(up, True), ring_step(down, False), send((1, -1)))
    up, down, here = yield (
        ring_step(add(join(2, near2[0]), up), True),
        ring_step(add(join(-2, near2[1]), down), False),
        send((0,)),
    )
    up, down = yield (
        ring_step(add(join(1, near1[0]), up), True),
        ring_step(add(join(-1, near1[1]), down), False),
    )
    total = add(join(0, here[0]).astype(F32) + up.astype(F32), down)
    (other,) = yield (swap_pairs(total, "seq"),)
    left, right = jnp.where(seq == 0, total, other), jnp.where(seq == 0, other, total)
    mine = jnp.concatenate(
        [left[:, :unit], add(left[:, unit:], right[:, :unit]), right[:, unit:]], axis=1
    )
    (other,) = yield (swap_pairs(mine, "rep"),)
    return jnp.where(
        rep == 0,
        jnp.concatenate([mine, other], axis=1),
        jnp.concatenate([other, mine], axis=1),
    ).astype(F32)


class Background:
    def __init__(self):
        self.running = []
        self.done = {}

    def start(self, key, grads):
        if not ring_fits(grads.shape[2]):
            self.done[key] = scatter_plain(grads)
            return
        stages = scatter_ring(grads)
        self.running.append((key, stages, next(stages)))

    def tick(self, value=None):
        waiting = [moving for _, _, moving in self.running]
        if value is not None and waiting:
            value, waiting = lax.optimization_barrier((value, waiting))
        still = []
        for (key, stages, _), moving in zip(self.running, waiting):
            try:
                still.append((key, stages, stages.send(moving)))
            except StopIteration as end:
                self.done[key] = end.value
        self.running = still
        return value

    def finish(self):
        while self.running:
            self.tick()
        return self.done


def scatter_plain(grads):
    owned = lax.psum_scatter(grads.astype(F32), "shard", scatter_dimension=0, tiled=False)
    return lax.psum(owned.astype(BF16), ("rep", "seq")).astype(F32)


def normalize(values):
    centered = values - jnp.mean(values, axis=-1, keepdims=True)
    scale = lax.rsqrt(jnp.mean(centered * centered, axis=-1, keepdims=True) + EPSILON)
    return centered * scale, scale


def norm_back(grad, normal, scale, factor):
    u = grad * (1.0 + factor)
    return (
        u
        - jnp.mean(u, axis=-1, keepdims=True)
        - normal * jnp.mean(u * normal, axis=-1, keepdims=True)
    ) * scale


def time_embed(steps, width):
    half_width = width // 2
    freqs = jnp.exp(-math.log(10000.0) * jnp.arange(half_width, dtype=F32) / half_width)
    angles = steps.astype(F32)[:, None] * freqs[None, :]
    return jnp.concatenate([jnp.cos(angles), jnp.sin(angles)], axis=-1)


def dot(left, right, left_dims, right_dims):
    return lax.dot_general(
        left, right, ((left_dims, right_dims), ((), ())), preferred_element_type=F32
    )


def nt(left, right, **kw):
    return lax.dot_general(left, right, (((1,), (1,)), ((), ())), preferred_element_type=F32, **kw)


def tn(left, right):
    return lax.dot_general(left, right, (((0,), (0,)), ((), ())), preferred_element_type=F32)


def nn(left, right):
    return lax.dot_general(left, right, (((1,), (0,)), ((), ())), preferred_element_type=F32)


def head_mask(values, head, size):
    lanes = lax.broadcasted_iota(jnp.int32, values.shape, 1)
    inside = (lanes >= head * size) & (lanes < (head + 1) * size)
    return jnp.where(inside, values, jnp.zeros_like(values))


def attend_kernel(size, q_ref, own_ref, other_ref, mixed_ref, log_ref):
    pair = q_ref.shape[1] // size
    queries = q_ref[...] * jnp.asarray(size**-0.5, BF16)
    blocks = []
    for head in range(pair):
        query = head_mask(queries, head, size)
        scores = [nt(own_ref[0], query), nt(other_ref[0], query)]
        top = jnp.maximum(*[jnp.max(part, axis=0, keepdims=True) for part in scores])
        expo = [jnp.exp(part - top) for part in scores]
        totals = sum(jnp.sum(part, axis=0, keepdims=True) for part in expo)
        mixed = tn(own_ref[1], expo[0].astype(BF16)) + tn(other_ref[1], expo[1].astype(BF16))
        blocks.append(mixed[head * size : (head + 1) * size] / totals)
        log_ref[0, head : head + 1, :] = top + jnp.log(totals)
    mixed_ref[...] = jnp.transpose(jnp.concatenate(blocks, axis=0)).astype(BF16)


def attend(queries, own_kv, other_kv):
    tokens, width = queries.shape
    pair = 128 // (width // HEADS)
    groups = HEADS // pair
    kv_spec = pl.BlockSpec((2, tokens, 128), lambda group: (0, 0, group))
    token_spec = pl.BlockSpec((tokens, 128), lambda group: (0, group))
    flops = 8 * tokens * tokens * width
    return pl.pallas_call(
        functools.partial(attend_kernel, width // HEADS),
        grid=(groups,),
        in_specs=[token_spec, kv_spec, kv_spec],
        out_specs=(token_spec, pl.BlockSpec((1, pair, tokens), lambda group: (group, 0, 0))),
        out_shape=(
            jax.ShapeDtypeStruct((tokens, width), BF16),
            jax.ShapeDtypeStruct((groups, pair, tokens), F32),
        ),
        compiler_params=pltpu.CompilerParams(vmem_limit_bytes=40 * 2**20),
        cost_estimate=pl.CostEstimate(
            flops=4 * flops, transcendentals=2 * HEADS * tokens**2, bytes_accessed=12 * queries.size
        ),
    )(queries, own_kv, other_kv)


def attend_back_kernel(
    size, q_ref, own_ref, other_ref, grad_ref, mixed_ref, log_ref, dq_ref, down_ref, dother_ref
):
    pair = q_ref.shape[1] // size
    scale = jnp.asarray(size**-0.5, BF16)
    queries = q_ref[...] * scale
    product = grad_ref[...].astype(F32) * mixed_ref[...].astype(F32)
    ones = jnp.ones((8, product.shape[1]), F32)
    grad_queries = []
    grad_kv = {}
    for head in range(pair):
        query, grad = head_mask(queries, head, size), head_mask(grad_ref[...], head, size)
        delta = nt(ones, head_mask(product, head, size), precision=lax.Precision.HIGHEST)[0:1]
        log_total = log_ref[0, head : head + 1, :]
        grad_query = None
        for side, kv_ref in enumerate((own_ref, other_ref)):
            probs = jnp.exp(nt(kv_ref[0], query) - log_total)
            grad_scores = (probs * (nt(kv_ref[1], grad) - delta)).astype(BF16)
            parts = (nn(grad_scores, query), nn(probs.astype(BF16), grad))
            before = grad_kv.get(side)
            grad_kv[side] = parts if before is None else tuple(a + b for a, b in zip(before, parts))
            part = tn(kv_ref[0], grad_scores)[head * size : (head + 1) * size]
            grad_query = part if grad_query is None else grad_query + part
        grad_queries.append(grad_query)
    total = jnp.transpose(jnp.concatenate(grad_queries, axis=0)) * (size**-0.5)
    dq_ref[...] = total.astype(BF16)
    for side, out_ref in enumerate((down_ref, dother_ref)):
        for at in range(2):
            out_ref[at] = grad_kv[side][at].astype(out_ref.dtype)


def attend_back(queries, own_kv, other_kv, grad_mixed, mixed, log_total):
    tokens, width = queries.shape
    pair = 128 // (width // HEADS)
    groups = HEADS // pair
    kv_spec = pl.BlockSpec((2, tokens, 128), lambda group: (0, 0, group))
    token_spec = pl.BlockSpec((tokens, 128), lambda group: (0, group))
    flops = 20 * tokens * tokens * width
    return pl.pallas_call(
        functools.partial(attend_back_kernel, width // HEADS),
        grid=(groups,),
        in_specs=[
            token_spec,
            kv_spec,
            kv_spec,
            token_spec,
            token_spec,
            pl.BlockSpec((1, pair, tokens), lambda group: (group, 0, 0)),
        ],
        out_specs=(token_spec, kv_spec, kv_spec),
        out_shape=(
            jax.ShapeDtypeStruct((tokens, width), BF16),
            jax.ShapeDtypeStruct(own_kv.shape, F32),
            jax.ShapeDtypeStruct(own_kv.shape, BF16),
        ),
        compiler_params=pltpu.CompilerParams(vmem_limit_bytes=40 * 2**20),
        cost_estimate=pl.CostEstimate(
            flops=4 * flops, transcendentals=2 * HEADS * tokens**2, bytes_accessed=24 * queries.size
        ),
    )(queries, own_kv, other_kv, grad_mixed, mixed, log_total)


def layer_forward(stream, modulation, weights, biases):
    qkv_w, proj_w, fc1_w, fc2_w = weights
    qkv_b, proj_b, fc1_b, fc2_b = biases
    width = stream.shape[-1]
    shift_attn, factor_attn, gate_attn, shift_mlp, factor_mlp, gate_mlp = modulation
    normal, scale = normalize(stream)
    normed = (normal * (1.0 + factor_attn) + shift_attn).astype(BF16)
    queries, keys, values = [
        (dot(normed, qkv_w[part], (1,), (0,)) + qkv_b[part]).astype(BF16) for part in range(3)
    ]
    own_kv = jnp.stack([keys, values])
    other_kv = swap_pairs(own_kv, "rep")
    mixed, log_total = attend(queries, own_kv, other_kv)
    attn_out = dot(mixed, proj_w, (1,), (0,)) + proj_b
    middle = stream + gate_attn * attn_out
    normal_mlp, scale_mlp = normalize(middle)
    normed_mlp = (normal_mlp * (1.0 + factor_mlp) + shift_mlp).astype(BF16)
    hidden = jnp.concatenate(
        [dot(normed_mlp, fc1_w[part], (1,), (0,)) for part in range(fc1_w.shape[0])], axis=-1
    )
    hidden = hidden + fc1_b
    activated = jax.nn.gelu(hidden, approximate=True).astype(BF16)
    mlp_out = dot(activated, fc2_w, (1,), (0,)) + fc2_b
    result = middle + gate_mlp * mlp_out
    return result, (
        stream, normed, queries, own_kv, other_kv, mixed, log_total, attn_out, middle, normed_mlp, hidden,
        activated, mlp_out,
    )


def token_sum(values):
    return jnp.sum(values.astype(F32), axis=0)


def by_shard(matrix, shards):
    return matrix.reshape(shards, matrix.shape[0] // shards, matrix.shape[1])


def layer_backward(layer, grad_out, modulation, weights, kept, shards, background):
    qkv_w, proj_w, fc1_w, fc2_w = weights
    (
        stream, normed, queries, own_kv, other_kv, mixed, log_total, attn_out, middle, normed_mlp, hidden,
        activated, mlp_out,
    ) = kept
    width = stream.shape[-1]
    shift_attn, factor_attn, gate_attn, shift_mlp, factor_mlp, gate_mlp = modulation
    grad_gate_mlp = token_sum(grad_out * mlp_out)
    grad_mlp = (grad_out * gate_mlp).astype(BF16)
    grad_fc2_w = dot(activated, grad_mlp, (0,), (0,)).astype(BF16)
    grad_fc2_b = token_sum(grad_mlp)
    grad_mlp = background.tick(grad_mlp)
    grad_activated = dot(grad_mlp, fc2_w, (1,), (1,))
    _, gelu_pull = jax.vjp(lambda v: jax.nn.gelu(v, approximate=True), hidden)
    grad_hidden = gelu_pull(grad_activated)[0].astype(BF16)
    parts = [
        grad_hidden[:, part * width : (part + 1) * width] for part in range(fc1_w.shape[0])
    ]
    parts = background.tick(parts)
    grad_fc1_w = [dot(normed_mlp, part, (0,), (0,)).astype(BF16) for part in parts]
    grad_fc1_b = token_sum(grad_hidden)
    grad_normed = sum(dot(part, fc1_w[at], (1,), (1,)) for at, part in enumerate(parts))
    fc2_grads = grad_fc2_w.reshape(shards, -1, width // shards, width)
    fc1_grads = jnp.stack([by_shard(part, shards) for part in grad_fc1_w], axis=1)
    grad_normed = background.tick(grad_normed)
    background.start(("mlp", layer), jnp.concatenate([fc1_grads, fc2_grads], axis=1))
    normal, scale = normalize(middle)
    grad_shift_mlp = token_sum(grad_normed)
    grad_factor_mlp = token_sum(grad_normed * normal)
    grad_middle = grad_out + norm_back(grad_normed, normal, scale, factor_mlp)
    grad_gate_attn = token_sum(grad_middle * attn_out)
    grad_attn = (grad_middle * gate_attn).astype(BF16)
    grad_proj_w = dot(mixed, grad_attn, (0,), (0,)).astype(BF16)
    grad_proj_b = token_sum(grad_attn)
    grad_attn = background.tick(grad_attn)
    grad_mixed = dot(grad_attn, proj_w, (1,), (1,)).astype(BF16)
    grad_mixed = background.tick(grad_mixed)
    grad_q, grad_own, grad_other = attend_back(
        queries, own_kv, other_kv, grad_mixed, mixed, log_total
    )
    grad_own = background.tick(grad_own)
    grad_kv = (grad_own + swap_pairs(grad_other, "rep").astype(F32)).astype(BF16)
    grad_projected = [grad_q, grad_kv[0], grad_kv[1]]
    grad_qkv_w = [dot(normed, part, (0,), (0,)).astype(BF16) for part in grad_projected]
    grad_qkv_w = background.tick(grad_qkv_w)
    background.start(
        ("attn", layer),
        jnp.stack([by_shard(part, shards) for part in grad_qkv_w + [grad_proj_w]], axis=1),
    )
    grad_qv_b = jnp.concatenate([token_sum(grad_projected[0]), token_sum(grad_projected[2])])
    grad_normed = sum(dot(part, qkv_w[at], (1,), (1,)) for at, part in enumerate(grad_projected))
    normal, scale = normalize(stream)
    grad_shift_attn = token_sum(grad_normed)
    grad_factor_attn = token_sum(grad_normed * normal)
    grad_normed = background.tick(grad_normed)
    grad_stream = grad_middle + norm_back(grad_normed, normal, scale, factor_attn)
    grad_modulation = jnp.concatenate(
        [
            grad_shift_attn,
            grad_factor_attn,
            grad_gate_attn,
            grad_shift_mlp,
            grad_factor_mlp,
            grad_gate_mlp,
        ]
    )
    bias_grads = [
        part.reshape(shards, -1) for part in (grad_qv_b, grad_proj_b, grad_fc1_b, grad_fc2_b)
    ]
    return grad_stream, grad_modulation, jnp.concatenate(bias_grads, axis=1)


def columns(matrix, width):
    return jnp.stack(jnp.split(matrix, matrix.shape[1] // width, axis=1))


def uncolumns(blocks):
    return jnp.concatenate(list(blocks), axis=1)


def shards_program(
    latents,
    image_loads,
    timesteps,
    classes,
    label_table,
    ada_weight,
    ada_bias,
    qkv_weight,
    qv_bias,
    proj_weight,
    proj_bias,
    fc1_weight,
    fc1_bias,
    fc2_weight,
    fc2_bias,
    cotangent,
):
    shards = lax.axis_size("shard")
    width = latents.shape[2]
    own_rows = width // shards
    ff_parts = fc1_weight.shape[2] // width
    shard, rep, seq = lax.axis_index("shard"), lax.axis_index("rep"), lax.axis_index("seq")

    one_hot = (
        classes[:, None] == jnp.arange(label_table.shape[0], dtype=jnp.int32)[None, :]
    ).astype(BF16)
    cond = dot(one_hot, label_table, (1,), (0,)) + time_embed(timesteps, width)
    cond_low = jax.nn.silu(cond).astype(BF16)
    live_own = (image_loads > 0).astype(BF16)
    shared = cube_gather(
        jnp.concatenate([cond_low[0], jnp.broadcast_to(live_own, (128,))]), ("rep", "shard")
    )
    live = lax.dynamic_slice(shared, (seq * shards + shard, width), (1, 1)).astype(F32)
    cond_rows = lax.dynamic_slice(
        shared[:, :width], (0, shard * own_rows), (shared.shape[0], own_rows)
    )
    stream = swap_layout(latents[0]).astype(F32)

    packs = []
    for layer in range(LAYERS):
        fc2_piece = fc2_weight[layer].reshape(ff_parts, own_rows, width)
        rest = jnp.concatenate(
            [proj_weight[layer][None], columns(fc1_weight[layer], width), fc2_piece]
        )
        packs.append((columns(qkv_weight[layer], width), rest))
    gathered = []
    for layer in range(LAYERS):
        (qkv_w,) = gather(packs[layer][0], 0)
        rest_w, fc2_w = gather(packs[layer][1], ff_parts)
        gathered.append((qkv_w, rest_w[0], rest_w[1:], fc2_w.reshape(ff_parts * width, width)))

    small = jnp.concatenate([ada_bias, qv_bias, proj_bias, fc1_bias, fc2_bias], axis=1)
    small = cube_gather(small, ("shard",)).astype(F32)
    ends = [0]
    for bias in (ada_bias, qv_bias, proj_bias, fc1_bias, fc2_bias):
        ends.append(ends[-1] + bias.shape[1])
    biases, ada_b = [], []
    for layer in range(LAYERS):
        full = [small[:, layer, ends[at] : ends[at + 1]].reshape(-1) for at in range(5)]
        ada_b.append(full[0])
        qkv_b = [full[1][:width], jnp.zeros((width,), F32), full[1][width:]]
        biases.append((qkv_b, full[2], full[3], full[4]))

    mine = lax.dynamic_slice(cond_rows, (seq * shards, 0), (shards, own_rows))
    partial = jnp.concatenate(
        [dot(mine, ada_weight[layer], (1,), (0,)) for layer in range(LAYERS)], axis=1
    )
    modulations = cube_scatter(partial, "shard")
    modulations = [
        jnp.split((modulations.reshape(LAYERS, -1)[layer] + ada_b[layer])[None, :], 6, axis=1)
        for layer in range(LAYERS)
    ]

    kept = []
    for layer in range(LAYERS):
        stream, layer_kept = layer_forward(stream, modulations[layer], gathered[layer], biases[layer])
        kept.append(layer_kept)
    activations = swap_layout((stream * live).astype(BF16)).astype(F32)
    grad_stream = swap_layout(cotangent[0]).astype(F32) * live

    weight_grads = [None] * LAYERS
    background = Background()
    bias_grads = [None] * LAYERS
    ada_w_grads = [None] * LAYERS
    ada_b_grads = [None] * LAYERS
    grad_cond = 0.0
    for layer in reversed(range(LAYERS)):
        grad_stream, grad_mod, bias_grads[layer] = layer_backward(
            layer, grad_stream, modulations[layer], gathered[layer], kept[layer], shards, background
        )
        grad_mod = (grad_mod + swap_pairs(grad_mod, "rep")).astype(BF16)
        all_mod = cube_gather(grad_mod, ("seq", "shard"))
        ada_w_grads[layer] = dot(cond_rows, all_mod, (0,), (0,))
        own_mod = lax.dynamic_slice(
            all_mod, (0, shard * ada_bias.shape[1]), (all_mod.shape[0], ada_bias.shape[1])
        )
        ada_b_grads[layer] = token_sum(own_mod)
        rep_mod = lax.dynamic_slice(all_mod, (rep * shards, 0), (shards, all_mod.shape[1]))
        grad_cond = grad_cond + dot(rep_mod, ada_weight[layer], (1,), (1,))

    latent_grad = swap_layout(grad_stream.astype(BF16)).astype(F32)
    all_cond = cube_gather(grad_cond, ("shard",))
    grad_cond_low = lax.dynamic_slice(all_cond, (0, shard, 0), (shards, 1, own_rows)).reshape(
        1, width
    )
    _, silu_pull = jax.vjp(jax.nn.silu, cond)
    cond_grad = silu_pull(grad_cond_low)[0]

    bias_total = cube_scatter(jnp.stack(bias_grads, axis=1), "shard")
    bias_total = bias_total + swap_pairs(bias_total, "rep")
    bias_total = bias_total + swap_pairs(bias_total, "seq")
    qv_b, proj_b, fc1_b, fc2_b = [
        bias_total[:, ends[at] - ends[1] : ends[at + 1] - ends[1]] for at in range(1, 5)
    ]
    done = background.finish()
    for layer in range(LAYERS):
        attn_grads, mlp_grads = done["attn", layer], done["mlp", layer]
        weight_grads[layer] = (
            uncolumns(attn_grads[:3]),
            attn_grads[3],
            uncolumns(mlp_grads[:ff_parts]),
            mlp_grads[ff_parts:].reshape(ff_parts * own_rows, width),
        )
    qkv_g, proj_g, fc1_g, fc2_g = [
        jnp.stack([weight_grads[layer][at] for layer in range(LAYERS)]) for at in range(4)
    ]
    return (
        activations[None],
        latent_grad[None],
        cond_grad,
        jnp.stack(ada_w_grads),
        jnp.stack(ada_b_grads),
        qkv_g,
        qv_b,
        proj_g,
        proj_b,
        fc1_g,
        fc1_b,
        fc2_g,
        fc2_b,
    )


def solution(mesh):
    tokens = P(("rep", "shard"), "seq", None)
    images = P(("rep", "shard"))
    matrix = P(None, "shard", None)
    vector = P(None, "shard")
    return jax.shard_map(
        shards_program,
        mesh=mesh,
        in_specs=(tokens, images, images, images, P())
        + (matrix, vector) * 5
        + (tokens,),
        out_specs=(tokens, tokens, P(("rep", "shard"), None)) + (matrix, vector) * 5,
        check_vma=False,
    )
```

```python
import functools
import math

import jax
import jax.numpy as jnp
from jax import lax
from jax.experimental import pallas as pl
from jax.experimental.pallas import tpu as pltpu
from jax.sharding import PartitionSpec as P

HEADS = 12
LAYERS = 2
EPSILON = 1e-06
BF16 = jnp.bfloat16
F32 = jnp.float32


def swap_pairs(value, axis):
    return lax.ppermute(value, axis, [(0, 1), (1, 0)])


def swap_layout(value):
    moved = lax.ppermute(value, ("rep", "seq"), [(1, 2), (2, 1)])
    return jnp.where(lax.axis_index("rep") == lax.axis_index("seq"), value, moved)


def cube_pairs(value, axis, bit):
    return lax.ppermute(value, axis, [(at, at ^ bit) for at in range(lax.axis_size(axis))])


def cube_bits(axis):
    return [1 << place for place in range(lax.axis_size(axis).bit_length() - 1)]


def cube_gather(value, axes):
    value = value[None]
    for axis in reversed(axes):
        for bit in cube_bits(axis):
            other = cube_pairs(value, axis, bit)
            value = jnp.where(
                lax.axis_index(axis) & bit == 0,
                jnp.concatenate([value, other]),
                jnp.concatenate([other, value]),
            )
    return value


def cube_scatter(value, axis):
    for bit in reversed(cube_bits(axis)):
        low, high = value[:bit], value[bit:]
        first = lax.axis_index(axis) & bit == 0
        value = jnp.where(first, low, high) + cube_pairs(jnp.where(first, high, low), axis, bit)
    return value[0]


def ring_order(size):
    half = size // 2
    return [2 * place for place in range(half)] + [2 * place + 1 for place in reversed(range(half))]


def ring_step(value, forward):
    size = lax.axis_size("shard")
    order = ring_order(size)
    step = 1 if forward else size - 1
    return lax.ppermute(
        value, "shard", [(order[at], order[(at + step) % size]) for at in range(size)]
    )


def ring_ids():
    size = lax.axis_size("shard")
    order = ring_order(size)
    places = [order.index(shard) for shard in range(size)]
    place = jnp.array(places, jnp.int32)[lax.axis_index("shard")]
    return jnp.array(order, jnp.int32)[(place + jnp.arange(size, dtype=jnp.int32)) % size]


OFFSETS = (-1, 1, -2, 2, -3, 3, 4)


def place_kernel(where, *refs):
    (own, *rest) = refs[:23]
    out, sem = refs[23:]
    blocks, beside = rest[0:7], rest[7:11]
    core_blocks, core_beside = rest[11:18], rest[18:22]
    rep, seq = where[8], where[9]
    unit = own.shape[1] // 6

    def put(src, shard, row, rows):
        start = pl.multiple_of(row * unit, unit)
        copy = pltpu.make_async_copy(src, out.at[shard, :, pl.ds(start, rows), :], sem)
        copy.start()
        return [copy]

    copies = put(own, where[0], 0, 6 * unit)
    for slot, offset in enumerate(OFFSETS):
        shard = where[offset % 8]
        far = 3 * rep + 2 * (1 - seq)
        copies += put(blocks[slot], shard, 3 * rep + seq, 2 * unit)
        copies += put(beside[slot // 2].at[slot % 2], shard, far, unit)
        far = 3 * (1 - rep) + 2 * (1 - seq)
        copies += put(core_blocks[slot], shard, 3 * (1 - rep) + seq, 2 * unit)
        copies += put(core_beside[slot // 2].at[slot % 2], shard, far, unit)
    for copy in copies:
        copy.wait()


def gather_ring(piece):
    count, rows, width = piece.shape
    shards = lax.axis_size("shard")
    unit = rows // 6
    rep, seq = lax.axis_index("rep"), lax.axis_index("seq")
    mine = lax.dynamic_slice(piece, (0, (3 * rep + seq) * unit, 0), (count, 2 * unit, width))

    def cross(*blocks):
        cut = [
            lax.dynamic_slice(block, (0, seq * unit, 0), (count, unit, width)) for block in blocks
        ]
        return swap_pairs(jnp.stack(cut), "seq")

    def core(block):
        return swap_pairs(block, "rep")

    def around(up, down):
        return ring_step(up, True), ring_step(down, False)

    up1, down1 = yield around(mine, mine)
    up2, down2, x1, *core1 = yield (
        *around(up1, down1), cross(up1, down1), core(up1), core(down1)
    )
    up3, down3, x2, *core2 = yield (
        *around(up2, down2), cross(up2, down2), core(up2), core(down2), core(x1)
    )
    up4, down4, x3, *core3 = yield (
        *around(up3[:, :unit], down3[:, unit:]), cross(up3, down3), core(up3), core(down3), core(x2)
    )
    far = jnp.concatenate([up4, down4], axis=1)
    x4, *core4 = yield (cross(far), core(far), core(x3))
    (core_x4,) = yield (core(x4),)
    parts = [up1, down1, up2, down2, up3, down3, far, x1, x2, x3, x4]
    parts += core1 + core2[:2] + core3[:2] + core4[:1]
    parts += [core2[2], core3[2], core4[1], core_x4]
    where = jnp.concatenate([ring_ids(), jnp.stack([rep, seq]).astype(jnp.int32)])
    anywhere = pl.BlockSpec(memory_space=pl.ANY)
    return pl.pallas_call(
        place_kernel,
        out_shape=jax.ShapeDtypeStruct((shards, count, rows, width), piece.dtype),
        in_specs=[pl.BlockSpec(memory_space=pltpu.SMEM)] + [anywhere] * 23,
        out_specs=pl.BlockSpec(memory_space=pltpu.VMEM),
        compiler_params=pltpu.CompilerParams(vmem_limit_bytes=32 * 2**20),
        scratch_shapes=[pltpu.SemaphoreType.DMA],
        cost_estimate=pl.CostEstimate(
            flops=0, transcendentals=0, bytes_accessed=2 * shards * piece.size * 2
        ),
    )(where, piece, *parts)


def gather_wide(piece):
    count, rows, width = piece.shape
    copies = lax.axis_size("rep") * lax.axis_size("seq")
    at = lax.axis_index("rep") * lax.axis_size("seq") + lax.axis_index("seq")
    own = lax.dynamic_slice(piece, (at * (count // copies), 0, 0), (count // copies, rows, width))
    whole_piece = lax.all_gather(
        own.reshape(-1, width), ("shard", "rep", "seq"), axis=0, tiled=True
    )
    return whole_piece.reshape(-1, count, rows, width)


def gather_plain(piece, stacked):
    first, parts = stacked
    width = piece.shape[2]
    whole_piece = lax.all_gather(piece, "shard", axis=0, tiled=False)
    flat = whole_piece.transpose(1, 0, 2, 3).reshape(-1, width, width)
    if parts:
        tall = whole_piece[:, first : first + parts].reshape(parts, width, width)
        flat = jnp.concatenate([flat[:first], tall, flat[first + parts :]])
    return flat[None]


def ring_fits(rows):
    return (
        lax.axis_size("shard") == 8
        and lax.axis_size("rep") == 2
        and lax.axis_size("seq") == 2
        and rows % 96 == 0
    )


def add(left, right):
    return (left.astype(F32) + right.astype(F32)).astype(BF16)


def scatter_ring(grads):
    shards, _, rows, width = grads[0].shape
    count = sum(part.shape[1] for part in grads)
    unit = rows // 6
    rep, seq = lax.axis_index("rep"), lax.axis_index("seq")
    ids = ring_ids()

    def half(which):
        cut = [
            lax.dynamic_slice(
                part, (0, 0, 3 * unit * which, 0), (shards, part.shape[1], 3 * unit, width)
            )
            for part in grads
        ]
        return jnp.concatenate(cut, axis=1)

    (got,) = yield (swap_pairs(half(1 - rep), "rep"),)
    paired = add(half(rep), got)

    def block(offset):
        return lax.dynamic_index_in_dim(paired, ids[offset % 8], 0, keepdims=False)

    def send(offsets):
        sent = [
            lax.dynamic_slice(block(offset), (0, 2 * (1 - seq) * unit, 0), (count, unit, width))
            for offset in offsets
        ]
        return swap_pairs(jnp.stack(sent), "seq")

    def join(offset, got):
        kept = lax.dynamic_slice(block(offset), (0, seq * unit, 0), (count, 2 * unit, width))
        zero = jnp.zeros_like(got)
        beside = jnp.where(
            seq == 0,
            jnp.concatenate([got, zero], axis=1),
            jnp.concatenate([zero, got], axis=1),
        )
        return add(kept, beside)

    far, near3 = yield (send((4,)), send((3, -3)))
    far = join(4, far[0])
    up, down, near2 = yield (
        ring_step(far[:, :unit], True),
        ring_step(far[:, unit:], False),
        send((2, -2)),
    )
    up3, down3 = join(3, near3[0]), join(-3, near3[1])
    up = jnp.concatenate([add(up3[:, :unit], up), up3[:, unit:]], axis=1)
    down = jnp.concatenate([down3[:, :unit], add(down3[:, unit:], down)], axis=1)
    up, down, near1 = yield (ring_step(up, True), ring_step(down, False), send((1, -1)))
    up, down, here = yield (
        ring_step(add(join(2, near2[0]), up), True),
        ring_step(add(join(-2, near2[1]), down), False),
        send((0,)),
    )
    up, down = yield (
        ring_step(add(join(1, near1[0]), up), True),
        ring_step(add(join(-1, near1[1]), down), False),
    )
    total = add(join(0, here[0]).astype(F32) + up.astype(F32), down)
    (other,) = yield (swap_pairs(total, "seq"),)
    left, right = jnp.where(seq == 0, total, other), jnp.where(seq == 0, other, total)
    mine = jnp.concatenate(
        [left[:, :unit], add(left[:, unit:], right[:, :unit]), right[:, unit:]], axis=1
    )
    (other,) = yield (swap_pairs(mine, "rep"),)
    return jnp.where(
        rep == 0,
        jnp.concatenate([mine, other], axis=1),
        jnp.concatenate([other, mine], axis=1),
    ).astype(F32)


class Moves:
    def __init__(self, queue=()):
        self.queue = list(queue)
        self.running = []
        self.done = {}
        if self.queue:
            self.pull()

    def pull(self):
        (key, piece, stacked) = self.queue.pop(0)
        if not ring_fits(piece.shape[1]):
            self.done[key] = gather_plain(piece, stacked)
            return
        if self.running:
            piece, moving = lax.optimization_barrier(
                (piece, [moving for _, _, moving, _ in self.running])
            )
            self.running = [
                (*move[:2], got, move[3]) for move, got in zip(self.running, moving)
            ]
        stages = gather_ring(piece)
        self.running.append((key, stages, next(stages), 1))

    def start(self, key, grads):
        stages = scatter_ring(grads)
        self.running.append((key, stages, next(stages), 9))

    def tick(self, value=None):
        waiting = [moving for _, _, moving, _ in self.running]
        if value is not None and waiting:
            value, waiting = lax.optimization_barrier((value, waiting))
        still = []
        for (key, stages, _, count), moving in zip(self.running, waiting):
            try:
                still.append((key, stages, stages.send(moving), count + 1))
            except StopIteration as end:
                self.done[key] = end.value
        self.running = still
        if self.queue and all(count > 4 for _, _, _, count in still):
            self.pull()
        return value

    def need(self, key):
        while key not in self.done:
            self.tick()
        return self.done[key]

    def finish(self):
        while self.running or self.queue:
            self.tick()
        return self.done


def scatter_wide(grads):
    return lax.psum_scatter(
        grads.reshape(-1, grads.shape[-1]),
        ("shard", "rep", "seq"),
        scatter_dimension=0,
        tiled=True,
    )


def scatter_plain(grads):
    owned = lax.psum_scatter(grads.astype(F32), "shard", scatter_dimension=0, tiled=False)
    return lax.psum(owned.astype(BF16), ("rep", "seq")).astype(F32)


def normalize(values):
    centered = values - jnp.mean(values, axis=-1, keepdims=True)
    scale = lax.rsqrt(jnp.mean(centered * centered, axis=-1, keepdims=True) + EPSILON)
    return centered * scale, scale


def norm_back(grad, normal, scale, factor):
    u = grad * (1.0 + factor)
    return (
        u
        - jnp.mean(u, axis=-1, keepdims=True)
        - normal * jnp.mean(u * normal, axis=-1, keepdims=True)
    ) * scale


def time_embed(steps, width):
    half_width = width // 2
    freqs = jnp.exp(-math.log(10000.0) * jnp.arange(half_width, dtype=F32) / half_width)
    angles = steps.astype(F32)[:, None] * freqs[None, :]
    return jnp.concatenate([jnp.cos(angles), jnp.sin(angles)], axis=-1)


def dot(left, right, left_dims, right_dims):
    return lax.dot_general(
        left, right, ((left_dims, right_dims), ((), ())), preferred_element_type=F32
    )


def nt(left, right, **kw):
    return lax.dot_general(left, right, (((1,), (1,)), ((), ())), preferred_element_type=F32, **kw)


def tn(left, right):
    return lax.dot_general(left, right, (((0,), (0,)), ((), ())), preferred_element_type=F32)


def nn(left, right):
    return lax.dot_general(left, right, (((1,), (0,)), ((), ())), preferred_element_type=F32)


def head_mask(values, head, size):
    lanes = lax.broadcasted_iota(jnp.int32, values.shape, 1)
    inside = (lanes >= head * size) & (lanes < (head + 1) * size)
    return jnp.where(inside, values, jnp.zeros_like(values))


def attend_kernel(size, q_ref, own_ref, other_ref, mixed_ref, log_ref):
    pair = q_ref.shape[1] // size
    queries = q_ref[...] * jnp.asarray(size**-0.5, BF16)
    blocks = []
    for head in range(pair):
        query = head_mask(queries, head, size)
        scores = [nt(own_ref[0], query), nt(other_ref[0], query)]
        top = jnp.maximum(*[jnp.max(part, axis=0, keepdims=True) for part in scores])
        expo = [jnp.exp(part - top) for part in scores]
        totals = sum(jnp.sum(part, axis=0, keepdims=True) for part in expo)
        mixed = tn(own_ref[1], expo[0].astype(BF16)) + tn(other_ref[1], expo[1].astype(BF16))
        blocks.append(mixed[head * size : (head + 1) * size] / totals)
        log_ref[0, head : head + 1, :] = top + jnp.log(totals)
    mixed_ref[...] = jnp.transpose(jnp.concatenate(blocks, axis=0)).astype(BF16)


def attend(queries, own_kv, other_kv):
    tokens, width = queries.shape
    pair = 128 // (width // HEADS)
    groups = HEADS // pair
    kv_spec = pl.BlockSpec((2, tokens, 128), lambda group: (0, 0, group))
    token_spec = pl.BlockSpec((tokens, 128), lambda group: (0, group))
    flops = 8 * tokens * tokens * width
    return pl.pallas_call(
        functools.partial(attend_kernel, width // HEADS),
        grid=(groups,),
        in_specs=[token_spec, kv_spec, kv_spec],
        out_specs=(token_spec, pl.BlockSpec((1, pair, tokens), lambda group: (group, 0, 0))),
        out_shape=(
            jax.ShapeDtypeStruct((tokens, width), BF16),
            jax.ShapeDtypeStruct((groups, pair, tokens), F32),
        ),
        compiler_params=pltpu.CompilerParams(vmem_limit_bytes=40 * 2**20),
        cost_estimate=pl.CostEstimate(
            flops=4 * flops, transcendentals=2 * HEADS * tokens**2, bytes_accessed=12 * queries.size
        ),
    )(queries, own_kv, other_kv)


def attend_back_kernel(
    size, q_ref, own_ref, other_ref, grad_ref, mixed_ref, log_ref, dq_ref, down_ref, dother_ref
):
    pair = q_ref.shape[1] // size
    scale = jnp.asarray(size**-0.5, BF16)
    queries = q_ref[...] * scale
    product = grad_ref[...].astype(F32) * mixed_ref[...].astype(F32)
    ones = jnp.ones((8, product.shape[1]), F32)
    grad_queries = []
    grad_kv = {}
    for head in range(pair):
        query, grad = head_mask(queries, head, size), head_mask(grad_ref[...], head, size)
        delta = nt(ones, head_mask(product, head, size), precision=lax.Precision.HIGHEST)[0:1]
        log_total = log_ref[0, head : head + 1, :]
        grad_query = None
        for side, kv_ref in enumerate((own_ref, other_ref)):
            probs = jnp.exp(nt(kv_ref[0], query) - log_total)
            grad_scores = (probs * (nt(kv_ref[1], grad) - delta)).astype(BF16)
            parts = (nn(grad_scores, query), nn(probs.astype(BF16), grad))
            before = grad_kv.get(side)
            grad_kv[side] = parts if before is None else tuple(a + b for a, b in zip(before, parts))
            part = tn(kv_ref[0], grad_scores)[head * size : (head + 1) * size]
            grad_query = part if grad_query is None else grad_query + part
        grad_queries.append(grad_query)
    total = jnp.transpose(jnp.concatenate(grad_queries, axis=0)) * (size**-0.5)
    dq_ref[...] = total.astype(BF16)
    for side, out_ref in enumerate((down_ref, dother_ref)):
        for at in range(2):
            out_ref[at] = grad_kv[side][at].astype(out_ref.dtype)


def attend_back(queries, own_kv, other_kv, grad_mixed, mixed, log_total):
    tokens, width = queries.shape
    pair = 128 // (width // HEADS)
    groups = HEADS // pair
    kv_spec = pl.BlockSpec((2, tokens, 128), lambda group: (0, 0, group))
    token_spec = pl.BlockSpec((tokens, 128), lambda group: (0, group))
    flops = 20 * tokens * tokens * width
    return pl.pallas_call(
        functools.partial(attend_back_kernel, width // HEADS),
        grid=(groups,),
        in_specs=[
            token_spec,
            kv_spec,
            kv_spec,
            token_spec,
            token_spec,
            pl.BlockSpec((1, pair, tokens), lambda group: (group, 0, 0)),
        ],
        out_specs=(token_spec, kv_spec, kv_spec),
        out_shape=(
            jax.ShapeDtypeStruct((tokens, width), BF16),
            jax.ShapeDtypeStruct(own_kv.shape, F32),
            jax.ShapeDtypeStruct(own_kv.shape, BF16),
        ),
        compiler_params=pltpu.CompilerParams(vmem_limit_bytes=40 * 2**20),
        cost_estimate=pl.CostEstimate(
            flops=4 * flops, transcendentals=2 * HEADS * tokens**2, bytes_accessed=24 * queries.size
        ),
    )(queries, own_kv, other_kv, grad_mixed, mixed, log_total)


def params_of(megabytes=48):
    return pltpu.CompilerParams(vmem_limit_bytes=megabytes * 2**20)


def whole(shape):
    return pl.BlockSpec(shape, lambda *at: (0,) * len(shape))


def column_sum(values):
    return jnp.sum(values, axis=0, keepdims=True)


def matrix_at(array, at, moving=True):
    shards, _, rows, width = array.shape
    return pl.BlockSpec(
        (shards, 1, rows, width), lambda part: (0, at + part if moving else at, 0, 0)
    )


def tall_at(array, at, parts):
    shards, _, rows, width = array.shape
    if shards == 1:
        return matrix_at(array, at)
    return pl.BlockSpec((shards // parts, parts, rows, width), lambda part: (part, at // parts, 0, 0))


def square(ref):
    return ref[...].reshape(ref.shape[-1], ref.shape[-1])


def put_square(ref, value):
    ref[...] = value.astype(ref.dtype).reshape(ref.shape)


def project_kernel(stream_ref, mod_ref, weight_ref, bias_ref, normed_ref, q_ref, kv_ref):
    part = pl.program_id(0)

    @pl.when(part == 0)
    def _():
        normal, _ = normalize(stream_ref[...])
        normed_ref[...] = (normal * (1.0 + mod_ref[1:2]) + mod_ref[0:1]).astype(BF16)

    result = (nn(normed_ref[...], square(weight_ref)) + bias_ref[0]).astype(BF16)

    @pl.when(part == 0)
    def _():
        q_ref[...] = result

    @pl.when(part > 0)
    def _():
        kv_ref[0] = result


def project(stream, modulation, weights, at, bias):
    tokens, width = stream.shape
    return pl.pallas_call(
        project_kernel,
        grid=(3,),
        in_specs=[
            whole((tokens, width)),
            whole((6, width)),
            matrix_at(weights, at),
            pl.BlockSpec((1, 1, width), lambda part: (part, 0, 0)),
        ],
        out_specs=(
            whole((tokens, width)),
            whole((tokens, width)),
            pl.BlockSpec((1, tokens, width), lambda part: (jnp.maximum(part - 1, 0), 0, 0)),
        ),
        out_shape=(
            jax.ShapeDtypeStruct((tokens, width), BF16),
            jax.ShapeDtypeStruct((tokens, width), BF16),
            jax.ShapeDtypeStruct((2, tokens, width), BF16),
        ),
        compiler_params=params_of(),
        cost_estimate=pl.CostEstimate(
            flops=6 * tokens * width**2, transcendentals=0, bytes_accessed=12 * tokens * width
        ),
    )(stream, modulation, weights, bias)


GELU_SCALE = math.sqrt(2.0 / math.pi)


def gelu_parts(value):
    square = value * value
    tanh = jnp.tanh(GELU_SCALE * value * (1.0 + 0.044715 * square))
    return square, tanh


def mlp_kernel(
    mixed_ref, stream_ref, mod_ref, proj_ref, proj_b_ref, fc1_ref, fc1_b_ref, fc2_ref, fc2_b_ref,
    attn_ref, middle_ref, normed_ref, hidden_ref, active_ref, mlp_ref, result_ref,
):
    part = pl.program_id(0)

    @pl.when(part == 0)
    def _():
        attn_out = nn(mixed_ref[...], square(proj_ref)) + proj_b_ref[...]
        attn_ref[...] = attn_out
        middle = stream_ref[...] + mod_ref[2:3] * attn_out
        middle_ref[...] = middle
        normal, _ = normalize(middle)
        normed_ref[...] = (normal * (1.0 + mod_ref[4:5]) + mod_ref[3:4]).astype(BF16)

    hidden = nn(normed_ref[...], square(fc1_ref)) + fc1_b_ref[0]
    hidden_ref[0] = hidden
    _, tanh = gelu_parts(hidden)
    active = (0.5 * hidden * (1.0 + tanh)).astype(BF16)
    active_ref[0] = active
    product = nn(active, square(fc2_ref))

    @pl.when(part == 0)
    def _():
        mlp_ref[...] = product + fc2_b_ref[...]

    @pl.when(part > 0)
    def _():
        mlp_ref[...] += product

    @pl.when(part == pl.num_programs(0) - 1)
    def _():
        result_ref[...] = middle_ref[...] + mod_ref[5:6] * mlp_ref[...]


def mlp(mixed, stream, modulation, weights, proj_b, fc1_b, fc2_b):
    tokens, width = stream.shape
    parts = fc1_b.shape[0]
    token, row = whole((tokens, width)), whole((1, width))
    by_part = lambda rows: pl.BlockSpec((1, rows, width), lambda part: (part, 0, 0))
    shape = lambda *dims: jax.ShapeDtypeStruct(dims[:-1], dims[-1])
    return pl.pallas_call(
        mlp_kernel,
        grid=(parts,),
        in_specs=[
            token, token, whole((6, width)), matrix_at(weights, 2 * parts, False), row,
            matrix_at(weights, 0), by_part(1), tall_at(weights, parts, parts), row,
        ],
        out_specs=(token, token, token, by_part(tokens), by_part(tokens), token, token),
        out_shape=(
            shape(tokens, width, F32),
            shape(tokens, width, F32),
            shape(tokens, width, BF16),
            shape(parts, tokens, width, F32),
            shape(parts, tokens, width, BF16),
            shape(tokens, width, F32),
            shape(tokens, width, F32),
        ),
        compiler_params=params_of(),
        cost_estimate=pl.CostEstimate(
            flops=(2 + 4 * parts) * tokens * width**2,
            transcendentals=parts * tokens * width,
            bytes_accessed=(20 + 6 * parts) * tokens * width,
        ),
    )(mixed, stream, modulation, weights, proj_b, weights, fc1_b, weights, fc2_b)


def mlp_back_kernel(
    grad_ref, mlp_ref, mod_ref, fc2_ref, fc1_ref, hidden_ref, active_ref, normed_ref, middle_ref,
    attn_ref, mixed_ref, proj_ref,
    fc2_g_ref, fc1_g_ref, proj_g_ref, fc1_b_ref, sums_ref, grad_middle_ref, grad_mixed_ref,
    low_ref, total_ref,
):
    part = pl.program_id(0)

    @pl.when(part == 0)
    def _():
        grad = grad_ref[...]
        sums_ref[2:3] = column_sum(grad * mlp_ref[...])
        low = (grad * mod_ref[5:6]).astype(BF16)
        low_ref[...] = low
        sums_ref[4:5] = column_sum(low.astype(F32))

    low = low_ref[...]
    put_square(fc2_g_ref, tn(active_ref[0], low))
    hidden = hidden_ref[0]
    squared, tanh = gelu_parts(hidden)
    slope = 0.5 * (1.0 + tanh) + (0.5 * GELU_SCALE) * hidden * (1.0 - tanh * tanh) * (
        1.0 + (3 * 0.044715) * squared
    )
    grad_hidden = (nt(low, square(fc2_ref)) * slope).astype(BF16)
    fc1_b_ref[0] = column_sum(grad_hidden.astype(F32))
    put_square(fc1_g_ref, tn(normed_ref[...], grad_hidden))
    product = nt(grad_hidden, square(fc1_ref))

    @pl.when(part == 0)
    def _():
        total_ref[...] = product

    @pl.when(part > 0)
    def _():
        total_ref[...] += product

    @pl.when(part == pl.num_programs(0) - 1)
    def _():
        grad_normed = total_ref[...]
        normal, scale = normalize(middle_ref[...])
        sums_ref[0:1] = column_sum(grad_normed)
        sums_ref[1:2] = column_sum(grad_normed * normal)
        grad_middle = grad_ref[...] + norm_back(grad_normed, normal, scale, mod_ref[4:5])
        grad_middle_ref[...] = grad_middle
        sums_ref[3:4] = column_sum(grad_middle * attn_ref[...])
        grad_attn = (grad_middle * mod_ref[2:3]).astype(BF16)
        sums_ref[5:6] = column_sum(grad_attn.astype(F32))
        put_square(proj_g_ref, tn(mixed_ref[...], grad_attn))
        grad_mixed_ref[...] = nt(grad_attn, square(proj_ref)).astype(BF16)


def mlp_back(grad, mlp_out, modulation, weights, hidden, active, normed, middle, attn_out, mixed):
    tokens, width = grad.shape
    parts = hidden.shape[0]
    token = whole((tokens, width))
    form = (weights.shape[0], parts) + weights.shape[2:]
    fc_form, proj_form = jax.ShapeDtypeStruct(form, BF16), jax.ShapeDtypeStruct(
        (form[0], 1) + form[2:], BF16
    )
    by_part = lambda rows: pl.BlockSpec((1, rows, width), lambda part: (part, 0, 0))
    shape = lambda *dims: jax.ShapeDtypeStruct(dims[:-1], dims[-1])
    return pl.pallas_call(
        mlp_back_kernel,
        grid=(parts,),
        in_specs=[
            token, token, whole((6, width)), tall_at(weights, parts, parts), matrix_at(weights, 0),
            by_part(tokens), by_part(tokens), token, token, token, token,
            matrix_at(weights, 2 * parts, False),
        ],
        out_specs=(
            tall_at(fc_form, 0, parts), matrix_at(fc_form, 0), matrix_at(proj_form, 0, False),
            by_part(1), whole((6, width)), token, token,
        ),
        out_shape=(
            fc_form,
            fc_form,
            proj_form,
            shape(parts, 1, width, F32),
            shape(6, width, F32),
            shape(tokens, width, F32),
            shape(tokens, width, BF16),
        ),
        scratch_shapes=[pltpu.VMEM((tokens, width), BF16), pltpu.VMEM((tokens, width), F32)],
        compiler_params=params_of(56),
        cost_estimate=pl.CostEstimate(
            flops=(4 + 8 * parts) * tokens * width**2,
            transcendentals=parts * tokens * width,
            bytes_accessed=(20 + 6 * parts) * tokens * width + 8 * parts * width**2,
        ),
    )(
        grad, mlp_out, modulation, weights, weights, hidden, active, normed, middle, attn_out,
        mixed, weights,
    )


def project_back_kernel(
    gq_ref, own_ref, back_ref, normed_ref, weight_ref, stream_ref, mod_ref, middle_ref,
    weight_g_ref, sums_ref, bias_ref, grad_ref, total_ref,
):
    part = pl.program_id(0)

    def step(grad, first):
        put_square(weight_g_ref, tn(normed_ref[...], grad))
        bias_ref[0] = column_sum(grad.astype(F32))
        product = nt(grad, square(weight_ref))
        total_ref[...] = product if first else total_ref[...] + product

    @pl.when(part == 0)
    def _():
        step(gq_ref[...], True)

    @pl.when(part > 0)
    def _():
        step((own_ref[0] + back_ref[0].astype(F32)).astype(BF16), False)

    @pl.when(part == 2)
    def _():
        grad_normed = total_ref[...]
        normal, scale = normalize(stream_ref[...])
        sums_ref[0:1] = column_sum(grad_normed)
        sums_ref[1:2] = column_sum(grad_normed * normal)
        grad_ref[...] = middle_ref[...] + norm_back(grad_normed, normal, scale, mod_ref[1:2])


def project_back(grad_q, grad_own, returned, normed, weights, at, stream, modulation, grad_middle):
    tokens, width = stream.shape
    token = whole((tokens, width))
    form = jax.ShapeDtypeStruct((weights.shape[0], 3) + weights.shape[2:], BF16)
    kv = pl.BlockSpec((1, tokens, width), lambda part: (jnp.maximum(part - 1, 0), 0, 0))
    return pl.pallas_call(
        project_back_kernel,
        grid=(3,),
        in_specs=[
            token, kv, kv, token, matrix_at(weights, at), token, whole((6, width)), token,
        ],
        out_specs=(
            matrix_at(form, 0),
            whole((2, width)),
            pl.BlockSpec((1, 1, width), lambda part: (part, 0, 0)),
            token,
        ),
        out_shape=(
            form,
            jax.ShapeDtypeStruct((2, width), F32),
            jax.ShapeDtypeStruct((3, 1, width), F32),
            jax.ShapeDtypeStruct((tokens, width), F32),
        ),
        scratch_shapes=[pltpu.VMEM((tokens, width), F32)],
        compiler_params=params_of(),
        cost_estimate=pl.CostEstimate(
            flops=12 * tokens * width**2,
            transcendentals=0,
            bytes_accessed=24 * tokens * width + 12 * width**2,
        ),
    )(grad_q, grad_own, returned, normed, weights, stream, modulation, grad_middle)


def layer_forward(stream, modulation, biases, moves, weights_of):
    qkv_b, proj_b, fc1_b, fc2_b = biases
    qkv_w, at = weights_of("qkv")
    normed, queries, own_kv = project(stream, modulation, qkv_w, at, qkv_b)
    own_kv = moves.tick(own_kv)
    other_kv = swap_pairs(own_kv, "rep")
    mixed, log_total = attend(queries, own_kv, other_kv)
    mixed = moves.tick(mixed)
    rest_w, _ = weights_of("rest")
    attn_out, middle, normed_mlp, hidden, active, mlp_out, result = mlp(
        mixed, stream, modulation, rest_w, proj_b, fc1_b, fc2_b
    )
    result = moves.tick(result)
    return result, (
        stream, normed, queries, own_kv, other_kv, mixed, log_total, attn_out, middle, normed_mlp,
        hidden, active, mlp_out, qkv_w, at, rest_w,
    )


def layer_backward(grad_out, modulation, kept, shards, moves, send_rest, send_qkv):
    (
        stream, normed, queries, own_kv, other_kv, mixed, log_total, attn_out, middle, normed_mlp,
        hidden, active, mlp_out, qkv_w, at, rest_w,
    ) = kept
    width = stream.shape[-1]
    fc2_g, fc1_g, proj_g, fc1_b, sums, grad_middle, grad_mixed = mlp_back(
        grad_out, mlp_out, modulation, rest_w, hidden, active, normed_mlp, middle, attn_out, mixed
    )
    grad_mixed = moves.tick(grad_mixed)
    send_rest(fc1_g, fc2_g, proj_g)
    grad_q, grad_own, grad_other = attend_back(
        queries, own_kv, other_kv, grad_mixed, mixed, log_total
    )
    grad_other = moves.tick(grad_other)
    returned = swap_pairs(grad_other, "rep")
    qkv_g, attn_sums, qkv_b, grad_stream = project_back(
        grad_q, grad_own, returned, normed, qkv_w, at, stream, modulation, grad_middle
    )
    grad_stream = moves.tick(grad_stream)
    send_qkv(qkv_g, proj_g)
    grad_modulation = jnp.concatenate(
        [attn_sums[0], attn_sums[1], sums[3], sums[0], sums[1], sums[2]]
    )
    query_value = jnp.concatenate([qkv_b[0, 0], qkv_b[2, 0]])
    bias_grads = [
        part.reshape(shards, -1) for part in (query_value, sums[5], fc1_b.reshape(-1), sums[4])
    ]
    return grad_stream, grad_modulation, jnp.concatenate(bias_grads, axis=1)


def columns(matrix, width):
    return jnp.stack(jnp.split(matrix, matrix.shape[1] // width, axis=1))


def uncolumns(blocks):
    return jnp.concatenate(list(blocks), axis=1)


def shards_program(
    latents,
    image_loads,
    timesteps,
    classes,
    label_table,
    ada_weight,
    ada_bias,
    qkv_weight,
    qv_bias,
    proj_weight,
    proj_bias,
    fc1_weight,
    fc1_bias,
    fc2_weight,
    fc2_bias,
    cotangent,
):
    shards = lax.axis_size("shard")
    width = latents.shape[2]
    own_rows = width // shards
    ff_parts = fc1_weight.shape[2] // width
    shard, rep, seq = lax.axis_index("shard"), lax.axis_index("rep"), lax.axis_index("seq")

    one_hot = (
        classes[:, None] == jnp.arange(label_table.shape[0], dtype=jnp.int32)[None, :]
    ).astype(BF16)
    cond = dot(one_hot, label_table, (1,), (0,)) + time_embed(timesteps, width)
    cond_low = jax.nn.silu(cond).astype(BF16)
    live_own = (image_loads > 0).astype(BF16)
    shared = cube_gather(
        jnp.concatenate([cond_low[0], jnp.broadcast_to(live_own, (128,))]), ("rep", "shard")
    )
    live = lax.dynamic_slice(shared, (seq * shards + shard, width), (1, 1)).astype(F32)
    cond_rows = lax.dynamic_slice(
        shared[:, :width], (0, shard * own_rows), (shared.shape[0], own_rows)
    )
    stream = swap_layout(latents[0]).astype(F32)

    rings = ring_fits(own_rows)
    packs = []
    for layer in range(LAYERS):
        fc2_piece = fc2_weight[layer].reshape(ff_parts, own_rows, width)
        packs.append(
            (
                jnp.concatenate(
                    [columns(fc1_weight[layer], width), fc2_piece, proj_weight[layer][None]]
                ),
                columns(qkv_weight[layer], width),
            )
        )
    tall = (ff_parts, ff_parts)
    moves = Moves([("qkv", packs[0][1], (0, 0)), ("rest", packs[0][0], tall)])
    later = jnp.concatenate(packs[1])
    later = gather_wide(later) if rings else gather_plain(later, tall)

    def first_weights(name):
        return moves.need(name), 0

    def later_weights(name):
        return later, 2 * ff_parts + 1

    small = jnp.concatenate([ada_bias, qv_bias, proj_bias, fc1_bias, fc2_bias], axis=1)
    small = cube_gather(small, ("shard",)).astype(F32)
    ends = [0]
    for bias in (ada_bias, qv_bias, proj_bias, fc1_bias, fc2_bias):
        ends.append(ends[-1] + bias.shape[1])
    biases, ada_b = [], []
    for layer in range(LAYERS):
        full = [small[:, layer, ends[at] : ends[at + 1]].reshape(-1) for at in range(5)]
        ada_b.append(full[0])
        qkv_b = jnp.concatenate([full[1][:width], jnp.zeros((width,), F32), full[1][width:]])
        biases.append(
            (
                qkv_b.reshape(3, 1, width),
                full[2][None],
                full[3].reshape(ff_parts, 1, width),
                full[4][None],
            )
        )

    mine = lax.dynamic_slice(cond_rows, (seq * shards, 0), (shards, own_rows))
    partial = jnp.concatenate(
        [dot(mine, ada_weight[layer], (1,), (0,)) for layer in range(LAYERS)], axis=1
    )
    modulations = cube_scatter(partial, "shard")
    modulations = [
        (modulations.reshape(LAYERS, -1)[layer] + ada_b[layer]).reshape(6, width)
        for layer in range(LAYERS)
    ]

    kept = []
    for layer in range(LAYERS):
        stream, layer_kept = layer_forward(
            stream,
            modulations[layer],
            biases[layer],
            moves,
            later_weights if layer else first_weights,
        )
        kept.append(layer_kept)
    moves = Moves()
    activations = swap_layout((stream * live).astype(BF16)).astype(F32)
    grad_stream = swap_layout(cotangent[0]).astype(F32) * live

    shares = []
    done = {}

    def flat(part):
        return part.reshape(part.shape[1], shards, own_rows, width).transpose(1, 0, 2, 3)

    def send_rest(layer, fc1_g, fc2_g, proj_g):
        if not rings:
            done["rest", layer] = scatter_plain(
                jnp.concatenate(
                    [flat(fc1_g), fc2_g.reshape(shards, ff_parts, own_rows, width), flat(proj_g)],
                    axis=1,
                )
            )
        elif layer:
            shares.extend([scatter_wide(fc1_g), scatter_wide(fc2_g)])
        else:
            moves.start("rest", [fc1_g, fc2_g, proj_g])

    def send_qkv(layer, qkv_g, proj_g):
        if not rings:
            done["qkv", layer] = scatter_plain(flat(qkv_g))
        elif layer:
            shares.append(scatter_wide(jnp.concatenate([proj_g, qkv_g], axis=1)))
        else:
            moves.start("qkv", [qkv_g])

    bias_grads = [None] * LAYERS
    ada_w_grads = [None] * LAYERS
    ada_b_grads = [None] * LAYERS
    grad_cond = 0.0
    for layer in reversed(range(LAYERS)):
        grad_stream, grad_mod, bias_grads[layer] = layer_backward(
            grad_stream,
            modulations[layer],
            kept[layer],
            shards,
            moves,
            functools.partial(send_rest, layer),
            functools.partial(send_qkv, layer),
        )
        grad_mod = (grad_mod + swap_pairs(grad_mod, "rep")).astype(BF16)
        all_mod = cube_gather(grad_mod, ("seq", "shard"))
        ada_w_grads[layer] = dot(cond_rows, all_mod, (0,), (0,))
        own_mod = lax.dynamic_slice(
            all_mod, (0, shard * ada_bias.shape[1]), (all_mod.shape[0], ada_bias.shape[1])
        )
        ada_b_grads[layer] = jnp.sum(own_mod.astype(F32), axis=0)
        rep_mod = lax.dynamic_slice(all_mod, (rep * shards, 0), (shards, all_mod.shape[1]))
        grad_cond = grad_cond + dot(rep_mod, ada_weight[layer], (1,), (1,))

    latent_grad = swap_layout(grad_stream.astype(BF16)).astype(F32)
    all_cond = cube_gather(grad_cond, ("shard",))
    grad_cond_low = lax.dynamic_slice(all_cond, (0, shard, 0), (shards, 1, own_rows)).reshape(
        1, width
    )
    _, silu_pull = jax.vjp(jax.nn.silu, cond)
    cond_grad = silu_pull(grad_cond_low)[0]

    bias_total = cube_scatter(jnp.stack(bias_grads, axis=1), "shard")
    bias_total = bias_total + swap_pairs(bias_total, "rep")
    bias_total = bias_total + swap_pairs(bias_total, "seq")
    qv_b, proj_b, fc1_b, fc2_b = [
        bias_total[:, ends[at] - ends[1] : ends[at + 1] - ends[1]] for at in range(1, 5)
    ]
    if rings:
        moved = moves.finish()
        done["qkv", 0], done["rest", 0] = moved["qkv"], moved["rest"]
        spread = cube_gather(jnp.stack([share.reshape(own_rows, width) for share in shares]), ("rep", "seq"))
        spread = spread.astype(F32)
        done["qkv", 1] = spread[1:, 2]
        done["rest", 1] = jnp.concatenate([spread[:, 0], spread[:, 1], spread[:1, 2]])
    weight_grads = []
    for layer in range(LAYERS):
        qkv_grads, rest_grads = done["qkv", layer], done["rest", layer]
        weight_grads.append(
            (
                uncolumns(qkv_grads),
                rest_grads[2 * ff_parts],
                uncolumns(rest_grads[:ff_parts]),
                rest_grads[ff_parts : 2 * ff_parts].reshape(ff_parts * own_rows, width),
            )
        )
    qkv_g, proj_g, fc1_g, fc2_g = [
        jnp.stack([weight_grads[layer][at] for layer in range(LAYERS)]) for at in range(4)
    ]
    return (
        activations[None],
        latent_grad[None],
        cond_grad,
        jnp.stack(ada_w_grads),
        jnp.stack(ada_b_grads),
        qkv_g,
        qv_b,
        proj_g,
        proj_b,
        fc1_g,
        fc1_b,
        fc2_g,
        fc2_b,
    )


def solution(mesh):
    tokens = P(("rep", "shard"), "seq", None)
    images = P(("rep", "shard"))
    matrix = P(None, "shard", None)
    vector = P(None, "shard")
    return jax.shard_map(
        shards_program,
        mesh=mesh,
        in_specs=(tokens, images, images, images, P())
        + (matrix, vector) * 5
        + (tokens,),
        out_specs=(tokens, tokens, P(("rep", "shard"), None)) + (matrix, vector) * 5,
        check_vma=False,
    )
```

```python
import functools
import math

import jax
import jax.numpy as jnp
from jax import lax
from jax.experimental import pallas as pl
from jax.experimental.pallas import tpu as pltpu
from jax.sharding import PartitionSpec as P

HEADS = 12
LAYERS = 2
EPSILON = 1e-06
BF16 = jnp.bfloat16
F32 = jnp.float32


def swap_pairs(value, axis):
    return lax.ppermute(value, axis, [(0, 1), (1, 0)])


def swap_layout(value):
    moved = lax.ppermute(value, ("rep", "seq"), [(1, 2), (2, 1)])
    return jnp.where(lax.axis_index("rep") == lax.axis_index("seq"), value, moved)


def cube_pairs(value, axis, bit):
    return lax.ppermute(value, axis, [(at, at ^ bit) for at in range(lax.axis_size(axis))])


def cube_bits(axis):
    return [1 << place for place in range(lax.axis_size(axis).bit_length() - 1)]


def cube_gather(value, axes):
    value = value[None]
    for axis in reversed(axes):
        for bit in cube_bits(axis):
            other = cube_pairs(value, axis, bit)
            value = jnp.where(
                lax.axis_index(axis) & bit == 0,
                jnp.concatenate([value, other]),
                jnp.concatenate([other, value]),
            )
    return value


def cube_scatter(value, axis):
    for bit in reversed(cube_bits(axis)):
        low, high = value[:bit], value[bit:]
        first = lax.axis_index(axis) & bit == 0
        value = jnp.where(first, low, high) + cube_pairs(jnp.where(first, high, low), axis, bit)
    return value[0]


def ring_order(size):
    half = size // 2
    return [2 * place for place in range(half)] + [2 * place + 1 for place in reversed(range(half))]


def ring_step(value, forward):
    size = lax.axis_size("shard")
    order = ring_order(size)
    step = 1 if forward else size - 1
    return lax.ppermute(
        value, "shard", [(order[at], order[(at + step) % size]) for at in range(size)]
    )


def ring_ids():
    size = lax.axis_size("shard")
    order = ring_order(size)
    places = [order.index(shard) for shard in range(size)]
    place = jnp.array(places, jnp.int32)[lax.axis_index("shard")]
    return jnp.array(order, jnp.int32)[(place + jnp.arange(size, dtype=jnp.int32)) % size]


OFFSETS = (-1, 1, -2, 2, -3, 3, 4)


def place_kernel(where, *refs):
    (own, *rest) = refs[:23]
    out, sem = refs[23:]
    blocks, beside = rest[0:7], rest[7:11]
    core_blocks, core_beside = rest[11:18], rest[18:22]
    rep, seq = where[8], where[9]
    unit = own.shape[1] // 6

    def put(src, shard, row, rows):
        start = pl.multiple_of(row * unit, unit)
        copy = pltpu.make_async_copy(src, out.at[shard, :, pl.ds(start, rows), :], sem)
        copy.start()
        return [copy]

    copies = put(own, where[0], 0, 6 * unit)
    for slot, offset in enumerate(OFFSETS):
        shard = where[offset % 8]
        far = 3 * rep + 2 * (1 - seq)
        copies += put(blocks[slot], shard, 3 * rep + seq, 2 * unit)
        copies += put(beside[slot // 2].at[slot % 2], shard, far, unit)
        far = 3 * (1 - rep) + 2 * (1 - seq)
        copies += put(core_blocks[slot], shard, 3 * (1 - rep) + seq, 2 * unit)
        copies += put(core_beside[slot // 2].at[slot % 2], shard, far, unit)
    for copy in copies:
        copy.wait()


def gather_ring(piece):
    count, rows, width = piece.shape
    shards = lax.axis_size("shard")
    unit = rows // 6
    rep, seq = lax.axis_index("rep"), lax.axis_index("seq")
    mine = lax.dynamic_slice(piece, (0, (3 * rep + seq) * unit, 0), (count, 2 * unit, width))

    def cross(*blocks):
        cut = [
            lax.dynamic_slice(block, (0, seq * unit, 0), (count, unit, width)) for block in blocks
        ]
        return swap_pairs(jnp.stack(cut), "seq")

    def core(block):
        return swap_pairs(block, "rep")

    def around(up, down):
        return ring_step(up, True), ring_step(down, False)

    up1, down1 = yield around(mine, mine)
    up2, down2, x1, *core1 = yield (
        *around(up1, down1), cross(up1, down1), core(up1), core(down1)
    )
    up3, down3, x2, *core2 = yield (
        *around(up2, down2), cross(up2, down2), core(up2), core(down2), core(x1)
    )
    up4, down4, x3, *core3 = yield (
        *around(up3[:, :unit], down3[:, unit:]), cross(up3, down3), core(up3), core(down3), core(x2)
    )
    far = jnp.concatenate([up4, down4], axis=1)
    x4, *core4 = yield (cross(far), core(far), core(x3))
    (core_x4,) = yield (core(x4),)
    parts = [up1, down1, up2, down2, up3, down3, far, x1, x2, x3, x4]
    parts += core1 + core2[:2] + core3[:2] + core4[:1]
    parts += [core2[2], core3[2], core4[1], core_x4]
    where = jnp.concatenate([ring_ids(), jnp.stack([rep, seq]).astype(jnp.int32)])
    anywhere = pl.BlockSpec(memory_space=pl.ANY)
    return pl.pallas_call(
        place_kernel,
        out_shape=jax.ShapeDtypeStruct((shards, count, rows, width), piece.dtype),
        in_specs=[pl.BlockSpec(memory_space=pltpu.SMEM)] + [anywhere] * 23,
        out_specs=pl.BlockSpec(memory_space=pltpu.VMEM),
        compiler_params=pltpu.CompilerParams(vmem_limit_bytes=32 * 2**20),
        scratch_shapes=[pltpu.SemaphoreType.DMA],
        cost_estimate=pl.CostEstimate(
            flops=0, transcendentals=0, bytes_accessed=2 * shards * piece.size * 2
        ),
    )(where, piece, *parts)


def gather_wide(piece, after=None):
    count, rows, width = piece.shape
    copies = lax.axis_size("rep") * lax.axis_size("seq")
    at = lax.axis_index("rep") * lax.axis_size("seq") + lax.axis_index("seq")
    own = lax.dynamic_slice(piece, (at * (count // copies), 0, 0), (count // copies, rows, width))
    if after is not None:
        own, after = lax.optimization_barrier((own, after))
    whole_piece = lax.all_gather(
        own.reshape(-1, width), ("shard", "rep", "seq"), axis=0, tiled=True
    )
    return whole_piece.reshape(-1, count, rows, width), after


def gather_plain(piece, stacked):
    first, parts = stacked
    width = piece.shape[2]
    whole_piece = lax.all_gather(piece, "shard", axis=0, tiled=False)
    flat = whole_piece.transpose(1, 0, 2, 3).reshape(-1, width, width)
    if parts:
        tall = whole_piece[:, first : first + parts].reshape(parts, width, width)
        flat = jnp.concatenate([flat[:first], tall, flat[first + parts :]])
    return flat[None]


def ring_fits(rows):
    return (
        lax.axis_size("shard") == 8
        and lax.axis_size("rep") == 2
        and lax.axis_size("seq") == 2
        and rows % 96 == 0
    )


def add(left, right):
    return (left.astype(F32) + right.astype(F32)).astype(BF16)


def scatter_ring(grads):
    shards, _, rows, width = grads[0].shape
    count = sum(part.shape[1] for part in grads)
    unit = rows // 6
    rep, seq = lax.axis_index("rep"), lax.axis_index("seq")
    ids = ring_ids()

    def half(which):
        cut = [
            lax.dynamic_slice(
                part, (0, 0, 3 * unit * which, 0), (shards, part.shape[1], 3 * unit, width)
            )
            for part in grads
        ]
        return jnp.concatenate(cut, axis=1)

    (got,) = yield (swap_pairs(half(1 - rep), "rep"),)
    paired = add(half(rep), got)

    def block(offset):
        return lax.dynamic_index_in_dim(paired, ids[offset % 8], 0, keepdims=False)

    def send(offsets):
        sent = [
            lax.dynamic_slice(block(offset), (0, 2 * (1 - seq) * unit, 0), (count, unit, width))
            for offset in offsets
        ]
        return swap_pairs(jnp.stack(sent), "seq")

    def join(offset, got):
        kept = lax.dynamic_slice(block(offset), (0, seq * unit, 0), (count, 2 * unit, width))
        zero = jnp.zeros_like(got)
        beside = jnp.where(
            seq == 0,
            jnp.concatenate([got, zero], axis=1),
            jnp.concatenate([zero, got], axis=1),
        )
        return add(kept, beside)

    far, near3 = yield (send((4,)), send((3, -3)))
    far = join(4, far[0])
    up, down, near2 = yield (
        ring_step(far[:, :unit], True),
        ring_step(far[:, unit:], False),
        send((2, -2)),
    )
    up3, down3 = join(3, near3[0]), join(-3, near3[1])
    up = jnp.concatenate([add(up3[:, :unit], up), up3[:, unit:]], axis=1)
    down = jnp.concatenate([down3[:, :unit], add(down3[:, unit:], down)], axis=1)
    up, down, near1 = yield (ring_step(up, True), ring_step(down, False), send((1, -1)))
    up, down, here = yield (
        ring_step(add(join(2, near2[0]), up), True),
        ring_step(add(join(-2, near2[1]), down), False),
        send((0,)),
    )
    up, down = yield (
        ring_step(add(join(1, near1[0]), up), True),
        ring_step(add(join(-1, near1[1]), down), False),
    )
    total = add(join(0, here[0]).astype(F32) + up.astype(F32), down)
    (other,) = yield (swap_pairs(total, "seq"),)
    left, right = jnp.where(seq == 0, total, other), jnp.where(seq == 0, other, total)
    mine = jnp.concatenate(
        [left[:, :unit], add(left[:, unit:], right[:, :unit]), right[:, unit:]], axis=1
    )
    (other,) = yield (swap_pairs(mine, "rep"),)
    return jnp.where(
        rep == 0,
        jnp.concatenate([mine, other], axis=1),
        jnp.concatenate([other, mine], axis=1),
    ).astype(F32)


class Moves:
    def __init__(self, queue=()):
        self.queue = list(queue)
        self.running = []
        self.done = {}
        if self.queue:
            self.pull()

    def pull(self):
        (key, piece, stacked) = self.queue.pop(0)
        if not ring_fits(piece.shape[1]):
            self.done[key] = gather_plain(piece, stacked)
            return
        if self.running:
            piece, moving = lax.optimization_barrier(
                (piece, [moving for _, _, moving, _ in self.running])
            )
            self.running = [
                (*move[:2], got, move[3]) for move, got in zip(self.running, moving)
            ]
        stages = gather_ring(piece)
        self.running.append((key, stages, next(stages), 1))

    def start(self, key, grads):
        stages = scatter_ring(grads)
        self.running.append((key, stages, next(stages), 9))

    def tick(self, value=None, only=None):
        waiting = [moving for _, _, moving, _ in self.running]
        if value is not None and waiting:
            value, waiting = lax.optimization_barrier((value, waiting))
        still = []
        for (key, stages, _, count), moving in zip(self.running, waiting):
            if only not in (None, key):
                still.append((key, stages, moving, count))
                continue
            try:
                still.append((key, stages, stages.send(moving), count + 1))
            except StopIteration as end:
                self.done[key] = end.value
        self.running = still
        if self.queue and all(count > 4 for _, _, _, count in still):
            self.pull()
        return value

    def need(self, key):
        while key not in self.done:
            self.tick(only=key if any(key == move[0] for move in self.running) else None)
        return self.done[key]

    def finish(self, lates):
        step = 0
        while self.running:
            step += 1
            value = self.tick(lates.get(step))
            if step in lates:
                lates[step] = value
        return self.done, lates


def scatter_wide(grads):
    return lax.psum_scatter(
        grads.reshape(-1, grads.shape[-1]),
        ("shard", "rep", "seq"),
        scatter_dimension=0,
        tiled=True,
    )


def scatter_plain(grads):
    owned = lax.psum_scatter(grads.astype(F32), "shard", scatter_dimension=0, tiled=False)
    return lax.psum(owned.astype(BF16), ("rep", "seq")).astype(F32)


def normalize(values):
    centered = values - jnp.mean(values, axis=-1, keepdims=True)
    scale = lax.rsqrt(jnp.mean(centered * centered, axis=-1, keepdims=True) + EPSILON)
    return centered * scale, scale


def norm_back(grad, normal, scale, factor):
    u = grad * (1.0 + factor)
    return (
        u
        - jnp.mean(u, axis=-1, keepdims=True)
        - normal * jnp.mean(u * normal, axis=-1, keepdims=True)
    ) * scale


def time_embed(steps, width):
    half_width = width // 2
    freqs = jnp.exp(-math.log(10000.0) * jnp.arange(half_width, dtype=F32) / half_width)
    angles = steps.astype(F32)[:, None] * freqs[None, :]
    return jnp.concatenate([jnp.cos(angles), jnp.sin(angles)], axis=-1)


def dot(left, right, left_dims, right_dims):
    return lax.dot_general(
        left, right, ((left_dims, right_dims), ((), ())), preferred_element_type=F32
    )


def nt(left, right, **kw):
    return lax.dot_general(left, right, (((1,), (1,)), ((), ())), preferred_element_type=F32, **kw)


def tn(left, right):
    return lax.dot_general(left, right, (((0,), (0,)), ((), ())), preferred_element_type=F32)


def nn(left, right):
    return lax.dot_general(left, right, (((1,), (0,)), ((), ())), preferred_element_type=F32)


def head_mask(values, head, size):
    lanes = lax.broadcasted_iota(jnp.int32, values.shape, 1)
    inside = (lanes >= head * size) & (lanes < (head + 1) * size)
    return jnp.where(inside, values, jnp.zeros_like(values))


def attend_kernel(size, q_ref, own_ref, other_ref, mixed_ref, log_ref):
    pair = q_ref.shape[1] // size
    queries = q_ref[...] * jnp.asarray(size**-0.5, BF16)
    blocks = []
    for head in range(pair):
        query = head_mask(queries, head, size)
        scores = [nt(own_ref[0], query), nt(other_ref[0], query)]
        top = jnp.maximum(*[jnp.max(part, axis=0, keepdims=True) for part in scores])
        expo = [jnp.exp(part - top) for part in scores]
        totals = sum(jnp.sum(part, axis=0, keepdims=True) for part in expo)
        mixed = tn(own_ref[1], expo[0].astype(BF16)) + tn(other_ref[1], expo[1].astype(BF16))
        blocks.append(mixed[head * size : (head + 1) * size] / totals)
        log_ref[0, head : head + 1, :] = top + jnp.log(totals)
    mixed_ref[...] = jnp.transpose(jnp.concatenate(blocks, axis=0)).astype(BF16)


def attend(queries, own_kv, other_kv):
    tokens, width = queries.shape
    pair = 128 // (width // HEADS)
    groups = HEADS // pair
    kv_spec = pl.BlockSpec((2, tokens, 128), lambda group: (0, 0, group))
    token_spec = pl.BlockSpec((tokens, 128), lambda group: (0, group))
    flops = 8 * tokens * tokens * width
    return pl.pallas_call(
        functools.partial(attend_kernel, width // HEADS),
        grid=(groups,),
        in_specs=[token_spec, kv_spec, kv_spec],
        out_specs=(token_spec, pl.BlockSpec((1, pair, tokens), lambda group: (group, 0, 0))),
        out_shape=(
            jax.ShapeDtypeStruct((tokens, width), BF16),
            jax.ShapeDtypeStruct((groups, pair, tokens), F32),
        ),
        compiler_params=pltpu.CompilerParams(vmem_limit_bytes=40 * 2**20),
        cost_estimate=pl.CostEstimate(
            flops=4 * flops, transcendentals=2 * HEADS * tokens**2, bytes_accessed=12 * queries.size
        ),
    )(queries, own_kv, other_kv)


def attend_back_kernel(
    size, q_ref, own_ref, other_ref, grad_ref, mixed_ref, log_ref, dq_ref, down_ref, dother_ref
):
    pair = q_ref.shape[1] // size
    scale = jnp.asarray(size**-0.5, BF16)
    queries = q_ref[...] * scale
    product = grad_ref[...].astype(F32) * mixed_ref[...].astype(F32)
    ones = jnp.ones((8, product.shape[1]), F32)
    grad_queries = []
    grad_kv = {}
    for head in range(pair):
        query, grad = head_mask(queries, head, size), head_mask(grad_ref[...], head, size)
        delta = nt(ones, head_mask(product, head, size), precision=lax.Precision.HIGHEST)[0:1]
        log_total = log_ref[0, head : head + 1, :]
        grad_query = None
        for side, kv_ref in enumerate((own_ref, other_ref)):
            probs = jnp.exp(nt(kv_ref[0], query) - log_total)
            grad_scores = (probs * (nt(kv_ref[1], grad) - delta)).astype(BF16)
            parts = (nn(grad_scores, query), nn(probs.astype(BF16), grad))
            before = grad_kv.get(side)
            grad_kv[side] = parts if before is None else tuple(a + b for a, b in zip(before, parts))
            part = tn(kv_ref[0], grad_scores)[head * size : (head + 1) * size]
            grad_query = part if grad_query is None else grad_query + part
        grad_queries.append(grad_query)
    total = jnp.transpose(jnp.concatenate(grad_queries, axis=0)) * (size**-0.5)
    dq_ref[...] = total.astype(BF16)
    for side, out_ref in enumerate((down_ref, dother_ref)):
        for at in range(2):
            out_ref[at] = grad_kv[side][at].astype(out_ref.dtype)


def attend_back(queries, own_kv, other_kv, grad_mixed, mixed, log_total):
    tokens, width = queries.shape
    pair = 128 // (width // HEADS)
    groups = HEADS // pair
    kv_spec = pl.BlockSpec((2, tokens, 128), lambda group: (0, 0, group))
    token_spec = pl.BlockSpec((tokens, 128), lambda group: (0, group))
    flops = 20 * tokens * tokens * width
    return pl.pallas_call(
        functools.partial(attend_back_kernel, width // HEADS),
        grid=(groups,),
        in_specs=[
            token_spec,
            kv_spec,
            kv_spec,
            token_spec,
            token_spec,
            pl.BlockSpec((1, pair, tokens), lambda group: (group, 0, 0)),
        ],
        out_specs=(token_spec, kv_spec, kv_spec),
        out_shape=(
            jax.ShapeDtypeStruct((tokens, width), BF16),
            jax.ShapeDtypeStruct(own_kv.shape, F32),
            jax.ShapeDtypeStruct(own_kv.shape, BF16),
        ),
        compiler_params=pltpu.CompilerParams(vmem_limit_bytes=40 * 2**20),
        cost_estimate=pl.CostEstimate(
            flops=4 * flops, transcendentals=2 * HEADS * tokens**2, bytes_accessed=24 * queries.size
        ),
    )(queries, own_kv, other_kv, grad_mixed, mixed, log_total)


def params_of(megabytes=48):
    return pltpu.CompilerParams(vmem_limit_bytes=megabytes * 2**20)


def whole(shape):
    return pl.BlockSpec(shape, lambda *at: (0,) * len(shape))


def column_sum(values):
    return jnp.sum(values, axis=0, keepdims=True)


def matrix_at(array, at, moving=True):
    shards, _, rows, width = array.shape
    return pl.BlockSpec(
        (shards, 1, rows, width), lambda part: (0, at + part if moving else at, 0, 0)
    )


def tall_at(array, at, parts):
    shards, _, rows, width = array.shape
    if shards == 1:
        return matrix_at(array, at)
    return pl.BlockSpec((shards // parts, parts, rows, width), lambda part: (part, at // parts, 0, 0))


def square(ref):
    return ref[...].reshape(ref.shape[-1], ref.shape[-1])


def put_square(ref, value):
    ref[...] = value.astype(ref.dtype).reshape(ref.shape)


def project_kernel(stream_ref, mod_ref, weight_ref, bias_ref, normed_ref, q_ref, kv_ref):
    part = pl.program_id(0)

    @pl.when(part == 0)
    def _():
        normal, _ = normalize(stream_ref[...])
        normed_ref[...] = (normal * (1.0 + mod_ref[1:2]) + mod_ref[0:1]).astype(BF16)

    result = (nn(normed_ref[...], square(weight_ref)) + bias_ref[0]).astype(BF16)

    @pl.when(part == 0)
    def _():
        q_ref[...] = result

    @pl.when(part > 0)
    def _():
        kv_ref[0] = result


def project(stream, modulation, weights, bias):
    tokens, width = stream.shape
    return pl.pallas_call(
        project_kernel,
        grid=(3,),
        in_specs=[
            whole((tokens, width)),
            whole((6, width)),
            matrix_at(weights, 0),
            pl.BlockSpec((1, 1, width), lambda part: (part, 0, 0)),
        ],
        out_specs=(
            whole((tokens, width)),
            whole((tokens, width)),
            pl.BlockSpec((1, tokens, width), lambda part: (jnp.maximum(part - 1, 0), 0, 0)),
        ),
        out_shape=(
            jax.ShapeDtypeStruct((tokens, width), BF16),
            jax.ShapeDtypeStruct((tokens, width), BF16),
            jax.ShapeDtypeStruct((2, tokens, width), BF16),
        ),
        compiler_params=params_of(),
        cost_estimate=pl.CostEstimate(
            flops=6 * tokens * width**2, transcendentals=0, bytes_accessed=12 * tokens * width
        ),
    )(stream, modulation, weights, bias)


GELU_SCALE = math.sqrt(2.0 / math.pi)


def gelu_parts(value):
    square = value * value
    tanh = jnp.tanh(GELU_SCALE * value * (1.0 + 0.044715 * square))
    return square, tanh


def mlp_kernel(
    mixed_ref, stream_ref, mod_ref, proj_ref, proj_b_ref, fc1_ref, fc1_b_ref, fc2_ref, fc2_b_ref,
    attn_ref, middle_ref, normed_ref, hidden_ref, active_ref, mlp_ref, result_ref,
):
    part = pl.program_id(0)

    @pl.when(part == 0)
    def _():
        attn_out = nn(mixed_ref[...], square(proj_ref)) + proj_b_ref[...]
        attn_ref[...] = attn_out
        middle = stream_ref[...] + mod_ref[2:3] * attn_out
        middle_ref[...] = middle
        normal, _ = normalize(middle)
        normed_ref[...] = (normal * (1.0 + mod_ref[4:5]) + mod_ref[3:4]).astype(BF16)

    hidden = nn(normed_ref[...], square(fc1_ref)) + fc1_b_ref[0]
    hidden_ref[0] = hidden
    _, tanh = gelu_parts(hidden)
    active = (0.5 * hidden * (1.0 + tanh)).astype(BF16)
    active_ref[0] = active
    product = nn(active, square(fc2_ref))

    @pl.when(part == 0)
    def _():
        mlp_ref[...] = product + fc2_b_ref[...]

    @pl.when(part > 0)
    def _():
        mlp_ref[...] += product

    @pl.when(part == pl.num_programs(0) - 1)
    def _():
        result_ref[...] = middle_ref[...] + mod_ref[5:6] * mlp_ref[...]


def mlp(mixed, stream, modulation, attn_w, weights, proj_b, fc1_b, fc2_b):
    tokens, width = stream.shape
    parts = fc1_b.shape[0]
    token, row = whole((tokens, width)), whole((1, width))
    by_part = lambda rows: pl.BlockSpec((1, rows, width), lambda part: (part, 0, 0))
    shape = lambda *dims: jax.ShapeDtypeStruct(dims[:-1], dims[-1])
    return pl.pallas_call(
        mlp_kernel,
        grid=(parts,),
        in_specs=[
            token, token, whole((6, width)), matrix_at(attn_w, 3, False), row,
            matrix_at(weights, 0), by_part(1), tall_at(weights, parts, parts), row,
        ],
        out_specs=(token, token, token, by_part(tokens), by_part(tokens), token, token),
        out_shape=(
            shape(tokens, width, F32),
            shape(tokens, width, F32),
            shape(tokens, width, BF16),
            shape(parts, tokens, width, F32),
            shape(parts, tokens, width, BF16),
            shape(tokens, width, F32),
            shape(tokens, width, F32),
        ),
        compiler_params=params_of(),
        cost_estimate=pl.CostEstimate(
            flops=(2 + 4 * parts) * tokens * width**2,
            transcendentals=parts * tokens * width,
            bytes_accessed=(20 + 6 * parts) * tokens * width,
        ),
    )(mixed, stream, modulation, attn_w, proj_b, weights, fc1_b, weights, fc2_b)


def mlp_back_kernel(
    grad_ref, mlp_ref, mod_ref, fc2_ref, fc1_ref, hidden_ref, active_ref, normed_ref, middle_ref,
    attn_ref, mixed_ref, proj_ref,
    fc2_g_ref, fc1_g_ref, proj_g_ref, fc1_b_ref, sums_ref, grad_middle_ref, grad_mixed_ref,
    low_ref, total_ref,
):
    part = pl.program_id(0)

    @pl.when(part == 0)
    def _():
        grad = grad_ref[...]
        sums_ref[2:3] = column_sum(grad * mlp_ref[...])
        low = (grad * mod_ref[5:6]).astype(BF16)
        low_ref[...] = low
        sums_ref[4:5] = column_sum(low.astype(F32))

    low = low_ref[...]
    put_square(fc2_g_ref, tn(active_ref[0], low))
    hidden = hidden_ref[0]
    squared, tanh = gelu_parts(hidden)
    slope = 0.5 * (1.0 + tanh) + (0.5 * GELU_SCALE) * hidden * (1.0 - tanh * tanh) * (
        1.0 + (3 * 0.044715) * squared
    )
    grad_hidden = (nt(low, square(fc2_ref)) * slope).astype(BF16)
    fc1_b_ref[0] = column_sum(grad_hidden.astype(F32))
    put_square(fc1_g_ref, tn(normed_ref[...], grad_hidden))
    product = nt(grad_hidden, square(fc1_ref))

    @pl.when(part == 0)
    def _():
        total_ref[...] = product

    @pl.when(part > 0)
    def _():
        total_ref[...] += product

    @pl.when(part == pl.num_programs(0) - 1)
    def _():
        grad_normed = total_ref[...]
        normal, scale = normalize(middle_ref[...])
        sums_ref[0:1] = column_sum(grad_normed)
        sums_ref[1:2] = column_sum(grad_normed * normal)
        grad_middle = grad_ref[...] + norm_back(grad_normed, normal, scale, mod_ref[4:5])
        grad_middle_ref[...] = grad_middle
        sums_ref[3:4] = column_sum(grad_middle * attn_ref[...])
        grad_attn = (grad_middle * mod_ref[2:3]).astype(BF16)
        sums_ref[5:6] = column_sum(grad_attn.astype(F32))
        put_square(proj_g_ref, tn(mixed_ref[...], grad_attn))
        grad_mixed_ref[...] = nt(grad_attn, square(proj_ref)).astype(BF16)


def mlp_back(
    grad, mlp_out, modulation, attn_w, weights, hidden, active, normed, middle, attn_out, mixed
):
    tokens, width = grad.shape
    parts = hidden.shape[0]
    token = whole((tokens, width))
    form = (weights.shape[0], parts) + weights.shape[2:]
    fc_form, proj_form = jax.ShapeDtypeStruct(form, BF16), jax.ShapeDtypeStruct(
        (form[0], 1) + form[2:], BF16
    )
    by_part = lambda rows: pl.BlockSpec((1, rows, width), lambda part: (part, 0, 0))
    shape = lambda *dims: jax.ShapeDtypeStruct(dims[:-1], dims[-1])
    return pl.pallas_call(
        mlp_back_kernel,
        grid=(parts,),
        in_specs=[
            token, token, whole((6, width)), tall_at(weights, parts, parts), matrix_at(weights, 0),
            by_part(tokens), by_part(tokens), token, token, token, token,
            matrix_at(attn_w, 3, False),
        ],
        out_specs=(
            tall_at(fc_form, 0, parts), matrix_at(fc_form, 0), matrix_at(proj_form, 0, False),
            by_part(1), whole((6, width)), token, token,
        ),
        out_shape=(
            fc_form,
            fc_form,
            proj_form,
            shape(parts, 1, width, F32),
            shape(6, width, F32),
            shape(tokens, width, F32),
            shape(tokens, width, BF16),
        ),
        scratch_shapes=[pltpu.VMEM((tokens, width), BF16), pltpu.VMEM((tokens, width), F32)],
        compiler_params=params_of(56),
        cost_estimate=pl.CostEstimate(
            flops=(4 + 8 * parts) * tokens * width**2,
            transcendentals=parts * tokens * width,
            bytes_accessed=(20 + 6 * parts) * tokens * width + 8 * parts * width**2,
        ),
    )(
        grad, mlp_out, modulation, weights, weights, hidden, active, normed, middle, attn_out,
        mixed, attn_w,
    )


def project_back_kernel(
    gq_ref, own_ref, back_ref, normed_ref, weight_ref, stream_ref, mod_ref, middle_ref,
    weight_g_ref, sums_ref, bias_ref, grad_ref, total_ref,
):
    part = pl.program_id(0)

    def step(grad, first):
        put_square(weight_g_ref, tn(normed_ref[...], grad))
        bias_ref[0] = column_sum(grad.astype(F32))
        product = nt(grad, square(weight_ref))
        total_ref[...] = product if first else total_ref[...] + product

    @pl.when(part == 0)
    def _():
        step(gq_ref[...], True)

    @pl.when(part > 0)
    def _():
        step((own_ref[0] + back_ref[0].astype(F32)).astype(BF16), False)

    @pl.when(part == 2)
    def _():
        grad_normed = total_ref[...]
        normal, scale = normalize(stream_ref[...])
        sums_ref[0:1] = column_sum(grad_normed)
        sums_ref[1:2] = column_sum(grad_normed * normal)
        grad_ref[...] = middle_ref[...] + norm_back(grad_normed, normal, scale, mod_ref[1:2])


def project_back(grad_q, grad_own, returned, normed, weights, stream, modulation, grad_middle):
    tokens, width = stream.shape
    token = whole((tokens, width))
    form = jax.ShapeDtypeStruct((weights.shape[0], 3) + weights.shape[2:], BF16)
    kv = pl.BlockSpec((1, tokens, width), lambda part: (jnp.maximum(part - 1, 0), 0, 0))
    return pl.pallas_call(
        project_back_kernel,
        grid=(3,),
        in_specs=[
            token, kv, kv, token, matrix_at(weights, 0), token, whole((6, width)), token,
        ],
        out_specs=(
            matrix_at(form, 0),
            whole((2, width)),
            pl.BlockSpec((1, 1, width), lambda part: (part, 0, 0)),
            token,
        ),
        out_shape=(
            form,
            jax.ShapeDtypeStruct((2, width), F32),
            jax.ShapeDtypeStruct((3, 1, width), F32),
            jax.ShapeDtypeStruct((tokens, width), F32),
        ),
        scratch_shapes=[pltpu.VMEM((tokens, width), F32)],
        compiler_params=params_of(),
        cost_estimate=pl.CostEstimate(
            flops=12 * tokens * width**2,
            transcendentals=0,
            bytes_accessed=24 * tokens * width + 12 * width**2,
        ),
    )(grad_q, grad_own, returned, normed, weights, stream, modulation, grad_middle)


def layer_forward(stream, modulation, biases, moves, attn_w, fetch_mlp):
    qkv_b, proj_b, fc1_b, fc2_b = biases
    normed, queries, own_kv = project(stream, modulation, attn_w, qkv_b)
    own_kv = moves.tick(own_kv)
    other_kv = moves.tick(swap_pairs(own_kv, "rep"))
    mixed, log_total = attend(queries, own_kv, other_kv)
    mixed = moves.tick(moves.tick(mixed))
    mlp_w, mixed = fetch_mlp(mixed)
    attn_out, middle, normed_mlp, hidden, active, mlp_out, result = mlp(
        mixed, stream, modulation, attn_w, mlp_w, proj_b, fc1_b, fc2_b
    )
    result = moves.tick(result)
    return result, (
        stream, normed, queries, own_kv, other_kv, mixed, log_total, attn_out, middle, normed_mlp,
        hidden, active, mlp_out, attn_w, mlp_w,
    )


def layer_backward(grad_out, modulation, kept, shards, moves, send_mlp, send_attn):
    (
        stream, normed, queries, own_kv, other_kv, mixed, log_total, attn_out, middle, normed_mlp,
        hidden, active, mlp_out, attn_w, mlp_w,
    ) = kept
    width = stream.shape[-1]
    fc2_g, fc1_g, proj_g, fc1_b, sums, grad_middle, grad_mixed = mlp_back(
        grad_out, mlp_out, modulation, attn_w, mlp_w, hidden, active, normed_mlp, middle, attn_out,
        mixed,
    )
    grad_mixed = moves.tick(grad_mixed)
    grad_mixed = send_mlp(fc1_g, fc2_g, grad_mixed)
    grad_q, grad_own, grad_other = attend_back(
        queries, own_kv, other_kv, grad_mixed, mixed, log_total
    )
    grad_other = moves.tick(grad_other)
    returned = swap_pairs(grad_other, "rep")
    qkv_g, attn_sums, qkv_b, grad_stream = project_back(
        grad_q, grad_own, returned, normed, attn_w, stream, modulation, grad_middle
    )
    grad_stream = moves.tick(grad_stream)
    send_attn(qkv_g, proj_g)
    grad_modulation = jnp.concatenate(
        [attn_sums[0], attn_sums[1], sums[3], sums[0], sums[1], sums[2]]
    )
    query_value = jnp.concatenate([qkv_b[0, 0], qkv_b[2, 0]])
    bias_grads = [
        part.reshape(shards, -1) for part in (query_value, sums[5], fc1_b.reshape(-1), sums[4])
    ]
    return grad_stream, grad_modulation, jnp.concatenate(bias_grads, axis=1)


def columns(matrix, width):
    return jnp.stack(jnp.split(matrix, matrix.shape[1] // width, axis=1))


def uncolumns(blocks):
    return jnp.concatenate(list(blocks), axis=1)


def shards_program(
    latents,
    image_loads,
    timesteps,
    classes,
    label_table,
    ada_weight,
    ada_bias,
    qkv_weight,
    qv_bias,
    proj_weight,
    proj_bias,
    fc1_weight,
    fc1_bias,
    fc2_weight,
    fc2_bias,
    cotangent,
):
    shards = lax.axis_size("shard")
    width = latents.shape[2]
    own_rows = width // shards
    ff_parts = fc1_weight.shape[2] // width
    shard, rep, seq = lax.axis_index("shard"), lax.axis_index("rep"), lax.axis_index("seq")

    one_hot = (
        classes[:, None] == jnp.arange(label_table.shape[0], dtype=jnp.int32)[None, :]
    ).astype(BF16)
    cond = dot(one_hot, label_table, (1,), (0,)) + time_embed(timesteps, width)
    cond_low = jax.nn.silu(cond).astype(BF16)
    live_own = (image_loads > 0).astype(BF16)
    shared = cube_gather(
        jnp.concatenate([cond_low[0], jnp.broadcast_to(live_own, (128,))]), ("rep", "shard")
    )
    live = lax.dynamic_slice(shared, (seq * shards + shard, width), (1, 1)).astype(F32)
    cond_rows = lax.dynamic_slice(
        shared[:, :width], (0, shard * own_rows), (shared.shape[0], own_rows)
    )
    stream = swap_layout(latents[0]).astype(F32)

    rings = ring_fits(own_rows)
    attn_packs, mlp_packs = [], []
    for layer in range(LAYERS):
        fc2_piece = fc2_weight[layer].reshape(ff_parts, own_rows, width)
        mlp_packs.append(jnp.concatenate([columns(fc1_weight[layer], width), fc2_piece]))
        attn_packs.append(
            jnp.concatenate([columns(qkv_weight[layer], width), proj_weight[layer][None]])
        )
    moves = Moves([(layer, attn_packs[layer], (0, 0)) for layer in range(LAYERS)])
    mlp_w = []

    def fetch_mlp(layer, mixed):
        if not rings:
            return gather_plain(mlp_packs[layer], (ff_parts, ff_parts)), mixed
        if layer == 0:
            mlp_w.append(gather_wide(mlp_packs[0])[0])
        if layer + 1 < LAYERS:
            later, (mlp_w[layer], mixed) = gather_wide(
                mlp_packs[layer + 1], (mlp_w[layer], mixed)
            )
            mlp_w.append(later)
        return mlp_w[layer], mixed

    small = jnp.concatenate([ada_bias, qv_bias, proj_bias, fc1_bias, fc2_bias], axis=1)
    small = cube_gather(small, ("shard",)).astype(F32)
    ends = [0]
    for bias in (ada_bias, qv_bias, proj_bias, fc1_bias, fc2_bias):
        ends.append(ends[-1] + bias.shape[1])
    biases, ada_b = [], []
    for layer in range(LAYERS):
        full = [small[:, layer, ends[at] : ends[at + 1]].reshape(-1) for at in range(5)]
        ada_b.append(full[0])
        qkv_b = jnp.concatenate([full[1][:width], jnp.zeros((width,), F32), full[1][width:]])
        biases.append(
            (
                qkv_b.reshape(3, 1, width),
                full[2][None],
                full[3].reshape(ff_parts, 1, width),
                full[4][None],
            )
        )

    mine = lax.dynamic_slice(cond_rows, (seq * shards, 0), (shards, own_rows))
    partial = jnp.concatenate(
        [dot(mine, ada_weight[layer], (1,), (0,)) for layer in range(LAYERS)], axis=1
    )
    modulations = cube_scatter(partial, "shard")
    modulations = [
        (modulations.reshape(LAYERS, -1)[layer] + ada_b[layer]).reshape(6, width)
        for layer in range(LAYERS)
    ]

    kept = []
    for layer in range(LAYERS):
        stream, layer_kept = layer_forward(
            stream,
            modulations[layer],
            biases[layer],
            moves,
            moves.need(layer),
            functools.partial(fetch_mlp, layer),
        )
        kept.append(layer_kept)
    moves = Moves()
    activations = swap_layout((stream * live).astype(BF16)).astype(F32)
    grad_stream = swap_layout(cotangent[0]).astype(F32) * live

    shares = []
    done = {}

    def flat(part):
        return part.reshape(part.shape[1], shards, own_rows, width).transpose(1, 0, 2, 3)

    def send_mlp(layer, fc1_g, fc2_g, grad_mixed):
        if not rings:
            tall = fc2_g.reshape(shards, ff_parts, own_rows, width)
            done["mlp", layer] = scatter_plain(jnp.concatenate([flat(fc1_g), tall], axis=1))
        else:
            both = jnp.concatenate([fc1_g, fc2_g], axis=1)
            both, grad_mixed = lax.optimization_barrier((both, grad_mixed))
            shares.append(scatter_wide(both))
        return grad_mixed

    def send_attn(layer, qkv_g, proj_g):
        if rings:
            moves.start(("attn", layer), [qkv_g, proj_g])
        else:
            both = jnp.concatenate([flat(qkv_g), flat(proj_g)], axis=1)
            done["attn", layer] = scatter_plain(both)

    bias_grads = [None] * LAYERS
    ada_w_grads = [None] * LAYERS
    ada_b_grads = [None] * LAYERS
    grad_cond = 0.0
    for layer in reversed(range(LAYERS)):
        grad_stream, grad_mod, bias_grads[layer] = layer_backward(
            grad_stream,
            modulations[layer],
            kept[layer],
            shards,
            moves,
            functools.partial(send_mlp, layer),
            functools.partial(send_attn, layer),
        )
        grad_mod = (grad_mod + swap_pairs(grad_mod, "rep")).astype(BF16)
        all_mod = cube_gather(grad_mod, ("seq", "shard"))
        ada_w_grads[layer] = dot(cond_rows, all_mod, (0,), (0,))
        own_mod = lax.dynamic_slice(
            all_mod, (0, shard * ada_bias.shape[1]), (all_mod.shape[0], ada_bias.shape[1])
        )
        ada_b_grads[layer] = jnp.sum(own_mod.astype(F32), axis=0)
        rep_mod = lax.dynamic_slice(all_mod, (rep * shards, 0), (shards, all_mod.shape[1]))
        grad_cond = grad_cond + dot(rep_mod, ada_weight[layer], (1,), (1,))

    latent_grad = swap_layout(grad_stream.astype(BF16)).astype(F32)
    all_cond = cube_gather(grad_cond, ("shard",))
    grad_cond_low = lax.dynamic_slice(all_cond, (0, shard, 0), (shards, 1, own_rows)).reshape(
        1, width
    )
    _, silu_pull = jax.vjp(jax.nn.silu, cond)
    cond_grad = silu_pull(grad_cond_low)[0]

    bias_total = cube_scatter(jnp.stack(bias_grads, axis=1), "shard")
    bias_total = bias_total + swap_pairs(bias_total, "rep")
    bias_total = bias_total + swap_pairs(bias_total, "seq")
    qv_b, proj_b, fc1_b, fc2_b = [
        bias_total[:, ends[at] - ends[1] : ends[at + 1] - ends[1]] for at in range(1, 5)
    ]
    if rings:
        moved, lates = moves.finish({3: shares[0], 8: shares[1]})
        done.update(moved)
        for layer, step in ((1, 3), (0, 8)):
            spread = cube_gather(lates[step], ("rep", "seq"))
            done["mlp", layer] = spread.reshape(-1, own_rows, width).astype(F32)
    weight_grads = []
    for layer in range(LAYERS):
        attn_grads, mlp_grads = done["attn", layer], done["mlp", layer]
        weight_grads.append(
            (
                uncolumns(attn_grads[:3]),
                attn_grads[3],
                uncolumns(mlp_grads[:ff_parts]),
                mlp_grads[ff_parts:].reshape(ff_parts * own_rows, width),
            )
        )
    qkv_g, proj_g, fc1_g, fc2_g = [
        jnp.stack([weight_grads[layer][at] for layer in range(LAYERS)]) for at in range(4)
    ]
    return (
        activations[None],
        latent_grad[None],
        cond_grad,
        jnp.stack(ada_w_grads),
        jnp.stack(ada_b_grads),
        qkv_g,
        qv_b,
        proj_g,
        proj_b,
        fc1_g,
        fc1_b,
        fc2_g,
        fc2_b,
    )


def solution(mesh):
    tokens = P(("rep", "shard"), "seq", None)
    images = P(("rep", "shard"))
    matrix = P(None, "shard", None)
    vector = P(None, "shard")
    return jax.shard_map(
        shards_program,
        mesh=mesh,
        in_specs=(tokens, images, images, images, P())
        + (matrix, vector) * 5
        + (tokens,),
        out_specs=(tokens, tokens, P(("rep", "shard"), None)) + (matrix, vector) * 5,
        check_vma=False,
    )
```

```python
import functools
import math

import jax
import jax.numpy as jnp
from jax import lax
from jax.experimental import pallas as pl
from jax.experimental.pallas import tpu as pltpu
from jax.sharding import PartitionSpec as P

HEADS = 12
LAYERS = 2
EPSILON = 1e-06
BF16 = jnp.bfloat16
F32 = jnp.float32


def swap_pairs(value, axis):
    return lax.ppermute(value, axis, [(0, 1), (1, 0)])


def swap_layout(value):
    moved = lax.ppermute(value, ("rep", "seq"), [(1, 2), (2, 1)])
    return jnp.where(lax.axis_index("rep") == lax.axis_index("seq"), value, moved)


def cube_pairs(value, axis, bit):
    return lax.ppermute(value, axis, [(at, at ^ bit) for at in range(lax.axis_size(axis))])


def cube_bits(axis):
    return [1 << place for place in range(lax.axis_size(axis).bit_length() - 1)]


def as_is(value):
    return value


def cube_gather(value, axes, tick=as_is):
    value = value[None]
    for axis in reversed(axes):
        for bit in cube_bits(axis):
            other = tick(cube_pairs(value, axis, bit))
            value = jnp.where(
                lax.axis_index(axis) & bit == 0,
                jnp.concatenate([value, other]),
                jnp.concatenate([other, value]),
            )
    return value


def cube_scatter(value, axis, tick=as_is):
    for bit in reversed(cube_bits(axis)):
        low, high = value[:bit], value[bit:]
        first = lax.axis_index(axis) & bit == 0
        other = tick(cube_pairs(jnp.where(first, high, low), axis, bit))
        value = jnp.where(first, low, high) + other
    return value[0]


def ring_order(size):
    half = size // 2
    return [2 * place for place in range(half)] + [2 * place + 1 for place in reversed(range(half))]


def ring_step(value, forward):
    size = lax.axis_size("shard")
    order = ring_order(size)
    step = 1 if forward else size - 1
    return lax.ppermute(
        value, "shard", [(order[at], order[(at + step) % size]) for at in range(size)]
    )


def ring_ids():
    size = lax.axis_size("shard")
    order = ring_order(size)
    places = [order.index(shard) for shard in range(size)]
    place = jnp.array(places, jnp.int32)[lax.axis_index("shard")]
    return jnp.array(order, jnp.int32)[(place + jnp.arange(size, dtype=jnp.int32)) % size]


OFFSETS = (-1, 1, -2, 2, -3, 3, 4)


def place_kernel(where, *refs):
    (own, *rest) = refs[:23]
    out, sem = refs[23:]
    blocks, beside = rest[0:7], rest[7:11]
    core_blocks, core_beside = rest[11:18], rest[18:22]
    rep, seq = where[8], where[9]
    unit = own.shape[1] // 6

    def put(src, shard, row, rows):
        start = pl.multiple_of(row * unit, unit)
        copy = pltpu.make_async_copy(src, out.at[shard, :, pl.ds(start, rows), :], sem)
        copy.start()
        return [copy]

    copies = put(own, where[0], 0, 6 * unit)
    for slot, offset in enumerate(OFFSETS):
        shard = where[offset % 8]
        far = 3 * rep + 2 * (1 - seq)
        copies += put(blocks[slot], shard, 3 * rep + seq, 2 * unit)
        copies += put(beside[slot // 2].at[slot % 2], shard, far, unit)
        far = 3 * (1 - rep) + 2 * (1 - seq)
        copies += put(core_blocks[slot], shard, 3 * (1 - rep) + seq, 2 * unit)
        copies += put(core_beside[slot // 2].at[slot % 2], shard, far, unit)
    for copy in copies:
        copy.wait()


def gather_ring(piece):
    count, rows, width = piece.shape
    shards = lax.axis_size("shard")
    unit = rows // 6
    rep, seq = lax.axis_index("rep"), lax.axis_index("seq")
    mine = lax.dynamic_slice(piece, (0, (3 * rep + seq) * unit, 0), (count, 2 * unit, width))

    def cross(*blocks):
        cut = [
            lax.dynamic_slice(block, (0, seq * unit, 0), (count, unit, width)) for block in blocks
        ]
        return swap_pairs(jnp.stack(cut), "seq")

    def core(block):
        return swap_pairs(block, "rep")

    def around(up, down):
        return ring_step(up, True), ring_step(down, False)

    up1, down1 = yield around(mine, mine)
    up2, down2, x1, *core1 = yield (
        *around(up1, down1), cross(up1, down1), core(up1), core(down1)
    )
    up3, down3, x2, *core2 = yield (
        *around(up2, down2), cross(up2, down2), core(up2), core(down2), core(x1)
    )
    up4, down4, x3, *core3 = yield (
        *around(up3[:, :unit], down3[:, unit:]), cross(up3, down3), core(up3), core(down3), core(x2)
    )
    far = jnp.concatenate([up4, down4], axis=1)
    x4, *core4 = yield (cross(far), core(far), core(x3))
    (core_x4,) = yield (core(x4),)
    parts = [up1, down1, up2, down2, up3, down3, far, x1, x2, x3, x4]
    parts += core1 + core2[:2] + core3[:2] + core4[:1]
    parts += [core2[2], core3[2], core4[1], core_x4]
    where = jnp.concatenate([ring_ids(), jnp.stack([rep, seq]).astype(jnp.int32)])
    anywhere = pl.BlockSpec(memory_space=pl.ANY)
    return pl.pallas_call(
        place_kernel,
        out_shape=jax.ShapeDtypeStruct((shards, count, rows, width), piece.dtype),
        in_specs=[pl.BlockSpec(memory_space=pltpu.SMEM)] + [anywhere] * 23,
        out_specs=pl.BlockSpec(memory_space=pltpu.VMEM),
        compiler_params=pltpu.CompilerParams(vmem_limit_bytes=32 * 2**20),
        scratch_shapes=[pltpu.SemaphoreType.DMA],
        cost_estimate=pl.CostEstimate(
            flops=0, transcendentals=0, bytes_accessed=2 * shards * piece.size * 2
        ),
    )(where, piece, *parts)


def gather_wide(piece, after=None):
    count, rows, width = piece.shape
    copies = lax.axis_size("rep") * lax.axis_size("seq")
    at = lax.axis_index("rep") * lax.axis_size("seq") + lax.axis_index("seq")
    own = lax.dynamic_slice(piece, (at * (count // copies), 0, 0), (count // copies, rows, width))
    if after is not None:
        own, after = lax.optimization_barrier((own, after))
    whole_piece = lax.all_gather(
        own.reshape(-1, width), ("shard", "rep", "seq"), axis=0, tiled=True
    )
    return whole_piece.reshape(-1, count, rows, width), after


def gather_plain(piece, stacked):
    first, parts = stacked
    width = piece.shape[2]
    whole_piece = lax.all_gather(piece, "shard", axis=0, tiled=False)
    flat = whole_piece.transpose(1, 0, 2, 3).reshape(-1, width, width)
    if parts:
        tall = whole_piece[:, first : first + parts].reshape(parts, width, width)
        flat = jnp.concatenate([flat[:first], tall, flat[first + parts :]])
    return flat[None]


def ring_fits(rows):
    return (
        lax.axis_size("shard") == 8
        and lax.axis_size("rep") == 2
        and lax.axis_size("seq") == 2
        and rows % 96 == 0
    )


def add(left, right):
    return (left.astype(F32) + right.astype(F32)).astype(BF16)


def scatter_ring(grads):
    shards, _, rows, width = grads[0].shape
    count = sum(part.shape[1] for part in grads)
    unit = rows // 6
    rep, seq = lax.axis_index("rep"), lax.axis_index("seq")
    ids = ring_ids()

    def half(which):
        cut = [
            lax.dynamic_slice(
                part, (0, 0, 3 * unit * which, 0), (shards, part.shape[1], 3 * unit, width)
            )
            for part in grads
        ]
        return jnp.concatenate(cut, axis=1)

    (got,) = yield (swap_pairs(half(1 - rep), "rep"),)
    paired = add(half(rep), got)

    def block(offset):
        return lax.dynamic_index_in_dim(paired, ids[offset % 8], 0, keepdims=False)

    def send(offsets):
        sent = [
            lax.dynamic_slice(block(offset), (0, 2 * (1 - seq) * unit, 0), (count, unit, width))
            for offset in offsets
        ]
        return swap_pairs(jnp.stack(sent), "seq")

    def join(offset, got):
        kept = lax.dynamic_slice(block(offset), (0, seq * unit, 0), (count, 2 * unit, width))
        zero = jnp.zeros_like(got)
        beside = jnp.where(
            seq == 0,
            jnp.concatenate([got, zero], axis=1),
            jnp.concatenate([zero, got], axis=1),
        )
        return add(kept, beside)

    far, near3 = yield (send((4,)), send((3, -3)))
    far = join(4, far[0])
    up, down, near2 = yield (
        ring_step(far[:, :unit], True),
        ring_step(far[:, unit:], False),
        send((2, -2)),
    )
    up3, down3 = join(3, near3[0]), join(-3, near3[1])
    up = jnp.concatenate([add(up3[:, :unit], up), up3[:, unit:]], axis=1)
    down = jnp.concatenate([down3[:, :unit], add(down3[:, unit:], down)], axis=1)
    up, down, near1 = yield (ring_step(up, True), ring_step(down, False), send((1, -1)))
    up, down, here = yield (
        ring_step(add(join(2, near2[0]), up), True),
        ring_step(add(join(-2, near2[1]), down), False),
        send((0,)),
    )
    up, down = yield (
        ring_step(add(join(1, near1[0]), up), True),
        ring_step(add(join(-1, near1[1]), down), False),
    )
    total = add(join(0, here[0]).astype(F32) + up.astype(F32), down)
    (other,) = yield (swap_pairs(total, "seq"),)
    left, right = jnp.where(seq == 0, total, other), jnp.where(seq == 0, other, total)
    mine = jnp.concatenate(
        [left[:, :unit], add(left[:, unit:], right[:, :unit]), right[:, unit:]], axis=1
    )
    (other,) = yield (swap_pairs(mine, "rep"),)
    return jnp.where(
        rep == 0,
        jnp.concatenate([mine, other], axis=1),
        jnp.concatenate([other, mine], axis=1),
    ).astype(F32)


class Moves:
    def __init__(self, queue=()):
        self.queue = list(queue)
        self.running = []
        self.done = {}
        self.held = True
        if self.queue:
            self.pull()

    def pull(self):
        (key, piece, stacked) = self.queue.pop(0)
        if not ring_fits(piece.shape[1]):
            self.done[key] = gather_plain(piece, stacked)
            return
        if self.running:
            piece, moving = lax.optimization_barrier(
                (piece, [moving for _, _, moving, _ in self.running])
            )
            self.running = [
                (*move[:2], got, move[3]) for move, got in zip(self.running, moving)
            ]
        stages = gather_ring(piece)
        self.running.append((key, stages, next(stages), 1))

    def start(self, key, grads):
        stages = scatter_ring(grads)
        self.running.append((key, stages, next(stages), 9))

    def tick(self, value=None, only=None):
        waiting = [moving for _, _, moving, _ in self.running]
        if value is not None and waiting:
            value, waiting = lax.optimization_barrier((value, waiting))
        still = []
        for (key, stages, _, count), moving in zip(self.running, waiting):
            if only not in (None, key):
                still.append((key, stages, moving, count))
                continue
            try:
                still.append((key, stages, stages.send(moving), count + 1))
            except StopIteration as end:
                self.done[key] = end.value
        self.running = still
        if self.queue and not self.held and all(count > 4 for _, _, _, count in still):
            self.pull()
        return value

    def need(self, key):
        while key not in self.done:
            self.tick(only=key if any(key == move[0] for move in self.running) else None)
        return self.done[key]

    def finish(self, lates):
        step = 0
        while self.running:
            step += 1
            value = self.tick(lates.get(step))
            if step in lates:
                lates[step] = value
        return self.done, lates


def scatter_wide(grads):
    return lax.psum_scatter(
        grads.reshape(-1, grads.shape[-1]),
        ("shard", "rep", "seq"),
        scatter_dimension=0,
        tiled=True,
    )


def scatter_plain(grads):
    owned = lax.psum_scatter(grads.astype(F32), "shard", scatter_dimension=0, tiled=False)
    return lax.psum(owned.astype(BF16), ("rep", "seq")).astype(F32)


def normalize(values):
    centered = values - jnp.mean(values, axis=-1, keepdims=True)
    scale = lax.rsqrt(jnp.mean(centered * centered, axis=-1, keepdims=True) + EPSILON)
    return centered * scale, scale


def norm_back(grad, normal, scale, factor):
    u = grad * (1.0 + factor)
    return (
        u
        - jnp.mean(u, axis=-1, keepdims=True)
        - normal * jnp.mean(u * normal, axis=-1, keepdims=True)
    ) * scale


def time_embed(steps, width):
    half_width = width // 2
    freqs = jnp.exp(-math.log(10000.0) * jnp.arange(half_width, dtype=F32) / half_width)
    angles = steps.astype(F32)[:, None] * freqs[None, :]
    return jnp.concatenate([jnp.cos(angles), jnp.sin(angles)], axis=-1)


def dot(left, right, left_dims, right_dims):
    return lax.dot_general(
        left, right, ((left_dims, right_dims), ((), ())), preferred_element_type=F32
    )


def nt(left, right, **kw):
    return lax.dot_general(left, right, (((1,), (1,)), ((), ())), preferred_element_type=F32, **kw)


def tn(left, right):
    return lax.dot_general(left, right, (((0,), (0,)), ((), ())), preferred_element_type=F32)


def nn(left, right):
    return lax.dot_general(left, right, (((1,), (0,)), ((), ())), preferred_element_type=F32)


def head_mask(values, head, size):
    lanes = lax.broadcasted_iota(jnp.int32, values.shape, 1)
    inside = (lanes >= head * size) & (lanes < (head + 1) * size)
    return jnp.where(inside, values, jnp.zeros_like(values))


def attend_kernel(size, q_ref, own_ref, other_ref, mixed_ref, log_ref):
    pair = q_ref.shape[1] // size
    queries = q_ref[...] * jnp.asarray(size**-0.5, BF16)
    blocks = []
    for head in range(pair):
        query = head_mask(queries, head, size)
        scores = [nt(own_ref[0], query), nt(other_ref[0], query)]
        top = jnp.maximum(*[jnp.max(part, axis=0, keepdims=True) for part in scores])
        expo = [jnp.exp(part - top) for part in scores]
        totals = sum(jnp.sum(part, axis=0, keepdims=True) for part in expo)
        mixed = tn(own_ref[1], expo[0].astype(BF16)) + tn(other_ref[1], expo[1].astype(BF16))
        blocks.append(mixed[head * size : (head + 1) * size] / totals)
        log_ref[0, head : head + 1, :] = top + jnp.log(totals)
    mixed_ref[...] = jnp.transpose(jnp.concatenate(blocks, axis=0)).astype(BF16)


def attend(queries, own_kv, other_kv):
    tokens, width = queries.shape
    pair = 128 // (width // HEADS)
    groups = HEADS // pair
    kv_spec = pl.BlockSpec((2, tokens, 128), lambda group: (0, 0, group))
    token_spec = pl.BlockSpec((tokens, 128), lambda group: (0, group))
    flops = 8 * tokens * tokens * width
    return pl.pallas_call(
        functools.partial(attend_kernel, width // HEADS),
        grid=(groups,),
        in_specs=[token_spec, kv_spec, kv_spec],
        out_specs=(token_spec, pl.BlockSpec((1, pair, tokens), lambda group: (group, 0, 0))),
        out_shape=(
            jax.ShapeDtypeStruct((tokens, width), BF16),
            jax.ShapeDtypeStruct((groups, pair, tokens), F32),
        ),
        compiler_params=pltpu.CompilerParams(vmem_limit_bytes=40 * 2**20),
        cost_estimate=pl.CostEstimate(
            flops=4 * flops, transcendentals=2 * HEADS * tokens**2, bytes_accessed=12 * queries.size
        ),
    )(queries, own_kv, other_kv)


def attend_back_kernel(
    size, q_ref, own_ref, other_ref, grad_ref, mixed_ref, log_ref, dq_ref, down_ref, dother_ref
):
    pair = q_ref.shape[1] // size
    scale = jnp.asarray(size**-0.5, BF16)
    queries = q_ref[...] * scale
    product = grad_ref[...].astype(F32) * mixed_ref[...].astype(F32)
    ones = jnp.ones((8, product.shape[1]), F32)
    grad_queries = []
    grad_kv = {}
    for head in range(pair):
        query, grad = head_mask(queries, head, size), head_mask(grad_ref[...], head, size)
        delta = nt(ones, head_mask(product, head, size), precision=lax.Precision.HIGHEST)[0:1]
        log_total = log_ref[0, head : head + 1, :]
        grad_query = None
        for side, kv_ref in enumerate((own_ref, other_ref)):
            probs = jnp.exp(nt(kv_ref[0], query) - log_total)
            grad_scores = (probs * (nt(kv_ref[1], grad) - delta)).astype(BF16)
            parts = (nn(grad_scores, query), nn(probs.astype(BF16), grad))
            before = grad_kv.get(side)
            grad_kv[side] = parts if before is None else tuple(a + b for a, b in zip(before, parts))
            part = tn(kv_ref[0], grad_scores)[head * size : (head + 1) * size]
            grad_query = part if grad_query is None else grad_query + part
        grad_queries.append(grad_query)
    total = jnp.transpose(jnp.concatenate(grad_queries, axis=0)) * (size**-0.5)
    dq_ref[...] = total.astype(BF16)
    for side, out_ref in enumerate((down_ref, dother_ref)):
        for at in range(2):
            out_ref[at] = grad_kv[side][at].astype(out_ref.dtype)


def attend_back(queries, own_kv, other_kv, grad_mixed, mixed, log_total):
    tokens, width = queries.shape
    pair = 128 // (width // HEADS)
    groups = HEADS // pair
    kv_spec = pl.BlockSpec((2, tokens, 128), lambda group: (0, 0, group))
    token_spec = pl.BlockSpec((tokens, 128), lambda group: (0, group))
    flops = 20 * tokens * tokens * width
    return pl.pallas_call(
        functools.partial(attend_back_kernel, width // HEADS),
        grid=(groups,),
        in_specs=[
            token_spec,
            kv_spec,
            kv_spec,
            token_spec,
            token_spec,
            pl.BlockSpec((1, pair, tokens), lambda group: (group, 0, 0)),
        ],
        out_specs=(token_spec, kv_spec, kv_spec),
        out_shape=(
            jax.ShapeDtypeStruct((tokens, width), BF16),
            jax.ShapeDtypeStruct(own_kv.shape, F32),
            jax.ShapeDtypeStruct(own_kv.shape, BF16),
        ),
        compiler_params=pltpu.CompilerParams(vmem_limit_bytes=40 * 2**20),
        cost_estimate=pl.CostEstimate(
            flops=4 * flops, transcendentals=2 * HEADS * tokens**2, bytes_accessed=24 * queries.size
        ),
    )(queries, own_kv, other_kv, grad_mixed, mixed, log_total)


def params_of(megabytes=48):
    return pltpu.CompilerParams(vmem_limit_bytes=megabytes * 2**20)


def whole(shape):
    return pl.BlockSpec(shape, lambda *at: (0,) * len(shape))


def column_sum(values):
    return jnp.sum(values, axis=0, keepdims=True)


def matrix_at(array, at, moving=True):
    shards, _, rows, width = array.shape
    return pl.BlockSpec(
        (shards, 1, rows, width), lambda part: (0, at + part if moving else at, 0, 0)
    )


def tall_at(array, at, parts):
    shards, _, rows, width = array.shape
    if shards == 1:
        return matrix_at(array, at)
    return pl.BlockSpec((shards // parts, parts, rows, width), lambda part: (part, at // parts, 0, 0))


def square(ref):
    return ref[...].reshape(ref.shape[-1], ref.shape[-1])


def put_square(ref, value):
    ref[...] = value.astype(ref.dtype).reshape(ref.shape)


def project_kernel(stream_ref, mod_ref, weight_ref, bias_ref, normed_ref, q_ref, kv_ref):
    part = pl.program_id(0)

    @pl.when(part == 0)
    def _():
        normal, _ = normalize(stream_ref[...])
        normed_ref[...] = (normal * (1.0 + mod_ref[1:2]) + mod_ref[0:1]).astype(BF16)

    result = (nn(normed_ref[...], square(weight_ref)) + bias_ref[0]).astype(BF16)

    @pl.when(part == 0)
    def _():
        q_ref[...] = result

    @pl.when(part > 0)
    def _():
        kv_ref[0] = result


def project(stream, modulation, weights, bias):
    tokens, width = stream.shape
    return pl.pallas_call(
        project_kernel,
        grid=(3,),
        in_specs=[
            whole((tokens, width)),
            whole((6, width)),
            matrix_at(weights, 0),
            pl.BlockSpec((1, 1, width), lambda part: (part, 0, 0)),
        ],
        out_specs=(
            whole((tokens, width)),
            whole((tokens, width)),
            pl.BlockSpec((1, tokens, width), lambda part: (jnp.maximum(part - 1, 0), 0, 0)),
        ),
        out_shape=(
            jax.ShapeDtypeStruct((tokens, width), BF16),
            jax.ShapeDtypeStruct((tokens, width), BF16),
            jax.ShapeDtypeStruct((2, tokens, width), BF16),
        ),
        compiler_params=params_of(),
        cost_estimate=pl.CostEstimate(
            flops=6 * tokens * width**2, transcendentals=0, bytes_accessed=12 * tokens * width
        ),
    )(stream, modulation, weights, bias)


GELU_SCALE = math.sqrt(2.0 / math.pi)


def gelu_parts(value):
    square = value * value
    tanh = jnp.tanh(GELU_SCALE * value * (1.0 + 0.044715 * square))
    return square, tanh


def mlp_kernel(
    mixed_ref, stream_ref, mod_ref, proj_ref, proj_b_ref, fc1_ref, fc1_b_ref, fc2_ref, fc2_b_ref,
    attn_ref, middle_ref, normed_ref, hidden_ref, active_ref, mlp_ref, result_ref,
):
    part = pl.program_id(0)

    @pl.when(part == 0)
    def _():
        attn_out = nn(mixed_ref[...], square(proj_ref)) + proj_b_ref[...]
        attn_ref[...] = attn_out
        middle = stream_ref[...] + mod_ref[2:3] * attn_out
        middle_ref[...] = middle
        normal, _ = normalize(middle)
        normed_ref[...] = (normal * (1.0 + mod_ref[4:5]) + mod_ref[3:4]).astype(BF16)

    hidden = nn(normed_ref[...], square(fc1_ref)) + fc1_b_ref[0]
    hidden_ref[0] = hidden
    _, tanh = gelu_parts(hidden)
    active = (0.5 * hidden * (1.0 + tanh)).astype(BF16)
    active_ref[0] = active
    product = nn(active, square(fc2_ref))

    @pl.when(part == 0)
    def _():
        mlp_ref[...] = product + fc2_b_ref[...]

    @pl.when(part > 0)
    def _():
        mlp_ref[...] += product

    @pl.when(part == pl.num_programs(0) - 1)
    def _():
        result_ref[...] = middle_ref[...] + mod_ref[5:6] * mlp_ref[...]


def mlp(mixed, stream, modulation, attn_w, weights, proj_b, fc1_b, fc2_b):
    tokens, width = stream.shape
    parts = fc1_b.shape[0]
    token, row = whole((tokens, width)), whole((1, width))
    by_part = lambda rows: pl.BlockSpec((1, rows, width), lambda part: (part, 0, 0))
    shape = lambda *dims: jax.ShapeDtypeStruct(dims[:-1], dims[-1])
    return pl.pallas_call(
        mlp_kernel,
        grid=(parts,),
        in_specs=[
            token, token, whole((6, width)), matrix_at(attn_w, 3, False), row,
            matrix_at(weights, 0), by_part(1), tall_at(weights, parts, parts), row,
        ],
        out_specs=(token, token, token, by_part(tokens), by_part(tokens), token, token),
        out_shape=(
            shape(tokens, width, F32),
            shape(tokens, width, F32),
            shape(tokens, width, BF16),
            shape(parts, tokens, width, F32),
            shape(parts, tokens, width, BF16),
            shape(tokens, width, F32),
            shape(tokens, width, F32),
        ),
        compiler_params=params_of(),
        cost_estimate=pl.CostEstimate(
            flops=(2 + 4 * parts) * tokens * width**2,
            transcendentals=parts * tokens * width,
            bytes_accessed=(20 + 6 * parts) * tokens * width,
        ),
    )(mixed, stream, modulation, attn_w, proj_b, weights, fc1_b, weights, fc2_b)


def mlp_back_kernel(
    grad_ref, mlp_ref, mod_ref, fc2_ref, fc1_ref, hidden_ref, active_ref, normed_ref, middle_ref,
    attn_ref, mixed_ref, proj_ref,
    fc2_g_ref, fc1_g_ref, proj_g_ref, fc1_b_ref, sums_ref, grad_middle_ref, grad_mixed_ref,
    low_ref, total_ref,
):
    part = pl.program_id(0)

    @pl.when(part == 0)
    def _():
        grad = grad_ref[...]
        sums_ref[2:3] = column_sum(grad * mlp_ref[...])
        low = (grad * mod_ref[5:6]).astype(BF16)
        low_ref[...] = low
        sums_ref[4:5] = column_sum(low.astype(F32))

    low = low_ref[...]
    put_square(fc2_g_ref, tn(active_ref[0], low))
    hidden = hidden_ref[0]
    squared, tanh = gelu_parts(hidden)
    slope = 0.5 * (1.0 + tanh) + (0.5 * GELU_SCALE) * hidden * (1.0 - tanh * tanh) * (
        1.0 + (3 * 0.044715) * squared
    )
    grad_hidden = (nt(low, square(fc2_ref)) * slope).astype(BF16)
    fc1_b_ref[0] = column_sum(grad_hidden.astype(F32))
    put_square(fc1_g_ref, tn(normed_ref[...], grad_hidden))
    product = nt(grad_hidden, square(fc1_ref))

    @pl.when(part == 0)
    def _():
        total_ref[...] = product

    @pl.when(part > 0)
    def _():
        total_ref[...] += product

    @pl.when(part == pl.num_programs(0) - 1)
    def _():
        grad_normed = total_ref[...]
        normal, scale = normalize(middle_ref[...])
        sums_ref[0:1] = column_sum(grad_normed)
        sums_ref[1:2] = column_sum(grad_normed * normal)
        grad_middle = grad_ref[...] + norm_back(grad_normed, normal, scale, mod_ref[4:5])
        grad_middle_ref[...] = grad_middle
        sums_ref[3:4] = column_sum(grad_middle * attn_ref[...])
        grad_attn = (grad_middle * mod_ref[2:3]).astype(BF16)
        sums_ref[5:6] = column_sum(grad_attn.astype(F32))
        put_square(proj_g_ref, tn(mixed_ref[...], grad_attn))
        grad_mixed_ref[...] = nt(grad_attn, square(proj_ref)).astype(BF16)


def mlp_back(
    grad, mlp_out, modulation, attn_w, weights, hidden, active, normed, middle, attn_out, mixed
):
    tokens, width = grad.shape
    parts = hidden.shape[0]
    token = whole((tokens, width))
    form = (weights.shape[0], parts) + weights.shape[2:]
    fc_form, proj_form = jax.ShapeDtypeStruct(form, BF16), jax.ShapeDtypeStruct(
        (form[0], 1) + form[2:], BF16
    )
    by_part = lambda rows: pl.BlockSpec((1, rows, width), lambda part: (part, 0, 0))
    shape = lambda *dims: jax.ShapeDtypeStruct(dims[:-1], dims[-1])
    return pl.pallas_call(
        mlp_back_kernel,
        grid=(parts,),
        in_specs=[
            token, token, whole((6, width)), tall_at(weights, parts, parts), matrix_at(weights, 0),
            by_part(tokens), by_part(tokens), token, token, token, token,
            matrix_at(attn_w, 3, False),
        ],
        out_specs=(
            tall_at(fc_form, 0, parts), matrix_at(fc_form, 0), matrix_at(proj_form, 0, False),
            by_part(1), whole((6, width)), token, token,
        ),
        out_shape=(
            fc_form,
            fc_form,
            proj_form,
            shape(parts, 1, width, F32),
            shape(6, width, F32),
            shape(tokens, width, F32),
            shape(tokens, width, BF16),
        ),
        scratch_shapes=[pltpu.VMEM((tokens, width), BF16), pltpu.VMEM((tokens, width), F32)],
        compiler_params=params_of(56),
        cost_estimate=pl.CostEstimate(
            flops=(4 + 8 * parts) * tokens * width**2,
            transcendentals=parts * tokens * width,
            bytes_accessed=(20 + 6 * parts) * tokens * width + 8 * parts * width**2,
        ),
    )(
        grad, mlp_out, modulation, weights, weights, hidden, active, normed, middle, attn_out,
        mixed, attn_w,
    )


def project_back_kernel(
    gq_ref, own_ref, back_ref, normed_ref, weight_ref, stream_ref, mod_ref, middle_ref,
    weight_g_ref, sums_ref, bias_ref, grad_ref, total_ref,
):
    part = pl.program_id(0)

    def step(grad, first):
        put_square(weight_g_ref, tn(normed_ref[...], grad))
        bias_ref[0] = column_sum(grad.astype(F32))
        product = nt(grad, square(weight_ref))
        total_ref[...] = product if first else total_ref[...] + product

    @pl.when(part == 0)
    def _():
        step(gq_ref[...], True)

    @pl.when(part > 0)
    def _():
        step((own_ref[0] + back_ref[0].astype(F32)).astype(BF16), False)

    @pl.when(part == 2)
    def _():
        grad_normed = total_ref[...]
        normal, scale = normalize(stream_ref[...])
        sums_ref[0:1] = column_sum(grad_normed)
        sums_ref[1:2] = column_sum(grad_normed * normal)
        grad_ref[...] = middle_ref[...] + norm_back(grad_normed, normal, scale, mod_ref[1:2])


def project_back(grad_q, grad_own, returned, normed, weights, stream, modulation, grad_middle):
    tokens, width = stream.shape
    token = whole((tokens, width))
    form = jax.ShapeDtypeStruct((weights.shape[0], 3) + weights.shape[2:], BF16)
    kv = pl.BlockSpec((1, tokens, width), lambda part: (jnp.maximum(part - 1, 0), 0, 0))
    return pl.pallas_call(
        project_back_kernel,
        grid=(3,),
        in_specs=[
            token, kv, kv, token, matrix_at(weights, 0), token, whole((6, width)), token,
        ],
        out_specs=(
            matrix_at(form, 0),
            whole((2, width)),
            pl.BlockSpec((1, 1, width), lambda part: (part, 0, 0)),
            token,
        ),
        out_shape=(
            form,
            jax.ShapeDtypeStruct((2, width), F32),
            jax.ShapeDtypeStruct((3, 1, width), F32),
            jax.ShapeDtypeStruct((tokens, width), F32),
        ),
        scratch_shapes=[pltpu.VMEM((tokens, width), F32)],
        compiler_params=params_of(),
        cost_estimate=pl.CostEstimate(
            flops=12 * tokens * width**2,
            transcendentals=0,
            bytes_accessed=24 * tokens * width + 12 * width**2,
        ),
    )(grad_q, grad_own, returned, normed, weights, stream, modulation, grad_middle)


def layer_forward(stream, modulation, biases, moves, attn_w, fetch_mlp):
    qkv_b, proj_b, fc1_b, fc2_b = biases
    normed, queries, own_kv = project(stream, modulation, attn_w, qkv_b)
    moves.held = False
    own_kv = moves.tick(fetch_mlp(own_kv))
    other_kv = moves.tick(swap_pairs(own_kv, "rep"))
    mixed, log_total = attend(queries, own_kv, other_kv)
    mixed = moves.tick(moves.tick(mixed))
    mlp_w = fetch_mlp()
    attn_out, middle, normed_mlp, hidden, active, mlp_out, result = mlp(
        mixed, stream, modulation, attn_w, mlp_w, proj_b, fc1_b, fc2_b
    )
    result = moves.tick(result)
    return result, (
        stream, normed, queries, own_kv, other_kv, mixed, log_total, attn_out, middle, normed_mlp,
        hidden, active, mlp_out, attn_w, mlp_w,
    )


def layer_backward(grad_out, modulation, kept, shards, moves, send_mlp, send_attn):
    (
        stream, normed, queries, own_kv, other_kv, mixed, log_total, attn_out, middle, normed_mlp,
        hidden, active, mlp_out, attn_w, mlp_w,
    ) = kept
    width = stream.shape[-1]
    fc2_g, fc1_g, proj_g, fc1_b, sums, grad_middle, grad_mixed = mlp_back(
        grad_out, mlp_out, modulation, attn_w, mlp_w, hidden, active, normed_mlp, middle, attn_out,
        mixed,
    )
    grad_mixed = moves.tick(grad_mixed)
    grad_mixed = send_mlp(fc1_g, fc2_g, grad_mixed)
    grad_q, grad_own, grad_other = attend_back(
        queries, own_kv, other_kv, grad_mixed, mixed, log_total
    )
    grad_other = moves.tick(grad_other)
    returned = swap_pairs(grad_other, "rep")
    qkv_g, attn_sums, qkv_b, grad_stream = project_back(
        grad_q, grad_own, returned, normed, attn_w, stream, modulation, grad_middle
    )
    grad_stream = moves.tick(grad_stream)
    send_attn(qkv_g, proj_g)
    grad_modulation = jnp.concatenate(
        [attn_sums[0], attn_sums[1], sums[3], sums[0], sums[1], sums[2]]
    )
    query_value = jnp.concatenate([qkv_b[0, 0], qkv_b[2, 0]])
    bias_grads = [
        part.reshape(shards, -1) for part in (query_value, sums[5], fc1_b.reshape(-1), sums[4])
    ]
    return grad_stream, grad_modulation, jnp.concatenate(bias_grads, axis=1)


def columns(matrix, width):
    return jnp.stack(jnp.split(matrix, matrix.shape[1] // width, axis=1))


def uncolumns(blocks):
    return jnp.concatenate(list(blocks), axis=1)


def shards_program(
    latents,
    image_loads,
    timesteps,
    classes,
    label_table,
    ada_weight,
    ada_bias,
    qkv_weight,
    qv_bias,
    proj_weight,
    proj_bias,
    fc1_weight,
    fc1_bias,
    fc2_weight,
    fc2_bias,
    cotangent,
):
    shards = lax.axis_size("shard")
    width = latents.shape[2]
    own_rows = width // shards
    ff_parts = fc1_weight.shape[2] // width
    shard, rep, seq = lax.axis_index("shard"), lax.axis_index("rep"), lax.axis_index("seq")

    rings = ring_fits(own_rows)
    attn_packs, mlp_packs = [], []
    for layer in range(LAYERS):
        fc2_piece = fc2_weight[layer].reshape(ff_parts, own_rows, width)
        mlp_packs.append(jnp.concatenate([columns(fc1_weight[layer], width), fc2_piece]))
        attn_packs.append(
            jnp.concatenate([columns(qkv_weight[layer], width), proj_weight[layer][None]])
        )
    moves = Moves([(layer, attn_packs[layer], (0, 0)) for layer in range(LAYERS)])

    one_hot = (
        classes[:, None] == jnp.arange(label_table.shape[0], dtype=jnp.int32)[None, :]
    ).astype(BF16)
    cond = dot(one_hot, label_table, (1,), (0,)) + time_embed(timesteps, width)
    cond_low = jax.nn.silu(cond).astype(BF16)
    live_own = (image_loads > 0).astype(BF16)
    shared = cube_gather(
        jnp.concatenate([cond_low[0], jnp.broadcast_to(live_own, (128,))]),
        ("rep", "shard"),
        moves.tick,
    )
    live = lax.dynamic_slice(shared, (seq * shards + shard, width), (1, 1)).astype(F32)
    cond_rows = lax.dynamic_slice(
        shared[:, :width], (0, shard * own_rows), (shared.shape[0], own_rows)
    )
    stream = swap_layout(latents[0]).astype(F32)

    mlp_w = []

    def fetch_mlp(layer, ahead=None):
        if not rings:
            if ahead is not None:
                return ahead
            return gather_plain(mlp_packs[layer], (ff_parts, ff_parts))
        if ahead is None:
            return mlp_w[layer]
        if layer + 1 < LAYERS:
            later, (mlp_w[layer], ahead) = gather_wide(mlp_packs[layer + 1], (mlp_w[layer], ahead))
            mlp_w.append(later)
        return ahead

    if rings:
        mlp_w.append(gather_wide(mlp_packs[0])[0])

    small = jnp.concatenate([ada_bias, qv_bias, proj_bias, fc1_bias, fc2_bias], axis=1)
    small = cube_gather(small, ("shard",)).astype(F32)
    ends = [0]
    for bias in (ada_bias, qv_bias, proj_bias, fc1_bias, fc2_bias):
        ends.append(ends[-1] + bias.shape[1])
    biases, ada_b = [], []
    for layer in range(LAYERS):
        full = [small[:, layer, ends[at] : ends[at + 1]].reshape(-1) for at in range(5)]
        ada_b.append(full[0])
        qkv_b = jnp.concatenate([full[1][:width], jnp.zeros((width,), F32), full[1][width:]])
        biases.append(
            (
                qkv_b.reshape(3, 1, width),
                full[2][None],
                full[3].reshape(ff_parts, 1, width),
                full[4][None],
            )
        )

    mine = lax.dynamic_slice(cond_rows, (seq * shards, 0), (shards, own_rows))
    partial = jnp.concatenate(
        [dot(mine, ada_weight[layer], (1,), (0,)) for layer in range(LAYERS)], axis=1
    )
    modulations = cube_scatter(partial, "shard", moves.tick)
    modulations = [
        (modulations.reshape(LAYERS, -1)[layer] + ada_b[layer]).reshape(6, width)
        for layer in range(LAYERS)
    ]

    kept = []
    for layer in range(LAYERS):
        stream, layer_kept = layer_forward(
            stream,
            modulations[layer],
            biases[layer],
            moves,
            moves.need(layer),
            functools.partial(fetch_mlp, layer),
        )
        kept.append(layer_kept)
    moves = Moves()
    activations = swap_layout((stream * live).astype(BF16)).astype(F32)
    grad_stream = swap_layout(cotangent[0]).astype(F32) * live

    shares = []
    done = {}

    def flat(part):
        return part.reshape(part.shape[1], shards, own_rows, width).transpose(1, 0, 2, 3)

    def send_mlp(layer, fc1_g, fc2_g, grad_mixed):
        if not rings:
            tall = fc2_g.reshape(shards, ff_parts, own_rows, width)
            done["mlp", layer] = scatter_plain(jnp.concatenate([flat(fc1_g), tall], axis=1))
        else:
            both = jnp.concatenate([fc1_g, fc2_g], axis=1)
            both, grad_mixed = lax.optimization_barrier((both, grad_mixed))
            shares.append(scatter_wide(both))
        return grad_mixed

    def send_attn(layer, qkv_g, proj_g):
        if rings:
            moves.start(("attn", layer), [qkv_g, proj_g])
        else:
            both = jnp.concatenate([flat(qkv_g), flat(proj_g)], axis=1)
            done["attn", layer] = scatter_plain(both)

    bias_grads = [None] * LAYERS
    ada_w_grads = [None] * LAYERS
    ada_b_grads = [None] * LAYERS
    grad_cond = 0.0
    for layer in reversed(range(LAYERS)):
        grad_stream, grad_mod, bias_grads[layer] = layer_backward(
            grad_stream,
            modulations[layer],
            kept[layer],
            shards,
            moves,
            functools.partial(send_mlp, layer),
            functools.partial(send_attn, layer),
        )
        grad_mod = (grad_mod + swap_pairs(grad_mod, "rep")).astype(BF16)
        all_mod = cube_gather(grad_mod, ("seq", "shard"))
        ada_w_grads[layer] = dot(cond_rows, all_mod, (0,), (0,))
        own_mod = lax.dynamic_slice(
            all_mod, (0, shard * ada_bias.shape[1]), (all_mod.shape[0], ada_bias.shape[1])
        )
        ada_b_grads[layer] = jnp.sum(own_mod.astype(F32), axis=0)
        rep_mod = lax.dynamic_slice(all_mod, (rep * shards, 0), (shards, all_mod.shape[1]))
        grad_cond = grad_cond + dot(rep_mod, ada_weight[layer], (1,), (1,))

    latent_grad = swap_layout(grad_stream.astype(BF16)).astype(F32)
    all_cond = cube_gather(grad_cond, ("shard",))
    grad_cond_low = lax.dynamic_slice(all_cond, (0, shard, 0), (shards, 1, own_rows)).reshape(
        1, width
    )
    _, silu_pull = jax.vjp(jax.nn.silu, cond)
    cond_grad = silu_pull(grad_cond_low)[0]

    bias_total = cube_scatter(jnp.stack(bias_grads, axis=1), "shard")
    bias_total = bias_total + swap_pairs(bias_total, "rep")
    bias_total = bias_total + swap_pairs(bias_total, "seq")
    qv_b, proj_b, fc1_b, fc2_b = [
        bias_total[:, ends[at] - ends[1] : ends[at + 1] - ends[1]] for at in range(1, 5)
    ]
    if rings:
        moved, lates = moves.finish({3: shares[0], 8: shares[1]})
        done.update(moved)
        for layer, step in ((1, 3), (0, 8)):
            spread = cube_gather(lates[step], ("rep", "seq"))
            done["mlp", layer] = spread.reshape(-1, own_rows, width).astype(F32)
    weight_grads = []
    for layer in range(LAYERS):
        attn_grads, mlp_grads = done["attn", layer], done["mlp", layer]
        weight_grads.append(
            (
                uncolumns(attn_grads[:3]),
                attn_grads[3],
                uncolumns(mlp_grads[:ff_parts]),
                mlp_grads[ff_parts:].reshape(ff_parts * own_rows, width),
            )
        )
    qkv_g, proj_g, fc1_g, fc2_g = [
        jnp.stack([weight_grads[layer][at] for layer in range(LAYERS)]) for at in range(4)
    ]
    return (
        activations[None],
        latent_grad[None],
        cond_grad,
        jnp.stack(ada_w_grads),
        jnp.stack(ada_b_grads),
        qkv_g,
        qv_b,
        proj_g,
        proj_b,
        fc1_g,
        fc1_b,
        fc2_g,
        fc2_b,
    )


def solution(mesh):
    tokens = P(("rep", "shard"), "seq", None)
    images = P(("rep", "shard"))
    matrix = P(None, "shard", None)
    vector = P(None, "shard")
    return jax.shard_map(
        shards_program,
        mesh=mesh,
        in_specs=(tokens, images, images, images, P())
        + (matrix, vector) * 5
        + (tokens,),
        out_specs=(tokens, tokens, P(("rep", "shard"), None)) + (matrix, vector) * 5,
        check_vma=False,
    )
```

```python
import functools
import math

import jax
import jax.numpy as jnp
from jax import lax
from jax.experimental import pallas as pl
from jax.experimental.pallas import tpu as pltpu
from jax.sharding import PartitionSpec as P

HEADS = 12
LAYERS = 2
EPSILON = 1e-06
BF16 = jnp.bfloat16
F32 = jnp.float32


def swap_pairs(value, axis):
    return lax.ppermute(value, axis, [(0, 1), (1, 0)])


def swap_layout(value):
    moved = lax.ppermute(value, ("rep", "seq"), [(1, 2), (2, 1)])
    return jnp.where(lax.axis_index("rep") == lax.axis_index("seq"), value, moved)


def cube_pairs(value, axis, bit):
    return lax.ppermute(value, axis, [(at, at ^ bit) for at in range(lax.axis_size(axis))])


def cube_bits(axis):
    return [1 << place for place in range(lax.axis_size(axis).bit_length() - 1)]


def as_is(value):
    return value


def cube_gather(value, axes, tick=as_is):
    value = value[None]
    for axis in reversed(axes):
        for bit in cube_bits(axis):
            other = tick(cube_pairs(value, axis, bit))
            value = jnp.where(
                lax.axis_index(axis) & bit == 0,
                jnp.concatenate([value, other]),
                jnp.concatenate([other, value]),
            )
    return value


def cube_scatter(value, axis, tick=as_is):
    for bit in reversed(cube_bits(axis)):
        low, high = value[:bit], value[bit:]
        first = lax.axis_index(axis) & bit == 0
        other = tick(cube_pairs(jnp.where(first, high, low), axis, bit))
        value = jnp.where(first, low, high) + other
    return value[0]


def ring_order(size):
    half = size // 2
    return [2 * place for place in range(half)] + [2 * place + 1 for place in reversed(range(half))]


def ring_step(value, forward):
    size = lax.axis_size("shard")
    order = ring_order(size)
    step = 1 if forward else size - 1
    return lax.ppermute(
        value, "shard", [(order[at], order[(at + step) % size]) for at in range(size)]
    )


def ring_ids():
    size = lax.axis_size("shard")
    order = ring_order(size)
    places = [order.index(shard) for shard in range(size)]
    place = jnp.array(places, jnp.int32)[lax.axis_index("shard")]
    return jnp.array(order, jnp.int32)[(place + jnp.arange(size, dtype=jnp.int32)) % size]


OFFSETS = (-1, 1, -2, 2, -3, 3, 4)


def place_kernel(where, *refs):
    (own, *rest) = refs[:23]
    out, sem = refs[23:]
    blocks, beside = rest[0:7], rest[7:11]
    core_blocks, core_beside = rest[11:18], rest[18:22]
    rep, seq = where[8], where[9]
    unit = own.shape[1] // 6

    def put(src, shard, row, rows):
        start = pl.multiple_of(row * unit, unit)
        copy = pltpu.make_async_copy(src, out.at[shard, :, pl.ds(start, rows), :], sem)
        copy.start()
        return [copy]

    copies = put(own, where[0], 0, 6 * unit)
    for slot, offset in enumerate(OFFSETS):
        shard = where[offset % 8]
        far = 3 * rep + 2 * (1 - seq)
        copies += put(blocks[slot], shard, 3 * rep + seq, 2 * unit)
        copies += put(beside[slot // 2].at[slot % 2], shard, far, unit)
        far = 3 * (1 - rep) + 2 * (1 - seq)
        copies += put(core_blocks[slot], shard, 3 * (1 - rep) + seq, 2 * unit)
        copies += put(core_beside[slot // 2].at[slot % 2], shard, far, unit)
    for copy in copies:
        copy.wait()


def gather_ring(piece):
    count, rows, width = piece.shape
    shards = lax.axis_size("shard")
    unit = rows // 6
    rep, seq = lax.axis_index("rep"), lax.axis_index("seq")
    mine = lax.dynamic_slice(piece, (0, (3 * rep + seq) * unit, 0), (count, 2 * unit, width))

    def cross(*blocks):
        cut = [
            lax.dynamic_slice(block, (0, seq * unit, 0), (count, unit, width)) for block in blocks
        ]
        return swap_pairs(jnp.stack(cut), "seq")

    def core(block):
        return swap_pairs(block, "rep")

    def around(up, down):
        return ring_step(up, True), ring_step(down, False)

    up1, down1 = yield around(mine, mine)
    up2, down2, x1, *core1 = yield (
        *around(up1, down1), cross(up1, down1), core(up1), core(down1)
    )
    up3, down3, x2, *core2 = yield (
        *around(up2, down2), cross(up2, down2), core(up2), core(down2), core(x1)
    )
    up4, down4, x3, *core3 = yield (
        *around(up3[:, :unit], down3[:, unit:]), cross(up3, down3), core(up3), core(down3), core(x2)
    )
    far = jnp.concatenate([up4, down4], axis=1)
    x4, *core4 = yield (cross(far), core(far), core(x3))
    (core_x4,) = yield (core(x4),)
    parts = [up1, down1, up2, down2, up3, down3, far, x1, x2, x3, x4]
    parts += core1 + core2[:2] + core3[:2] + core4[:1]
    parts += [core2[2], core3[2], core4[1], core_x4]
    where = jnp.concatenate([ring_ids(), jnp.stack([rep, seq]).astype(jnp.int32)])
    anywhere = pl.BlockSpec(memory_space=pl.ANY)
    return pl.pallas_call(
        place_kernel,
        out_shape=jax.ShapeDtypeStruct((shards, count, rows, width), piece.dtype),
        in_specs=[pl.BlockSpec(memory_space=pltpu.SMEM)] + [anywhere] * 23,
        out_specs=pl.BlockSpec(memory_space=pltpu.VMEM),
        compiler_params=pltpu.CompilerParams(vmem_limit_bytes=32 * 2**20),
        scratch_shapes=[pltpu.SemaphoreType.DMA],
        cost_estimate=pl.CostEstimate(
            flops=0, transcendentals=0, bytes_accessed=2 * shards * piece.size * 2
        ),
    )(where, piece, *parts)


def gather_wide(piece, after=None):
    count, rows, width = piece.shape
    copies = lax.axis_size("rep") * lax.axis_size("seq")
    at = lax.axis_index("rep") * lax.axis_size("seq") + lax.axis_index("seq")
    own = lax.dynamic_slice(piece, (at * (count // copies), 0, 0), (count // copies, rows, width))
    if after is not None:
        own, after = lax.optimization_barrier((own, after))
    whole_piece = lax.all_gather(
        own.reshape(-1, width), ("shard", "rep", "seq"), axis=0, tiled=True
    )
    return whole_piece.reshape(-1, count, rows, width), after


def gather_plain(piece, stacked):
    first, parts = stacked
    width = piece.shape[2]
    whole_piece = lax.all_gather(piece, "shard", axis=0, tiled=False)
    flat = whole_piece.transpose(1, 0, 2, 3).reshape(-1, width, width)
    if parts:
        tall = whole_piece[:, first : first + parts].reshape(parts, width, width)
        flat = jnp.concatenate([flat[:first], tall, flat[first + parts :]])
    return flat[None]


def ring_fits(rows):
    return (
        lax.axis_size("shard") == 8
        and lax.axis_size("rep") == 2
        and lax.axis_size("seq") == 2
        and rows % 96 == 0
    )


def add(left, right):
    return (left.astype(F32) + right.astype(F32)).astype(BF16)


def scatter_ring(grads):
    shards, _, rows, width = grads[0].shape
    count = sum(part.shape[1] for part in grads)
    unit = rows // 6
    rep, seq = lax.axis_index("rep"), lax.axis_index("seq")
    ids = ring_ids()

    def half(which):
        cut = [
            lax.dynamic_slice(
                part, (0, 0, 3 * unit * which, 0), (shards, part.shape[1], 3 * unit, width)
            )
            for part in grads
        ]
        return jnp.concatenate(cut, axis=1)

    (got,) = yield (swap_pairs(half(1 - rep), "rep"),)
    paired = add(half(rep), got)

    def block(offset):
        return lax.dynamic_index_in_dim(paired, ids[offset % 8], 0, keepdims=False)

    def send(offsets):
        sent = [
            lax.dynamic_slice(block(offset), (0, 2 * (1 - seq) * unit, 0), (count, unit, width))
            for offset in offsets
        ]
        return swap_pairs(jnp.stack(sent), "seq")

    def join(offset, got):
        kept = lax.dynamic_slice(block(offset), (0, seq * unit, 0), (count, 2 * unit, width))
        zero = jnp.zeros_like(got)
        beside = jnp.where(
            seq == 0,
            jnp.concatenate([got, zero], axis=1),
            jnp.concatenate([zero, got], axis=1),
        )
        return add(kept, beside)

    far, near3 = yield (send((4,)), send((3, -3)))
    far = join(4, far[0])
    up, down, near2 = yield (
        ring_step(far[:, :unit], True),
        ring_step(far[:, unit:], False),
        send((2, -2)),
    )
    up3, down3 = join(3, near3[0]), join(-3, near3[1])
    up = jnp.concatenate([add(up3[:, :unit], up), up3[:, unit:]], axis=1)
    down = jnp.concatenate([down3[:, :unit], add(down3[:, unit:], down)], axis=1)
    up, down, near1 = yield (ring_step(up, True), ring_step(down, False), send((1, -1)))
    up, down, here = yield (
        ring_step(add(join(2, near2[0]), up), True),
        ring_step(add(join(-2, near2[1]), down), False),
        send((0,)),
    )
    up, down = yield (
        ring_step(add(join(1, near1[0]), up), True),
        ring_step(add(join(-1, near1[1]), down), False),
    )
    total = add(join(0, here[0]).astype(F32) + up.astype(F32), down)
    (other,) = yield (swap_pairs(total, "seq"),)
    left, right = jnp.where(seq == 0, total, other), jnp.where(seq == 0, other, total)
    mine = jnp.concatenate(
        [left[:, :unit], add(left[:, unit:], right[:, :unit]), right[:, unit:]], axis=1
    )
    (other,) = yield (swap_pairs(mine, "rep"),)
    return jnp.where(
        rep == 0,
        jnp.concatenate([mine, other], axis=1),
        jnp.concatenate([other, mine], axis=1),
    ).astype(F32)


class Moves:
    def __init__(self, queue=()):
        self.queue = list(queue)
        self.running = []
        self.done = {}
        self.held = True
        if self.queue:
            self.pull()

    def pull(self):
        (key, piece, stacked) = self.queue.pop(0)
        if not ring_fits(piece.shape[1]):
            self.done[key] = gather_plain(piece, stacked)
            return
        if self.running:
            piece, moving = lax.optimization_barrier(
                (piece, [moving for _, _, moving, _ in self.running])
            )
            self.running = [
                (*move[:2], got, move[3]) for move, got in zip(self.running, moving)
            ]
        stages = gather_ring(piece)
        self.running.append((key, stages, next(stages), 1))

    def start(self, key, grads):
        stages = scatter_ring(grads)
        self.running.append((key, stages, next(stages), 9))

    def tick(self, value=None, only=None):
        waiting = [moving for _, _, moving, _ in self.running]
        if value is not None and waiting:
            value, waiting = lax.optimization_barrier((value, waiting))
        still = []
        for (key, stages, _, count), moving in zip(self.running, waiting):
            if only not in (None, key):
                still.append((key, stages, moving, count))
                continue
            try:
                still.append((key, stages, stages.send(moving), count + 1))
            except StopIteration as end:
                self.done[key] = end.value
        self.running = still
        if self.queue and not self.held and all(count > 4 for _, _, _, count in still):
            self.pull()
        return value

    def need(self, key):
        while key not in self.done:
            self.tick(only=key if any(key == move[0] for move in self.running) else None)
        return self.done[key]

    def finish(self, lates):
        step = 0
        while self.running:
            step += 1
            value = self.tick(lates.get(step))
            if step in lates:
                lates[step] = value
        return self.done, lates


def scatter_wide(grads):
    return lax.psum_scatter(
        grads.reshape(-1, grads.shape[-1]),
        ("shard", "rep", "seq"),
        scatter_dimension=0,
        tiled=True,
    )


def scatter_plain(grads):
    owned = lax.psum_scatter(grads.astype(F32), "shard", scatter_dimension=0, tiled=False)
    return lax.psum(owned.astype(BF16), ("rep", "seq")).astype(F32)


def normalize(values):
    centered = values - jnp.mean(values, axis=-1, keepdims=True)
    scale = lax.rsqrt(jnp.mean(centered * centered, axis=-1, keepdims=True) + EPSILON)
    return centered * scale, scale


def norm_back(grad, normal, scale, factor):
    u = grad * (1.0 + factor)
    return (
        u
        - jnp.mean(u, axis=-1, keepdims=True)
        - normal * jnp.mean(u * normal, axis=-1, keepdims=True)
    ) * scale


def time_embed(steps, width):
    half_width = width // 2
    freqs = jnp.exp(-math.log(10000.0) * jnp.arange(half_width, dtype=F32) / half_width)
    angles = steps.astype(F32)[:, None] * freqs[None, :]
    return jnp.concatenate([jnp.cos(angles), jnp.sin(angles)], axis=-1)


def dot(left, right, left_dims, right_dims):
    return lax.dot_general(
        left, right, ((left_dims, right_dims), ((), ())), preferred_element_type=F32
    )


def nt(left, right, **kw):
    return lax.dot_general(left, right, (((1,), (1,)), ((), ())), preferred_element_type=F32, **kw)


def tn(left, right):
    return lax.dot_general(left, right, (((0,), (0,)), ((), ())), preferred_element_type=F32)


def nn(left, right):
    return lax.dot_general(left, right, (((1,), (0,)), ((), ())), preferred_element_type=F32)


def head_mask(values, head, size):
    lanes = lax.broadcasted_iota(jnp.int32, values.shape, 1)
    inside = (lanes >= head * size) & (lanes < (head + 1) * size)
    return jnp.where(inside, values, jnp.zeros_like(values))


def attend_kernel(size, q_ref, own_ref, other_ref, mixed_ref, log_ref):
    pair = q_ref.shape[1] // size
    queries = q_ref[...] * jnp.asarray(size**-0.5, BF16)
    blocks = []
    for head in range(pair):
        query = head_mask(queries, head, size)
        scores = [nt(own_ref[0], query), nt(other_ref[0], query)]
        top = jnp.maximum(*[jnp.max(part, axis=0, keepdims=True) for part in scores])
        expo = [jnp.exp(part - top) for part in scores]
        totals = sum(jnp.sum(part, axis=0, keepdims=True) for part in expo)
        mixed = tn(own_ref[1], expo[0].astype(BF16)) + tn(other_ref[1], expo[1].astype(BF16))
        blocks.append(mixed[head * size : (head + 1) * size] / totals)
        log_ref[0, head : head + 1, :] = top + jnp.log(totals)
    mixed_ref[...] = jnp.transpose(jnp.concatenate(blocks, axis=0)).astype(BF16)


def attend(queries, own_kv, other_kv):
    tokens, width = queries.shape
    pair = 128 // (width // HEADS)
    groups = HEADS // pair
    kv_spec = pl.BlockSpec((2, tokens, 128), lambda group: (0, 0, group))
    token_spec = pl.BlockSpec((tokens, 128), lambda group: (0, group))
    flops = 8 * tokens * tokens * width
    return pl.pallas_call(
        functools.partial(attend_kernel, width // HEADS),
        grid=(groups,),
        in_specs=[token_spec, kv_spec, kv_spec],
        out_specs=(token_spec, pl.BlockSpec((1, pair, tokens), lambda group: (group, 0, 0))),
        out_shape=(
            jax.ShapeDtypeStruct((tokens, width), BF16),
            jax.ShapeDtypeStruct((groups, pair, tokens), F32),
        ),
        compiler_params=pltpu.CompilerParams(vmem_limit_bytes=40 * 2**20),
        cost_estimate=pl.CostEstimate(
            flops=4 * flops, transcendentals=2 * HEADS * tokens**2, bytes_accessed=12 * queries.size
        ),
    )(queries, own_kv, other_kv)


def attend_back_kernel(
    size, q_ref, own_ref, other_ref, grad_ref, mixed_ref, log_ref, dq_ref, down_ref, dother_ref
):
    pair = q_ref.shape[1] // size
    scale = jnp.asarray(size**-0.5, BF16)
    queries = q_ref[...] * scale
    product = grad_ref[...].astype(F32) * mixed_ref[...].astype(F32)
    ones = jnp.ones((8, product.shape[1]), F32)
    grad_queries = []
    grad_kv = {}
    for head in range(pair):
        query, grad = head_mask(queries, head, size), head_mask(grad_ref[...], head, size)
        delta = nt(ones, head_mask(product, head, size), precision=lax.Precision.HIGHEST)[0:1]
        log_total = log_ref[0, head : head + 1, :]
        grad_query = None
        for side, kv_ref in enumerate((own_ref, other_ref)):
            probs = jnp.exp(nt(kv_ref[0], query) - log_total)
            grad_scores = (probs * (nt(kv_ref[1], grad) - delta)).astype(BF16)
            parts = (nn(grad_scores, query), nn(probs.astype(BF16), grad))
            before = grad_kv.get(side)
            grad_kv[side] = parts if before is None else tuple(a + b for a, b in zip(before, parts))
            part = tn(kv_ref[0], grad_scores)[head * size : (head + 1) * size]
            grad_query = part if grad_query is None else grad_query + part
        grad_queries.append(grad_query)
    total = jnp.transpose(jnp.concatenate(grad_queries, axis=0)) * (size**-0.5)
    dq_ref[...] = total.astype(BF16)
    for side, out_ref in enumerate((down_ref, dother_ref)):
        for at in range(2):
            out_ref[at] = grad_kv[side][at].astype(out_ref.dtype)


def attend_back(queries, own_kv, other_kv, grad_mixed, mixed, log_total):
    tokens, width = queries.shape
    pair = 128 // (width // HEADS)
    groups = HEADS // pair
    kv_spec = pl.BlockSpec((2, tokens, 128), lambda group: (0, 0, group))
    token_spec = pl.BlockSpec((tokens, 128), lambda group: (0, group))
    flops = 20 * tokens * tokens * width
    return pl.pallas_call(
        functools.partial(attend_back_kernel, width // HEADS),
        grid=(groups,),
        in_specs=[
            token_spec,
            kv_spec,
            kv_spec,
            token_spec,
            token_spec,
            pl.BlockSpec((1, pair, tokens), lambda group: (group, 0, 0)),
        ],
        out_specs=(token_spec, kv_spec, kv_spec),
        out_shape=(
            jax.ShapeDtypeStruct((tokens, width), BF16),
            jax.ShapeDtypeStruct(own_kv.shape, F32),
            jax.ShapeDtypeStruct(own_kv.shape, BF16),
        ),
        compiler_params=pltpu.CompilerParams(vmem_limit_bytes=40 * 2**20),
        cost_estimate=pl.CostEstimate(
            flops=4 * flops, transcendentals=2 * HEADS * tokens**2, bytes_accessed=24 * queries.size
        ),
    )(queries, own_kv, other_kv, grad_mixed, mixed, log_total)


def params_of(megabytes=48):
    return pltpu.CompilerParams(vmem_limit_bytes=megabytes * 2**20)


def whole(shape):
    return pl.BlockSpec(shape, lambda *at: (0,) * len(shape))


def column_sum(values):
    return jnp.sum(values, axis=0, keepdims=True)


def matrix_at(array, at, moving=True):
    shards, _, rows, width = array.shape
    return pl.BlockSpec(
        (shards, 1, rows, width), lambda part: (0, at + part if moving else at, 0, 0)
    )


def tall_at(array, at, parts):
    shards, _, rows, width = array.shape
    if shards == 1:
        return matrix_at(array, at)
    return pl.BlockSpec((shards // parts, parts, rows, width), lambda part: (part, at // parts, 0, 0))


def square(ref):
    return ref[...].reshape(ref.shape[-1], ref.shape[-1])


def put_square(ref, value):
    ref[...] = value.astype(ref.dtype).reshape(ref.shape)


def project_kernel(stream_ref, mod_ref, weight_ref, bias_ref, normed_ref, q_ref, kv_ref):
    part = pl.program_id(0)

    @pl.when(part == 0)
    def _():
        normal, _ = normalize(stream_ref[...])
        normed_ref[...] = (normal * (1.0 + mod_ref[1:2]) + mod_ref[0:1]).astype(BF16)

    result = (nn(normed_ref[...], square(weight_ref)) + bias_ref[0]).astype(BF16)

    @pl.when(part == 0)
    def _():
        q_ref[...] = result

    @pl.when(part > 0)
    def _():
        kv_ref[0] = result


def project(stream, modulation, weights, bias):
    tokens, width = stream.shape
    return pl.pallas_call(
        project_kernel,
        grid=(3,),
        in_specs=[
            whole((tokens, width)),
            whole((6, width)),
            matrix_at(weights, 0),
            pl.BlockSpec((1, 1, width), lambda part: (part, 0, 0)),
        ],
        out_specs=(
            whole((tokens, width)),
            whole((tokens, width)),
            pl.BlockSpec((1, tokens, width), lambda part: (jnp.maximum(part - 1, 0), 0, 0)),
        ),
        out_shape=(
            jax.ShapeDtypeStruct((tokens, width), BF16),
            jax.ShapeDtypeStruct((tokens, width), BF16),
            jax.ShapeDtypeStruct((2, tokens, width), BF16),
        ),
        compiler_params=params_of(),
        cost_estimate=pl.CostEstimate(
            flops=6 * tokens * width**2, transcendentals=0, bytes_accessed=12 * tokens * width
        ),
    )(stream, modulation, weights, bias)


GELU_SCALE = math.sqrt(2.0 / math.pi)


def gelu_parts(value):
    square = value * value
    tanh = jnp.tanh(GELU_SCALE * value * (1.0 + 0.044715 * square))
    return square, tanh


def mlp_kernel(
    mixed_ref, stream_ref, mod_ref, proj_ref, proj_b_ref, fc1_ref, fc1_b_ref, fc2_ref, fc2_b_ref,
    attn_ref, middle_ref, normed_ref, hidden_ref, active_ref, mlp_ref, result_ref,
):
    part = pl.program_id(0)

    @pl.when(part == 0)
    def _():
        attn_out = nn(mixed_ref[...], square(proj_ref)) + proj_b_ref[...]
        attn_ref[...] = attn_out
        middle = stream_ref[...] + mod_ref[2:3] * attn_out
        middle_ref[...] = middle
        normal, _ = normalize(middle)
        normed_ref[...] = (normal * (1.0 + mod_ref[4:5]) + mod_ref[3:4]).astype(BF16)

    hidden = nn(normed_ref[...], square(fc1_ref)) + fc1_b_ref[0]
    hidden_ref[0] = hidden
    _, tanh = gelu_parts(hidden)
    active = (0.5 * hidden * (1.0 + tanh)).astype(BF16)
    active_ref[0] = active
    product = nn(active, square(fc2_ref))

    @pl.when(part == 0)
    def _():
        mlp_ref[...] = product + fc2_b_ref[...]

    @pl.when(part > 0)
    def _():
        mlp_ref[...] += product

    @pl.when(part == pl.num_programs(0) - 1)
    def _():
        result_ref[...] = middle_ref[...] + mod_ref[5:6] * mlp_ref[...]


def mlp(mixed, stream, modulation, attn_w, weights, proj_b, fc1_b, fc2_b):
    tokens, width = stream.shape
    parts = fc1_b.shape[0]
    token, row = whole((tokens, width)), whole((1, width))
    by_part = lambda rows: pl.BlockSpec((1, rows, width), lambda part: (part, 0, 0))
    shape = lambda *dims: jax.ShapeDtypeStruct(dims[:-1], dims[-1])
    return pl.pallas_call(
        mlp_kernel,
        grid=(parts,),
        in_specs=[
            token, token, whole((6, width)), matrix_at(attn_w, 3, False), row,
            matrix_at(weights, 0), by_part(1), tall_at(weights, parts, parts), row,
        ],
        out_specs=(token, token, token, by_part(tokens), by_part(tokens), token, token),
        out_shape=(
            shape(tokens, width, F32),
            shape(tokens, width, F32),
            shape(tokens, width, BF16),
            shape(parts, tokens, width, F32),
            shape(parts, tokens, width, BF16),
            shape(tokens, width, F32),
            shape(tokens, width, F32),
        ),
        compiler_params=params_of(),
        cost_estimate=pl.CostEstimate(
            flops=(2 + 4 * parts) * tokens * width**2,
            transcendentals=parts * tokens * width,
            bytes_accessed=(20 + 6 * parts) * tokens * width,
        ),
    )(mixed, stream, modulation, attn_w, proj_b, weights, fc1_b, weights, fc2_b)


def mlp_back_kernel(
    grad_ref, mlp_ref, mod_ref, fc2_ref, fc1_ref, hidden_ref, active_ref, normed_ref, middle_ref,
    attn_ref, mixed_ref, proj_ref,
    fc2_g_ref, fc1_g_ref, proj_g_ref, fc1_b_ref, sums_ref, grad_middle_ref, grad_mixed_ref,
    low_ref, total_ref,
):
    part = pl.program_id(0)

    @pl.when(part == 0)
    def _():
        grad = grad_ref[...]
        sums_ref[2:3] = column_sum(grad * mlp_ref[...])
        low = (grad * mod_ref[5:6]).astype(BF16)
        low_ref[...] = low
        sums_ref[4:5] = column_sum(low.astype(F32))

    low = low_ref[...]
    put_square(fc2_g_ref, tn(active_ref[0], low))
    hidden = hidden_ref[0]
    squared, tanh = gelu_parts(hidden)
    slope = 0.5 * (1.0 + tanh) + (0.5 * GELU_SCALE) * hidden * (1.0 - tanh * tanh) * (
        1.0 + (3 * 0.044715) * squared
    )
    grad_hidden = (nt(low, square(fc2_ref)) * slope).astype(BF16)
    fc1_b_ref[0] = column_sum(grad_hidden.astype(F32))
    put_square(fc1_g_ref, tn(normed_ref[...], grad_hidden))
    product = nt(grad_hidden, square(fc1_ref))

    @pl.when(part == 0)
    def _():
        total_ref[...] = product

    @pl.when(part > 0)
    def _():
        total_ref[...] += product

    @pl.when(part == pl.num_programs(0) - 1)
    def _():
        grad_normed = total_ref[...]
        normal, scale = normalize(middle_ref[...])
        sums_ref[0:1] = column_sum(grad_normed)
        sums_ref[1:2] = column_sum(grad_normed * normal)
        grad_middle = grad_ref[...] + norm_back(grad_normed, normal, scale, mod_ref[4:5])
        grad_middle_ref[...] = grad_middle
        sums_ref[3:4] = column_sum(grad_middle * attn_ref[...])
        grad_attn = (grad_middle * mod_ref[2:3]).astype(BF16)
        sums_ref[5:6] = column_sum(grad_attn.astype(F32))
        put_square(proj_g_ref, tn(mixed_ref[...], grad_attn))
        grad_mixed_ref[...] = nt(grad_attn, square(proj_ref)).astype(BF16)


def mlp_back(
    grad, mlp_out, modulation, attn_w, weights, hidden, active, normed, middle, attn_out, mixed
):
    tokens, width = grad.shape
    parts = hidden.shape[0]
    token = whole((tokens, width))
    form = (weights.shape[0], parts) + weights.shape[2:]
    fc_form, proj_form = jax.ShapeDtypeStruct(form, BF16), jax.ShapeDtypeStruct(
        (form[0], 1) + form[2:], BF16
    )
    by_part = lambda rows: pl.BlockSpec((1, rows, width), lambda part: (part, 0, 0))
    shape = lambda *dims: jax.ShapeDtypeStruct(dims[:-1], dims[-1])
    return pl.pallas_call(
        mlp_back_kernel,
        grid=(parts,),
        in_specs=[
            token, token, whole((6, width)), tall_at(weights, parts, parts), matrix_at(weights, 0),
            by_part(tokens), by_part(tokens), token, token, token, token,
            matrix_at(attn_w, 3, False),
        ],
        out_specs=(
            tall_at(fc_form, 0, parts), matrix_at(fc_form, 0), matrix_at(proj_form, 0, False),
            by_part(1), whole((6, width)), token, token,
        ),
        out_shape=(
            fc_form,
            fc_form,
            proj_form,
            shape(parts, 1, width, F32),
            shape(6, width, F32),
            shape(tokens, width, F32),
            shape(tokens, width, BF16),
        ),
        scratch_shapes=[pltpu.VMEM((tokens, width), BF16), pltpu.VMEM((tokens, width), F32)],
        compiler_params=params_of(56),
        cost_estimate=pl.CostEstimate(
            flops=(4 + 8 * parts) * tokens * width**2,
            transcendentals=parts * tokens * width,
            bytes_accessed=(20 + 6 * parts) * tokens * width + 8 * parts * width**2,
        ),
    )(
        grad, mlp_out, modulation, weights, weights, hidden, active, normed, middle, attn_out,
        mixed, attn_w,
    )


def project_back_kernel(
    gq_ref, own_ref, back_ref, normed_ref, weight_ref, stream_ref, mod_ref, middle_ref,
    weight_g_ref, sums_ref, bias_ref, grad_ref, total_ref,
):
    part = pl.program_id(0)

    def step(grad, first):
        put_square(weight_g_ref, tn(normed_ref[...], grad))
        bias_ref[0] = column_sum(grad.astype(F32))
        product = nt(grad, square(weight_ref))
        total_ref[...] = product if first else total_ref[...] + product

    @pl.when(part == 0)
    def _():
        step(gq_ref[...], True)

    @pl.when(part > 0)
    def _():
        step((own_ref[0] + back_ref[0].astype(F32)).astype(BF16), False)

    @pl.when(part == 2)
    def _():
        grad_normed = total_ref[...]
        normal, scale = normalize(stream_ref[...])
        sums_ref[0:1] = column_sum(grad_normed)
        sums_ref[1:2] = column_sum(grad_normed * normal)
        grad_ref[...] = middle_ref[...] + norm_back(grad_normed, normal, scale, mod_ref[1:2])


def project_back(grad_q, grad_own, returned, normed, weights, stream, modulation, grad_middle):
    tokens, width = stream.shape
    token = whole((tokens, width))
    form = jax.ShapeDtypeStruct((weights.shape[0], 3) + weights.shape[2:], BF16)
    kv = pl.BlockSpec((1, tokens, width), lambda part: (jnp.maximum(part - 1, 0), 0, 0))
    return pl.pallas_call(
        project_back_kernel,
        grid=(3,),
        in_specs=[
            token, kv, kv, token, matrix_at(weights, 0), token, whole((6, width)), token,
        ],
        out_specs=(
            matrix_at(form, 0),
            whole((2, width)),
            pl.BlockSpec((1, 1, width), lambda part: (part, 0, 0)),
            token,
        ),
        out_shape=(
            form,
            jax.ShapeDtypeStruct((2, width), F32),
            jax.ShapeDtypeStruct((3, 1, width), F32),
            jax.ShapeDtypeStruct((tokens, width), F32),
        ),
        scratch_shapes=[pltpu.VMEM((tokens, width), F32)],
        compiler_params=params_of(),
        cost_estimate=pl.CostEstimate(
            flops=12 * tokens * width**2,
            transcendentals=0,
            bytes_accessed=24 * tokens * width + 12 * width**2,
        ),
    )(grad_q, grad_own, returned, normed, weights, stream, modulation, grad_middle)


def layer_forward(stream, modulation, biases, moves, attn_w, fetch_mlp):
    qkv_b, proj_b, fc1_b, fc2_b = biases
    normed, queries, own_kv = project(stream, modulation, attn_w, qkv_b)
    moves.held = False
    own_kv = moves.tick(fetch_mlp(own_kv))
    other_kv = moves.tick(swap_pairs(own_kv, "rep"))
    mixed, log_total = attend(queries, own_kv, other_kv)
    mixed = moves.tick(moves.tick(mixed))
    mlp_w = fetch_mlp()
    attn_out, middle, normed_mlp, hidden, active, mlp_out, result = mlp(
        mixed, stream, modulation, attn_w, mlp_w, proj_b, fc1_b, fc2_b
    )
    result = moves.tick(result)
    return result, (
        stream, normed, queries, own_kv, other_kv, mixed, log_total, attn_out, middle, normed_mlp,
        hidden, active, mlp_out, attn_w, mlp_w,
    )


def layer_backward(grad_out, modulation, kept, shards, moves, send_mlp, send_attn):
    (
        stream, normed, queries, own_kv, other_kv, mixed, log_total, attn_out, middle, normed_mlp,
        hidden, active, mlp_out, attn_w, mlp_w,
    ) = kept
    width = stream.shape[-1]
    fc2_g, fc1_g, proj_g, fc1_b, sums, grad_middle, grad_mixed = mlp_back(
        grad_out, mlp_out, modulation, attn_w, mlp_w, hidden, active, normed_mlp, middle, attn_out,
        mixed,
    )
    grad_mixed = moves.tick(grad_mixed)
    grad_mixed = send_mlp(fc1_g, fc2_g, grad_mixed)
    grad_q, grad_own, grad_other = attend_back(
        queries, own_kv, other_kv, grad_mixed, mixed, log_total
    )
    grad_other = moves.tick(grad_other)
    returned = swap_pairs(grad_other, "rep")
    qkv_g, attn_sums, qkv_b, grad_stream = project_back(
        grad_q, grad_own, returned, normed, attn_w, stream, modulation, grad_middle
    )
    grad_stream = moves.tick(grad_stream)
    send_attn(qkv_g, proj_g)
    grad_modulation = jnp.concatenate(
        [attn_sums[0], attn_sums[1], sums[3], sums[0], sums[1], sums[2]]
    )
    query_value = jnp.concatenate([qkv_b[0, 0], qkv_b[2, 0]])
    bias_grads = [
        part.reshape(shards, -1) for part in (query_value, sums[5], fc1_b.reshape(-1), sums[4])
    ]
    return grad_stream, grad_modulation, jnp.concatenate(bias_grads, axis=1)


def columns(matrix, width):
    return jnp.stack(jnp.split(matrix, matrix.shape[1] // width, axis=1))


def uncolumns(blocks):
    return jnp.concatenate(list(blocks), axis=1)


def shards_program(
    latents,
    image_loads,
    timesteps,
    classes,
    label_table,
    ada_weight,
    ada_bias,
    qkv_weight,
    qv_bias,
    proj_weight,
    proj_bias,
    fc1_weight,
    fc1_bias,
    fc2_weight,
    fc2_bias,
    cotangent,
):
    shards = lax.axis_size("shard")
    width = latents.shape[2]
    own_rows = width // shards
    ff_parts = fc1_weight.shape[2] // width
    shard, rep, seq = lax.axis_index("shard"), lax.axis_index("rep"), lax.axis_index("seq")

    rings = ring_fits(own_rows)
    attn_packs, mlp_packs = [], []
    for layer in range(LAYERS):
        fc2_piece = fc2_weight[layer].reshape(ff_parts, own_rows, width)
        mlp_packs.append(jnp.concatenate([columns(fc1_weight[layer], width), fc2_piece]))
        attn_packs.append(
            jnp.concatenate([columns(qkv_weight[layer], width), proj_weight[layer][None]])
        )
    moves = Moves([(layer, attn_packs[layer], (0, 0)) for layer in range(LAYERS)])

    one_hot = (
        classes[:, None] == jnp.arange(label_table.shape[0], dtype=jnp.int32)[None, :]
    ).astype(BF16)
    cond = dot(one_hot, label_table, (1,), (0,)) + time_embed(timesteps, width)
    cond_low = jax.nn.silu(cond).astype(BF16)
    live_own = (image_loads > 0).astype(BF16)
    shared = cube_gather(
        jnp.concatenate([cond_low[0], jnp.broadcast_to(live_own, (128,))]),
        ("rep", "shard"),
        moves.tick,
    )
    live = lax.dynamic_slice(shared, (seq * shards + shard, width), (1, 1)).astype(F32)
    cond_rows = lax.dynamic_slice(
        shared[:, :width], (0, shard * own_rows), (shared.shape[0], own_rows)
    )
    stream = swap_layout(latents[0]).astype(F32)

    mlp_w = []

    def fetch_mlp(layer, ahead=None):
        if not rings:
            if ahead is not None:
                return ahead
            return gather_plain(mlp_packs[layer], (ff_parts, ff_parts))
        if ahead is None:
            return mlp_w[layer]
        if layer + 1 < LAYERS:
            later, (mlp_w[layer], ahead) = gather_wide(mlp_packs[layer + 1], (mlp_w[layer], ahead))
            mlp_w.append(later)
        return ahead

    if rings:
        mlp_w.append(gather_wide(mlp_packs[0])[0])

    small = jnp.concatenate([ada_bias, qv_bias, proj_bias, fc1_bias, fc2_bias], axis=1)
    small = cube_gather(small, ("shard",)).astype(F32)
    ends = [0]
    for bias in (ada_bias, qv_bias, proj_bias, fc1_bias, fc2_bias):
        ends.append(ends[-1] + bias.shape[1])
    biases, ada_b = [], []
    for layer in range(LAYERS):
        full = [small[:, layer, ends[at] : ends[at + 1]].reshape(-1) for at in range(5)]
        ada_b.append(full[0])
        qkv_b = jnp.concatenate([full[1][:width], jnp.zeros((width,), F32), full[1][width:]])
        biases.append(
            (
                qkv_b.reshape(3, 1, width),
                full[2][None],
                full[3].reshape(ff_parts, 1, width),
                full[4][None],
            )
        )

    mine = lax.dynamic_slice(cond_rows, (seq * shards, 0), (shards, own_rows))
    partial = jnp.concatenate(
        [dot(mine, ada_weight[layer], (1,), (0,)) for layer in range(LAYERS)], axis=1
    )
    modulations = cube_scatter(partial, "shard", moves.tick)
    modulations = [
        (modulations.reshape(LAYERS, -1)[layer] + ada_b[layer]).reshape(6, width)
        for layer in range(LAYERS)
    ]

    kept = []
    for layer in range(LAYERS):
        stream, layer_kept = layer_forward(
            stream,
            modulations[layer],
            biases[layer],
            moves,
            moves.need(layer),
            functools.partial(fetch_mlp, layer),
        )
        kept.append(layer_kept)
    moves = Moves()
    activations = swap_layout((stream * live).astype(BF16)).astype(F32)
    grad_stream = swap_layout(cotangent[0]).astype(F32) * live

    shares = []
    done = {}

    def flat(part):
        return part.reshape(part.shape[1], shards, own_rows, width).transpose(1, 0, 2, 3)

    def send_mlp(layer, fc1_g, fc2_g, grad_mixed):
        if not rings:
            tall = fc2_g.reshape(shards, ff_parts, own_rows, width)
            done["mlp", layer] = scatter_plain(jnp.concatenate([flat(fc1_g), tall], axis=1))
        else:
            both = jnp.concatenate([fc1_g, fc2_g], axis=1)
            both, grad_mixed = lax.optimization_barrier((both, grad_mixed))
            shares.append(scatter_wide(both))
        return grad_mixed

    def send_attn(layer, qkv_g, proj_g):
        if rings:
            moves.start(("attn", layer), [qkv_g, proj_g])
        else:
            both = jnp.concatenate([flat(qkv_g), flat(proj_g)], axis=1)
            done["attn", layer] = scatter_plain(both)

    bias_grads = [None] * LAYERS
    ada_w_grads = [None] * LAYERS
    grad_mods = [None] * LAYERS
    ada_b_grads = [None] * LAYERS
    grad_cond = 0.0
    for layer in reversed(range(LAYERS)):
        grad_stream, grad_mod, bias_grads[layer] = layer_backward(
            grad_stream,
            modulations[layer],
            kept[layer],
            shards,
            moves,
            functools.partial(send_mlp, layer),
            functools.partial(send_attn, layer),
        )
        grad_mods[layer] = grad_mod

    both_mods = jnp.stack(grad_mods)
    both_mods = (both_mods + swap_pairs(both_mods, "rep")).astype(BF16)
    both_mods = cube_gather(both_mods, ("seq", "shard"))
    for layer in range(LAYERS):
        all_mod = both_mods[:, layer]
        ada_w_grads[layer] = dot(cond_rows, all_mod, (0,), (0,))
        own_mod = lax.dynamic_slice(
            all_mod, (0, shard * ada_bias.shape[1]), (all_mod.shape[0], ada_bias.shape[1])
        )
        ada_b_grads[layer] = jnp.sum(own_mod.astype(F32), axis=0)
        rep_mod = lax.dynamic_slice(all_mod, (rep * shards, 0), (shards, all_mod.shape[1]))
        grad_cond = grad_cond + dot(rep_mod, ada_weight[layer], (1,), (1,))

    latent_grad = swap_layout(grad_stream.astype(BF16)).astype(F32)
    all_cond = cube_gather(grad_cond, ("shard",))
    grad_cond_low = lax.dynamic_slice(all_cond, (0, shard, 0), (shards, 1, own_rows)).reshape(
        1, width
    )
    _, silu_pull = jax.vjp(jax.nn.silu, cond)
    cond_grad = silu_pull(grad_cond_low)[0]

    bias_total = cube_scatter(jnp.stack(bias_grads, axis=1), "shard")
    bias_total = bias_total + swap_pairs(bias_total, "rep")
    bias_total = bias_total + swap_pairs(bias_total, "seq")
    qv_b, proj_b, fc1_b, fc2_b = [
        bias_total[:, ends[at] - ends[1] : ends[at + 1] - ends[1]] for at in range(1, 5)
    ]
    if rings:
        moved, lates = moves.finish({3: shares[0], 7: shares[1]})
        done.update(moved)
        for layer, step in ((1, 3), (0, 7)):
            spread = cube_gather(lates[step], ("rep", "seq"))
            done["mlp", layer] = spread.reshape(-1, own_rows, width).astype(F32)
    weight_grads = []
    for layer in range(LAYERS):
        attn_grads, mlp_grads = done["attn", layer], done["mlp", layer]
        weight_grads.append(
            (
                uncolumns(attn_grads[:3]),
                attn_grads[3],
                uncolumns(mlp_grads[:ff_parts]),
                mlp_grads[ff_parts:].reshape(ff_parts * own_rows, width),
            )
        )
    qkv_g, proj_g, fc1_g, fc2_g = [
        jnp.stack([weight_grads[layer][at] for layer in range(LAYERS)]) for at in range(4)
    ]
    return (
        activations[None],
        latent_grad[None],
        cond_grad,
        jnp.stack(ada_w_grads),
        jnp.stack(ada_b_grads),
        qkv_g,
        qv_b,
        proj_g,
        proj_b,
        fc1_g,
        fc1_b,
        fc2_g,
        fc2_b,
    )


def solution(mesh):
    tokens = P(("rep", "shard"), "seq", None)
    images = P(("rep", "shard"))
    matrix = P(None, "shard", None)
    vector = P(None, "shard")
    return jax.shard_map(
        shards_program,
        mesh=mesh,
        in_specs=(tokens, images, images, images, P())
        + (matrix, vector) * 5
        + (tokens,),
        out_specs=(tokens, tokens, P(("rep", "shard"), None)) + (matrix, vector) * 5,
        check_vma=False,
    )
```
